128 devices in a mesh: gx: 8 (over y, core), gy: 16 (over x, z).
Axes of the slice: x: 4, y: 4, z: 4, core: 2. Of those that a mesh axis runs over, the one named last changes fastest.
Arguments:
- parent: float32 [5, 20, 256, 2048], P(None, None, 'gx', 'gy'), may hold values from -6 to 6
- metric: float32 [256, 2048], P('gx', 'gy'), may hold values from 0.5 to 1.5
- buoyancy: float32 [20], replicated, may hold values from 0.1 to 0.9
- nest: float32 [5, 20, 192, 2048], P(None, None, 'gx', 'gy'), may hold values from -6 to 6
- nest_metric: float32 [192, 2048], P('gx', 'gy'), may hold values from 0.5 to 1.5
- strip_col: int32 [131072], P(('gx', 'gy')), may hold values from 0 to 4095
- strip_dest: int32 [131072, 1], P(('gx', 'gy')), may hold values from 0 to 127; in each aligned block of 1024 rows (0 to 1023, 1024 to 2047, ...) at most 32 rows name the same one
- strip_pos: int32 [131072], P(('gx', 'gy')), may hold values from 0 to 3071
- panel_src: int32 [131072], P(('gx', 'gy')), may hold values from 0 to 3071
- panel_dest: int32 [131072, 1], P(('gx', 'gy')), may hold values from 0 to 127; in each aligned block of 1024 rows (0 to 1023, 1024 to 2047, ...) at most 32 rows name the same one
- panel_col: int32 [131072], P(('gx', 'gy')), may hold values from 0 to 4095
Outputs:
- parent_out: float32 [5, 20, 256, 2048], P(None, None, 'gx', 'gy')
- nest_out: float32 [5, 20, 192, 2048], P(None, None, 'gx', 'gy')
The draws below stay inside these ranges and needn't reach their ends.
Inputs may be any that keep to these rules, and one draw needn't show every extreme that they name: `strip_dest`: among the 1024 rows of one device no device is named more than 32 times. `panel_dest`: among the 1024 rows of one device no device is named more than 32 times.
All inputs are finite; a program needn't handle non-finite values.
Results may differ from the reference program's by a relative error of at most 0.00002.
Values sent between devices are 32-bit elements; how exact they have to be, the bound alone decides.
No kernel may reach another device: no remote copies, remote signals or barrier semaphores. Data moves between devices by JAX's collectives and lax.ppermute only.
A program may use at most 128 MiB of HBM per device.

```python
import math
import jax
import jax.numpy as jnp
import numpy as np

CX = 32
CY = 128
LZ = 20
NBX = 24
NBY = 128
SLOTS = 1024
PANELS = 1024
CAP = 32
NSP = 4
NSN = 6
NX = 256
NY = 2048
MX = 192
MY = 2048
N_GX = 8
N_GY = 16


def plant(entries, rng, least, high):
    dims = entries.shape
    place = [jax.random.randint(jax.random.fold_in(rng, axis), (), 0, dims[axis]) for axis in range(len(dims))]
    entries = entries.at[tuple(place)].set(least)
    longest = dims.index(max(dims))
    place[longest] = (place[longest] + 1) % dims[longest]
    return entries.at[tuple(place)].set(high)


def block_scale(rng, dims, shards, low, largest):
    loudness, own = 1.0, jax.random.fold_in(rng, 6)
    for position, blocks in shards:
        heights = jnp.exp(jax.random.uniform(jax.random.fold_in(own, position), (blocks,), jnp.float32, low / len(shards), largest / len(shards)))
        loudness = loudness * jnp.repeat(heights, dims[position] // blocks).reshape([-1 if axis == position else 1 for axis in range(len(dims))])
    return loudness


def assign_block(stream_key, own, number, rows, count, top, reach, skew):
    sequence = jax.random.permutation(stream_key, count)
    crowded, usual = shares(count, rows * top, reach, skew, True), shares(count, rows * top, reach, skew, False)
    places = jnp.arange(count)

    def named(tallies, rotation):
        used = int((tallies > 0).sum())
        fixed = max(1, used // 4)
        passed = fixed + (places - fixed + rotation * (used - fixed)) % max(1, count - fixed)
        return jnp.zeros((count,), jnp.int32).at[sequence[jnp.where(places < fixed, places, passed)]].set(jnp.asarray(tallies, jnp.int32))

    tallies = jnp.where(number % 4 == 0, named(crowded, number // 4), named(usual, number - number // 4 - 1))
    mixed = jax.random.permutation(jax.random.fold_in(own, 3), count)
    giver, taker = mixed[0:count // 2 * 2:2], mixed[1:count // 2 * 2:2]
    room = jnp.minimum(tallies[giver] - 1, reach - tallies[taker]) // 2
    room = jnp.where((giver == sequence[0]) | (taker == sequence[0]) | (tallies[taker] == 0), 0, jnp.maximum(room, 0))
    passed = jax.random.randint(jax.random.fold_in(own, 4), (count // 2,), 0, 1 << 20) % (room + 1)
    tallies = tallies.at[giver].add(-passed).at[taker].add(passed)
    members = jnp.searchsorted(jnp.cumsum(tallies), jnp.arange(rows * top), side="right").astype(jnp.int32)
    grid = members.reshape(top, rows).T
    grid = grid[jax.random.permutation(jax.random.fold_in(own, 1), rows)]
    rotation = jax.random.randint(jax.random.fold_in(own, 2), (rows, 1), 0, top)
    return jnp.take_along_axis(grid, (jnp.arange(top)[None, :] + rotation) % top, axis=1)


def shares(amount, total, bound, lean, full):
    portions = [(1 << 20) // math.isqrt(grade ** lean) + 1 for grade in range(1, amount + 1)]
    largest = bound if full else min(bound, max(-(-total // amount), total * portions[0] // sum(portions)))
    least = 1 if total - largest >= amount - 1 else 0
    given, rest = [largest] + [least] * (amount - 1), total - largest - least * (amount - 1)
    while rest > 0:
        free = [i for i in range(1, amount) if given[i] < largest] or [i for i in range(1, amount) if given[i] < bound]
        mass, remaining = sum([portions[i] for i in free]), rest
        for i in free:
            addition = min(bound - given[i], max(1, remaining * portions[i] // mass), rest)
            given[i] = given[i] + addition
            rest = rest - addition
    return np.array(given)


def bell_draw(key, extent, spread, bound, split=(), kind=jnp.bfloat16):
    result = spread * jax.random.normal(key, extent, jnp.float32)
    if split:
        result = result * block_scale(key, extent, split, -0.22, 0.18)
    return jnp.clip(result, -bound, bound).astype(kind)


def setup_inputs(seed: int = 0) -> dict:
    streams_of = jax.random.split(jax.random.key(seed), 12)
    parent = bell_draw(streams_of[0], (5, LZ, NX, NY), 1.0, 6.0, ((2, 8), (3, 16)), jnp.float32)
    metric = jnp.clip(0.5 + 1.0 * jax.random.uniform(streams_of[1], (NX, NY), jnp.float32) ** block_scale(streams_of[1], (NX, NY), ((0, 8), (1, 16)), -0.2, 0.2), 0.5, 1.5)
    buoyancy = jnp.clip(jax.random.uniform(streams_of[2], (LZ,), jnp.float32, 0.1, 0.9), 0.1, 0.9)
    nest = bell_draw(streams_of[3], (5, LZ, MX, MY), 1.0, 6.0, ((2, 8), (3, 16)), jnp.float32)
    nest_metric = jnp.clip(0.5 + 1.0 * jax.random.uniform(streams_of[4], (MX, MY), jnp.float32) ** block_scale(streams_of[4], (MX, MY), ((0, 8), (1, 16)), -0.2, 0.2), 0.5, 1.5)
    strip_col = plant(jax.random.randint(streams_of[5], (N_GX * N_GY * SLOTS,), 0, CX * CY), jax.random.fold_in(streams_of[5], 1), 0, (CX * CY) - 1).astype(jnp.int32)
    strip_dest_keys = jax.random.split(jax.random.fold_in(streams_of[6], 1), (N_GX * N_GY * SLOTS) // SLOTS)
    strip_dest_turns = jax.random.permutation(jax.random.fold_in(streams_of[6], 3), (N_GX * N_GY * SLOTS) // SLOTS)
    strip_dest = jax.vmap(lambda own, number: assign_block(jax.random.fold_in(streams_of[6], 2), own, number, SLOTS, N_GX * N_GY, 1, CAP, 2))(strip_dest_keys, strip_dest_turns).reshape((N_GX * N_GY * SLOTS, 1))
    strip_pos = plant(jax.random.randint(streams_of[7], (N_GX * N_GY * SLOTS,), 0, NBX * NBY), jax.random.fold_in(streams_of[7], 1), 0, (NBX * NBY) - 1).astype(jnp.int32)
    panel_src = plant(jax.random.randint(streams_of[8], (N_GX * N_GY * PANELS,), 0, NBX * NBY), jax.random.fold_in(streams_of[8], 1), 0, (NBX * NBY) - 1).astype(jnp.int32)
    panel_dest_keys = jax.random.split(jax.random.fold_in(streams_of[9], 1), (N_GX * N_GY * PANELS) // PANELS)
    panel_dest_turns = jax.random.permutation(jax.random.fold_in(streams_of[9], 3), (N_GX * N_GY * PANELS) // PANELS)
    panel_dest = jax.vmap(lambda own, number: assign_block(jax.random.fold_in(streams_of[9], 2), own, number, PANELS, N_GX * N_GY, 1, CAP, 2))(panel_dest_keys, panel_dest_turns).reshape((N_GX * N_GY * PANELS, 1))
    panel_col = plant(jax.random.randint(streams_of[10], (N_GX * N_GY * PANELS,), 0, CX * CY), jax.random.fold_in(streams_of[10], 1), 0, (CX * CY) - 1).astype(jnp.int32)
    return {"parent": parent, "metric": metric, "buoyancy": buoyancy, "nest": nest, "nest_metric": nest_metric, "strip_col": strip_col, "strip_dest": strip_dest, "strip_pos": strip_pos, "panel_src": panel_src, "panel_dest": panel_dest, "panel_col": panel_col}


COURANT = 0.35


def small_step(fields, metric, buoyancy):
    u_wind, v_wind, w_wind, theta, pressure = fields[0], fields[1], fields[2], fields[3], fields[4]
    extended = jnp.pad(jnp.stack([u_wind, v_wind, pressure]), ((0, 0), (0, 0), (1, 1), (1, 1)))
    u_ext, v_ext, p_ext = extended[0], extended[1], extended[2]
    width_x, width_y = u_wind.shape[1], u_wind.shape[2]
    u_face = u_ext[:, 0:width_x + 1, 1:width_y + 1] - COURANT * (p_ext[:, 1:width_x + 2, 1:width_y + 1] - p_ext[:, 0:width_x + 1, 1:width_y + 1])
    v_face = v_ext[:, 1:width_x + 1, 0:width_y + 1] - COURANT * (p_ext[:, 1:width_x + 1, 1:width_y + 2] - p_ext[:, 1:width_x + 1, 0:width_y + 1])
    p_above = jnp.concatenate([pressure[1:], jnp.zeros_like(pressure[:1])], 0)
    levels = buoyancy[:, None, None]
    w_new = w_wind - COURANT * (p_above - pressure) + COURANT * levels * theta
    theta_new = theta - COURANT * levels * w_new
    w_below = jnp.concatenate([jnp.zeros_like(w_new[:1]), w_new[:-1]], 0)
    diverge = (u_face[:, 1:] - u_face[:, :-1]) + (v_face[:, :, 1:] - v_face[:, :, :-1]) + (w_new - w_below)
    p_new = pressure - COURANT * metric[None] * diverge
    return jnp.stack([u_face[:, 1:], v_face[:, :, 1:], w_new, theta_new, p_new])


def to_columns(array, size_x, size_y):
    fields = array.shape[0] * array.shape[1]
    shaped = array.reshape(array.shape[0], array.shape[1], N_GX, size_x, N_GY, size_y)
    return shaped.transpose(2, 4, 0, 1, 3, 5).reshape(N_GX * N_GY, fields, size_x * size_y)


def from_columns(columns, size_x, size_y):
    shaped = columns.reshape(N_GX, N_GY, 5, LZ, size_x, size_y)
    return shaped.transpose(2, 3, 0, 4, 1, 5).reshape(5, LZ, N_GX * size_x, N_GY * size_y)


def deliver(source_cols, count_each, picks, dest, spots, cells):
    devices = N_GX * N_GY
    owners = (jnp.arange(devices * count_each) // count_each).astype(jnp.int32)
    values = source_cols[owners, :, picks]
    flat = (dest * cells + spots).astype(jnp.int32)
    total = jnp.zeros((devices * cells, 5 * LZ), jnp.float32).at[flat].add(values)
    counts = jnp.zeros((devices * cells,), jnp.float32).at[flat].add(1.0)
    total = total.reshape(devices, cells, 5 * LZ).transpose(0, 2, 1)
    return total, counts.reshape(devices, 1, cells)


def reference(parent, metric, buoyancy, nest, nest_metric, strip_col, strip_dest, strip_pos, panel_src, panel_dest, panel_col):
    parent_cols = to_columns(parent, CX, CY)
    strip_sum, strip_count = deliver(parent_cols, SLOTS, strip_col, strip_dest[:, 0], strip_pos, NBX * NBY)
    nest_cols = (to_columns(nest, NBX, NBY) + strip_sum) / (1.0 + strip_count)
    nest_state = from_columns(nest_cols, NBX, NBY)
    blocks = nest_state.reshape(5, LZ, N_GX, NBX, N_GY, NBY).transpose(2, 4, 0, 1, 3, 5)
    block_metric = nest_metric.reshape(N_GX, NBX, N_GY, NBY).transpose(0, 2, 1, 3)
    stepper = jax.vmap(jax.vmap(small_step, in_axes=(0, 0, None)), in_axes=(0, 0, None))
    for step in range(NSN):
        blocks = stepper(blocks, block_metric, buoyancy)
    nest_out = blocks.transpose(2, 3, 0, 4, 1, 5).reshape(5, LZ, N_GX * NBX, N_GY * NBY)
    state = parent
    for step in range(NSP):
        state = small_step(state, metric, buoyancy)
    panel_sum, panel_count = deliver(to_columns(nest_out, NBX, NBY), PANELS, panel_src, panel_dest[:, 0], panel_col, CX * CY)
    final_cols = (to_columns(state, CX, CY) + panel_sum) / (1.0 + panel_count)
    return from_columns(final_cols, CX, CY), nest_out
```

```python
import functools

import jax
import jax.numpy as jnp
from jax import lax
from jax.experimental import pallas as pl
from jax.experimental.pallas import tpu as pltpu
from jax.sharding import PartitionSpec as P

CAP = 32
NSP = 4
NSN = 6
COURANT = 0.35
WIDTH = NSP

ROW = 128
SPOT = 100
TALLY = 101
DEPTH = 256
VMEM_BYTES = 48 * 1024 * 1024


def slot_rows(dest):
    groups = dest.shape[0]
    dest = dest.astype(jnp.float32)
    shape = (ROW, ROW)
    earlier = lax.broadcasted_iota(jnp.int32, shape, 0) < lax.broadcasted_iota(jnp.int32, shape, 1)
    counts = [jnp.zeros((8, ROW), jnp.float32) for _ in range(groups)]
    for a in range(groups):
        column = jnp.broadcast_to(dest[a : a + 1], shape).T
        for b in range(a, groups):
            same = column == dest[b : b + 1]
            if a == b:
                same = same & earlier
            ones = jnp.where(same, 1.0, 0.0)
            counts[b] = counts[b] + jnp.sum(ones.reshape(ROW // 8, 8, ROW), axis=0)
    rank = jnp.concatenate([jnp.sum(c, axis=0, keepdims=True) for c in counts], 0)
    return (dest * CAP + rank).astype(jnp.int32)


def to_rows(fields, rows, channels, size_x):
    tail_row = lax.broadcasted_iota(jnp.int32, (ROW - channels, ROW), 0)
    tail = jnp.where(tail_row == TALLY - channels, 1.0, 0.0)
    for i in range(size_x):
        block = fields[pl.ds(i, channels, stride=size_x), :]
        rows[i * ROW : (i + 1) * ROW, :] = jnp.concatenate([block, tail], 0).T


def pack_rows(rows, picks, spots, slots, packed):
    lane = lax.broadcasted_iota(jnp.int32, (1, ROW), 1)
    empty = jnp.where(lane == SPOT, -1.0, 0.0)
    packed[...] = jnp.broadcast_to(empty, packed.shape)
    groups = slots.shape[0]

    def group(a, carry):
        def move(b, carry):
            r = a * ROW + b
            spot = jnp.full((1, ROW), spots[r], jnp.int32).astype(jnp.float32)
            row = rows[pl.ds(picks[r], 1), :]
            packed[pl.ds(slots[a, b], 1), :] = jnp.where(lane == SPOT, spot, row)
            return carry

        return lax.fori_loop(0, ROW, move, carry, unroll=16)

    lax.fori_loop(0, groups, group, 0)


def add_rows(moved, sums, size_x):
    sums[...] = jnp.zeros(sums.shape, jnp.float32)
    lane = lax.broadcasted_iota(jnp.int32, (16, 2 * ROW), 1)
    pick = jnp.where((lane == SPOT) | (lane == SPOT + ROW), 1.0, 0.0).astype(jnp.bfloat16)
    north = lax.broadcasted_iota(jnp.int32, (ROW, DEPTH), 0)
    step = 8

    def tile(t, carry):
        values = moved[pl.ds(pl.multiple_of(t * DEPTH, DEPTH), DEPTH), :]
        high = values.astype(jnp.bfloat16)
        low = (values - high.astype(jnp.float32)).astype(jnp.bfloat16)
        both = jnp.concatenate([high, low], 1)
        spot = lax.dot_general(
            pick, both, (((1,), (1,)), ((), ())), preferred_element_type=jnp.float32
        ).astype(jnp.int32)
        east, within = spot >> 7, spot & (ROW - 1)
        column = jnp.where(north == within[0:1], 1.0, 0.0).astype(jnp.bfloat16)
        column = column.reshape(ROW // 16, 16, DEPTH)
        for g in range(size_x // step):
            parts = []
            for i in range(g * step, (g + 1) * step):
                here = jnp.where(east == i, 1.0, 0.0).astype(jnp.bfloat16)
                parts.append((column * here[None]).reshape(ROW, DEPTH))
            block = slice(g * step * ROW, (g + 1) * step * ROW)
            sums[block, :] += jnp.dot(
                jnp.concatenate(parts, 0), both, preferred_element_type=jnp.float32
            )
        return carry

    lax.fori_loop(0, moved.shape[0] // DEPTH, tile, 0)


def relax(fields, sums, out, channels, size_x):
    for i in range(size_x):
        block = slice(i * ROW, (i + 1) * ROW)
        total = (sums[block, :ROW] + sums[block, ROW:]).T
        share = 1.0 / (1.0 + total[TALLY : TALLY + 1])
        where = pl.ds(i, channels, stride=size_x)
        out[where, :] = (fields[where, :] + total[:channels]) * share


def nest_step(state, metric, buoyancy, levels, size_x):
    shape = (size_x, ROW)
    row = lax.broadcasted_iota(jnp.int32, shape, 0)
    lane = lax.broadcasted_iota(jnp.int32, shape, 1)
    scaled = COURANT * metric[...]

    def at(field, k):
        start = (field * levels + k) * size_x
        return slice(start, start + size_x)

    w_below = jnp.zeros(shape, jnp.float32)
    p = state[at(4, 0), :]
    for k in range(levels):
        n = COURANT * buoyancy[k]
        p_above = state[at(4, k + 1), :] if k + 1 < levels else jnp.zeros(shape, jnp.float32)
        p_east = jnp.where(row == size_x - 1, 0.0, pltpu.roll(p, size_x - 1, 0))
        p_north = jnp.where(lane == ROW - 1, 0.0, pltpu.roll(p, ROW - 1, 1))
        u = state[at(0, k), :] - COURANT * (p_east - p)
        v = state[at(1, k), :] - COURANT * (p_north - p)
        edge = -COURANT * p
        u_west = jnp.where(row == 0, edge, pltpu.roll(u, 1, 0))
        v_south = jnp.where(lane == 0, edge, pltpu.roll(v, 1, 1))
        theta = state[at(3, k), :]
        w = state[at(2, k), :] - COURANT * (p_above - p) + n * theta
        state[at(0, k), :] = u
        state[at(1, k), :] = v
        state[at(2, k), :] = w
        state[at(3, k), :] = theta - n * w
        state[at(4, k), :] = p - scaled * ((u - u_west) + (v - v_south) + (w - w_below))
        w_below = w
        p = p_above


def strip_kernel(parent, dest, picks, spots, packed, rows, slots_v, slots, *, size_x):
    channels = parent.shape[0] // size_x
    slots_v[...] = slot_rows(dest[...])
    pltpu.sync_copy(slots_v, slots)
    to_rows(parent, rows, channels, size_x)
    pack_rows(rows, picks, spots, slots, packed)


def nest_kernel(
    moved, nest, metric, dest, buoyancy, picks, spots, out, packed, sums, rows, slots_v, slots,
    *, size_x
):
    channels = nest.shape[0] // size_x
    slots_v[...] = slot_rows(dest[...])
    pltpu.sync_copy(slots_v, slots)
    add_rows(moved, sums, size_x)
    relax(nest, sums, out, channels, size_x)

    def step(_, carry):
        nest_step(out, metric, buoyancy, channels // 5, size_x)
        return carry

    lax.fori_loop(0, NSN, step, 0)
    to_rows(out, rows, channels, size_x)
    pack_rows(rows, picks, spots, slots, packed)


def parent_kernel(edge, buoyancy, parent, rim, side, metric, out, state, scaled):
    channels, size_x = side.shape[0] - 1, metric.shape[0]
    levels = channels // 5
    tall = side.shape[1]
    shape = (tall, 2 * ROW)
    scaled[:size_x, :ROW] = COURANT * metric[...]
    scaled[size_x:, :ROW] = COURANT * rim[channels]
    scaled[:, ROW:] = COURANT * side[channels]

    def fill(c, carry):
        state[c, :size_x, :ROW] = parent[c]
        state[c, size_x:, :ROW] = rim[c]
        state[c, :, ROW:] = side[c]
        return carry

    lax.fori_loop(0, channels, fill, 0)
    row = lax.broadcasted_iota(jnp.int32, shape, 0)
    lane = lax.broadcasted_iota(jnp.int32, shape, 1)
    u_keep = jnp.where((row >= tall - WIDTH) & (edge[0] == 1), 0.0, 1.0)
    v_keep = jnp.where((lane >= 2 * ROW - WIDTH) & (edge[1] == 1), 0.0, 1.0)

    def step(_, carry):
        def level(k, w_below):
            n = COURANT * buoyancy[k]
            p = state[4 * levels + k]
            above = state[4 * levels + jnp.minimum(k + 1, levels - 1)]
            p_above = above * jnp.where(k + 1 < levels, 1.0, 0.0)
            u = state[k] - COURANT * (pltpu.roll(p, tall - 1, 0) - p)
            v = state[levels + k] - COURANT * (pltpu.roll(p, 2 * ROW - 1, 1) - p)
            theta = state[3 * levels + k]
            w = state[2 * levels + k] - COURANT * (p_above - p) + n * theta
            spread = (u - pltpu.roll(u, 1, 0)) + (v - pltpu.roll(v, 1, 1)) + (w - w_below)
            state[k] = u * u_keep
            state[levels + k] = v * v_keep
            state[2 * levels + k] = w
            state[3 * levels + k] = theta - n * w
            state[4 * levels + k] = p - scaled[...] * spread
            return w

        lax.fori_loop(0, levels, level, jnp.zeros(shape, jnp.float32))
        return carry

    lax.fori_loop(0, NSP, step, 0)

    def drain(c, carry):
        out[c] = state[c, :size_x, :ROW]
        return carry

    lax.fori_loop(0, channels, drain, 0)


def final_kernel(moved, parent, out, sums, *, size_x):
    channels = parent.shape[0] // size_x
    add_rows(moved, sums, size_x)
    relax(parent, sums, out, channels, size_x)


def vmem():
    return pl.BlockSpec(memory_space=pltpu.VMEM)


def smem():
    return pl.BlockSpec(memory_space=pltpu.SMEM)


def params():
    return pltpu.CompilerParams(vmem_limit_bytes=VMEM_BYTES)


def exchange(packed, devices):
    moved = lax.all_to_all(
        packed.reshape(devices, CAP, ROW), ("gx", "gy"), split_axis=0, concat_axis=0, tiled=True
    )
    return moved.reshape(devices * CAP, ROW)


def shifted(first, last, axis):
    size = lax.axis_size(axis)
    up = [(i, i + 1) for i in range(size - 1)]
    down = [(j, i) for i, j in up]
    return lax.ppermute(first, axis, down), lax.ppermute(last, axis, up)


def rims(parent, metric):
    channels, size_x, size_y = parent.shape
    first = jnp.concatenate([parent[:, :WIDTH], metric[None, :WIDTH]], 0)
    last = jnp.concatenate([parent[:, size_x - WIDTH :], metric[None, size_x - WIDTH :]], 0)
    after, before = shifted(first, last, "gx")
    rim = jnp.concatenate([after, before], 1)

    def strip(lanes):
        own = jnp.concatenate([parent[:, :, lanes], metric[None, :, lanes]], 0)
        return jnp.concatenate([own, rim[:, :, lanes]], 1)

    after, before = shifted(strip(slice(0, WIDTH)), strip(slice(size_y - WIDTH, size_y)), "gy")
    gap = jnp.zeros(after.shape[:2] + (ROW - 2 * WIDTH,), jnp.float32)
    return rim, jnp.concatenate([after, gap, before], 2)


def on_device(
    parent,
    metric,
    buoyancy,
    nest,
    nest_metric,
    strip_col,
    strip_dest,
    strip_pos,
    panel_src,
    panel_dest,
    panel_col,
):
    devices = lax.axis_size("gx") * lax.axis_size("gy")
    channels = parent.shape[0] * parent.shape[1]
    tile_x, tile_y = parent.shape[2:]
    block_x, block_y = nest.shape[2:]
    slots = strip_col.shape[0]
    packed_type = jax.ShapeDtypeStruct((devices * CAP, ROW), jnp.float32)
    index_scratch = [
        pltpu.VMEM((slots // ROW, ROW), jnp.int32),
        pltpu.SMEM((slots // ROW, ROW), jnp.int32),
    ]

    packed = pl.pallas_call(
        functools.partial(strip_kernel, size_x=tile_x),
        out_shape=packed_type,
        in_specs=[vmem(), vmem(), smem(), smem()],
        out_specs=vmem(),
        scratch_shapes=[pltpu.VMEM((tile_x * tile_y, ROW), jnp.float32)] + index_scratch,
        compiler_params=params(),
        name="pack_strips",
    )(
        parent.reshape(channels * tile_x, tile_y),
        strip_dest.reshape(slots // ROW, ROW),
        strip_col,
        strip_pos,
    )

    packed, late_parent, late_metric = lax.optimization_barrier((packed, parent, metric))
    moved = exchange(packed, devices)
    late_parent = late_parent.reshape(channels, tile_x, tile_y)
    rim, side = rims(late_parent, late_metric)
    edge = jnp.stack([lax.axis_index("gx") == 0, lax.axis_index("gy") == 0]).astype(jnp.int32)
    tall = tile_x + 2 * WIDTH
    parent_state = pl.pallas_call(
        parent_kernel,
        out_shape=jax.ShapeDtypeStruct((channels, tile_x, tile_y), jnp.float32),
        in_specs=[smem(), smem(), vmem(), vmem(), vmem(), vmem()],
        out_specs=vmem(),
        scratch_shapes=[
            pltpu.VMEM((channels, tall, 2 * ROW), jnp.float32),
            pltpu.VMEM((tall, 2 * ROW), jnp.float32),
        ],
        compiler_params=params(),
        cost_estimate=pl.CostEstimate(flops=20_000_000, bytes_accessed=8_000_000, transcendentals=0),
        name="step_parent",
    )(edge, buoyancy, late_parent, rim, side, late_metric)

    nest_out, packed = pl.pallas_call(
        functools.partial(nest_kernel, size_x=block_x),
        out_shape=(
            jax.ShapeDtypeStruct((channels * block_x, block_y), jnp.float32),
            packed_type,
        ),
        in_specs=[vmem(), vmem(), vmem(), vmem(), smem(), smem(), smem()],
        out_specs=(vmem(), vmem()),
        scratch_shapes=[
            pltpu.VMEM((block_x * block_y, 2 * ROW), jnp.float32),
            pltpu.VMEM((block_x * block_y, ROW), jnp.float32),
        ]
        + index_scratch,
        compiler_params=params(),
        name="step_nest",
    )(
        moved,
        nest.reshape(channels * block_x, block_y),
        nest_metric,
        panel_dest.reshape(slots // ROW, ROW),
        buoyancy,
        panel_src,
        panel_col,
    )
    moved = exchange(packed, devices)

    parent_out = pl.pallas_call(
        functools.partial(final_kernel, size_x=tile_x),
        out_shape=jax.ShapeDtypeStruct((channels * tile_x, tile_y), jnp.float32),
        in_specs=[vmem(), vmem()],
        out_specs=vmem(),
        scratch_shapes=[pltpu.VMEM((tile_x * tile_y, 2 * ROW), jnp.float32)],
        compiler_params=params(),
        name="add_panels",
    )(moved, parent_state.reshape(channels * tile_x, tile_y))
    return (parent_out.reshape(parent.shape), nest_out.reshape(nest.shape))


def solution(mesh):
    placed = (
        P(None, None, "gx", "gy"),
        P("gx", "gy"),
        P(),
        P(None, None, "gx", "gy"),
        P("gx", "gy"),
        P(("gx", "gy")),
        P(("gx", "gy"), None),
        P(("gx", "gy")),
        P(("gx", "gy")),
        P(("gx", "gy"), None),
        P(("gx", "gy")),
    )
    return jax.shard_map(
        on_device,
        mesh=mesh,
        in_specs=placed,
        out_specs=(P(None, None, "gx", "gy"), P(None, None, "gx", "gy")),
        check_vma=False,
    )
```

```python
import functools

import jax
import jax.numpy as jnp
from jax import lax
from jax.experimental import pallas as pl
from jax.experimental.pallas import tpu as pltpu
from jax.sharding import PartitionSpec as P

CAP = 32
NSP = 4
NSN = 6
COURANT = 0.35
WIDTH = NSP

ROW = 128
SPOT = 100
TALLY = 101
DEPTH = 1024
VMEM_BYTES = 48 * 1024 * 1024


def slot_rows(dest):
    groups = dest.shape[0]
    dest = dest.astype(jnp.float32)
    shape = (ROW, ROW)
    earlier = lax.broadcasted_iota(jnp.int32, shape, 0) < lax.broadcasted_iota(jnp.int32, shape, 1)
    counts = [jnp.zeros((8, ROW), jnp.float32) for _ in range(groups)]
    for a in range(groups):
        column = jnp.broadcast_to(dest[a : a + 1], shape).T
        for b in range(a, groups):
            same = column == dest[b : b + 1]
            if a == b:
                same = same & earlier
            ones = jnp.where(same, 1.0, 0.0)
            counts[b] = counts[b] + jnp.sum(ones.reshape(ROW // 8, 8, ROW), axis=0)
    rank = jnp.concatenate([jnp.sum(c, axis=0, keepdims=True) for c in counts], 0)
    return (dest * CAP + rank).astype(jnp.int32)


def to_rows(fields, rows, channels, size_x):
    tail_row = lax.broadcasted_iota(jnp.int32, (ROW - channels, ROW), 0)
    tail = jnp.where(tail_row == TALLY - channels, 1.0, 0.0)
    for i in range(size_x):
        block = fields[pl.ds(i, channels, stride=size_x), :]
        rows[i * ROW : (i + 1) * ROW, :] = jnp.concatenate([block, tail], 0).T


def pack_rows(rows, picks, spots, slots, packed):
    lane = lax.broadcasted_iota(jnp.int32, (1, ROW), 1)
    empty = jnp.where(lane == SPOT, -1.0, 0.0)
    packed[...] = jnp.broadcast_to(empty, packed.shape)

    def move(r, carry):
        spot = jnp.full((1, ROW), spots[r], jnp.int32).astype(jnp.float32)
        row = rows[pl.ds(picks[r], 1), :]
        packed[pl.ds(slots[r], 1), :] = jnp.where(lane == SPOT, spot, row)
        return carry

    lax.fori_loop(0, slots.shape[0], move, 0, unroll=32)


def add_rows(moved, sums, size_x):
    sums[...] = jnp.zeros(sums.shape, jnp.float32)
    lane = lax.broadcasted_iota(jnp.int32, (16, 2 * ROW), 1)
    pick = jnp.where((lane == SPOT) | (lane == SPOT + ROW), 1.0, 0.0).astype(jnp.bfloat16)
    north = lax.broadcasted_iota(jnp.int32, (ROW, DEPTH), 0)
    step = 4

    def tile(t, carry):
        values = moved[pl.ds(pl.multiple_of(t * DEPTH, DEPTH), DEPTH), :]
        high = values.astype(jnp.bfloat16)
        low = (values - high.astype(jnp.float32)).astype(jnp.bfloat16)
        both = jnp.concatenate([high, low], 1)
        spot = lax.dot_general(
            pick, both, (((1,), (1,)), ((), ())), preferred_element_type=jnp.float32
        ).astype(jnp.int32)
        east, within = spot >> 7, spot & (ROW - 1)
        column = jnp.where(north == within[0:1], 1.0, 0.0).astype(jnp.bfloat16)
        column = column.reshape(ROW // 16, 16, DEPTH)
        for g in range(size_x // step):
            parts = []
            for i in range(g * step, (g + 1) * step):
                here = jnp.where(east == i, 1.0, 0.0).astype(jnp.bfloat16)
                parts.append((column * here[None]).reshape(ROW, DEPTH))
            block = slice(g * step * ROW, (g + 1) * step * ROW)
            sums[block, :] += jnp.dot(
                jnp.concatenate(parts, 0), both, preferred_element_type=jnp.float32
            )
        return carry

    lax.fori_loop(0, moved.shape[0] // DEPTH, tile, 0)


def relax(fields, sums, out, channels, size_x):
    for i in range(size_x):
        block = slice(i * ROW, (i + 1) * ROW)
        total = (sums[block, :ROW] + sums[block, ROW:]).T
        share = 1.0 / (1.0 + total[TALLY : TALLY + 1])
        where = pl.ds(i, channels, stride=size_x)
        out[where, :] = (fields[where, :] + total[:channels]) * share


def nest_step(state, metric, buoyancy, levels, size_x):
    shape = (size_x, ROW)
    row = lax.broadcasted_iota(jnp.int32, shape, 0)
    lane = lax.broadcasted_iota(jnp.int32, shape, 1)
    scaled = COURANT * metric[...]

    def at(field, k):
        start = (field * levels + k) * size_x
        return slice(start, start + size_x)

    w_below = jnp.zeros(shape, jnp.float32)
    p = state[at(4, 0), :]
    for k in range(levels):
        n = COURANT * buoyancy[k]
        p_above = state[at(4, k + 1), :] if k + 1 < levels else jnp.zeros(shape, jnp.float32)
        p_east = jnp.where(row == size_x - 1, 0.0, pltpu.roll(p, size_x - 1, 0))
        p_north = jnp.where(lane == ROW - 1, 0.0, pltpu.roll(p, ROW - 1, 1))
        u = state[at(0, k), :] - COURANT * (p_east - p)
        v = state[at(1, k), :] - COURANT * (p_north - p)
        edge = -COURANT * p
        u_west = jnp.where(row == 0, edge, pltpu.roll(u, 1, 0))
        v_south = jnp.where(lane == 0, edge, pltpu.roll(v, 1, 1))
        theta = state[at(3, k), :]
        w = state[at(2, k), :] - COURANT * (p_above - p) + n * theta
        state[at(0, k), :] = u
        state[at(1, k), :] = v
        state[at(2, k), :] = w
        state[at(3, k), :] = theta - n * w
        state[at(4, k), :] = p - scaled * ((u - u_west) + (v - v_south) + (w - w_below))
        w_below = w
        p = p_above


def strip_kernel(parent, dest, picks, spots, packed, rows, slots_v, slots, sems, *, size_x):
    channels = parent.shape[0] // size_x
    slots_v[...] = slot_rows(dest[...])
    copies = [
        pltpu.make_async_copy(slots_v.at[a], slots.at[pl.ds(a * ROW, ROW)], sems.at[a])
        for a in range(slots_v.shape[0])
    ]
    for copy in copies:
        copy.start()
    to_rows(parent, rows, channels, size_x)
    for copy in copies:
        copy.wait()
    pack_rows(rows, picks, spots, slots, packed)


def nest_kernel(
    moved, nest, metric, buoyancy, picks, spots, slots, out, packed, sums, rows, *, size_x
):
    channels = nest.shape[0] // size_x
    add_rows(moved, sums, size_x)
    relax(nest, sums, out, channels, size_x)

    def step(_, carry):
        nest_step(out, metric, buoyancy, channels // 5, size_x)
        return carry

    lax.fori_loop(0, NSN, step, 0)
    to_rows(out, rows, channels, size_x)
    pack_rows(rows, picks, spots, slots, packed)


def rim_kernel(parent, metric, after, before, dest, first, last, slots):
    channels, size_x = parent.shape[:2]
    slots[...] = slot_rows(dest[...])
    tall = size_x + 2 * WIDTH
    per = ROW // WIDTH
    lane = lax.broadcasted_iota(jnp.int32, (tall, ROW), 1) // WIDTH
    for q in range(pl.cdiv(channels + 1, per)):
        ahead = jnp.zeros((tall, ROW), jnp.float32)
        behind = ahead
        for m in range(min(per, channels + 1 - q * per)):
            c = q * per + m
            own = parent[c] if c < channels else metric[...]
            block = jnp.concatenate([own, jnp.concatenate([after[c], before[c]], 0)], 0)
            ahead = jnp.where(lane == m, pltpu.roll(block, m * WIDTH, 1), ahead)
            behind = jnp.where(lane == m, pltpu.roll(block, (m + 1) * WIDTH % ROW, 1), behind)
        first[q * tall : (q + 1) * tall, :] = ahead
        last[q * tall : (q + 1) * tall, :] = behind


def parent_kernel(
    edge, buoyancy, parent, metric, after_x, before_x, after_y, before_y, out, state, scaled
):
    channels, size_x = parent.shape[:2]
    levels = channels // 5
    tall = size_x + 2 * WIDTH
    per = ROW // WIDTH
    shape = (tall, 2 * ROW)
    group = lax.broadcasted_iota(jnp.int32, (tall, ROW), 1) // WIDTH

    def extended(c, own):
        rows = slice(c // per * tall, (c // per + 1) * tall)
        m = c % per
        ahead = pltpu.roll(after_y[rows, :], -m * WIDTH % ROW, 1)
        behind = pltpu.roll(before_y[rows, :], (per - 1 - m) * WIDTH, 1)
        side = jnp.where(group == 0, ahead, jnp.where(group == per - 1, behind, 0.0))
        middle = jnp.concatenate([own, jnp.concatenate([after_x[c], before_x[c]], 0)], 0)
        return jnp.concatenate([middle, side], 1)

    for c in range(channels):
        state[c] = extended(c, parent[c])
    scaled[...] = COURANT * extended(channels, metric[...])
    row = lax.broadcasted_iota(jnp.int32, shape, 0)
    lane = lax.broadcasted_iota(jnp.int32, shape, 1)
    u_keep = jnp.where((row >= tall - WIDTH) & (edge[0] == 1), 0.0, 1.0)
    v_keep = jnp.where((lane >= 2 * ROW - WIDTH) & (edge[1] == 1), 0.0, 1.0)

    def step(_, carry):
        w_below = jnp.zeros(shape, jnp.float32)
        p = state[4 * levels]
        for k in range(levels):
            n = COURANT * buoyancy[k]
            p_above = state[4 * levels + k + 1] if k + 1 < levels else jnp.zeros(shape, jnp.float32)
            u = state[k] - COURANT * (pltpu.roll(p, tall - 1, 0) - p)
            v = state[levels + k] - COURANT * (pltpu.roll(p, 2 * ROW - 1, 1) - p)
            theta = state[3 * levels + k]
            w = state[2 * levels + k] - COURANT * (p_above - p) + n * theta
            spread = (u - pltpu.roll(u, 1, 0)) + (v - pltpu.roll(v, 1, 1)) + (w - w_below)
            state[k] = u * u_keep
            state[levels + k] = v * v_keep
            state[2 * levels + k] = w
            state[3 * levels + k] = theta - n * w
            state[4 * levels + k] = p - scaled[...] * spread
            w_below = w
            p = p_above
        return carry

    lax.fori_loop(0, NSP, step, 0)
    for c in range(channels):
        out[c] = state[c, :size_x, :ROW]


def final_kernel(moved, parent, out, sums, *, size_x):
    channels = parent.shape[0] // size_x
    add_rows(moved, sums, size_x)
    relax(parent, sums, out, channels, size_x)


def vmem():
    return pl.BlockSpec(memory_space=pltpu.VMEM)


def smem():
    return pl.BlockSpec(memory_space=pltpu.SMEM)


def params():
    return pltpu.CompilerParams(vmem_limit_bytes=VMEM_BYTES)


def exchange(packed, devices):
    moved = lax.all_to_all(
        packed.reshape(devices, CAP, ROW), ("gx", "gy"), split_axis=0, concat_axis=0, tiled=True
    )
    return moved.reshape(devices * CAP, ROW)


def shifted(first, last, axis):
    size = lax.axis_size(axis)
    up = [(i, i + 1) for i in range(size - 1)]
    down = [(j, i) for i, j in up]
    return lax.ppermute(first, axis, down), lax.ppermute(last, axis, up)


def gx_rims(parent, metric):
    size_x = parent.shape[1]
    first = jnp.concatenate([parent[:, :WIDTH], metric[None, :WIDTH]], 0)
    last = jnp.concatenate([parent[:, size_x - WIDTH :], metric[None, size_x - WIDTH :]], 0)
    return shifted(first, last, "gx")


def on_device(
    parent,
    metric,
    buoyancy,
    nest,
    nest_metric,
    strip_col,
    strip_dest,
    strip_pos,
    panel_src,
    panel_dest,
    panel_col,
):
    devices = lax.axis_size("gx") * lax.axis_size("gy")
    channels = parent.shape[0] * parent.shape[1]
    tile_x, tile_y = parent.shape[2:]
    block_x, block_y = nest.shape[2:]
    slots = strip_col.shape[0]
    packed_type = jax.ShapeDtypeStruct((devices * CAP, ROW), jnp.float32)
    groups = slots // ROW

    packed = pl.pallas_call(
        functools.partial(strip_kernel, size_x=tile_x),
        out_shape=packed_type,
        in_specs=[vmem(), vmem(), smem(), smem()],
        out_specs=vmem(),
        scratch_shapes=[
            pltpu.VMEM((tile_x * tile_y, ROW), jnp.float32),
            pltpu.VMEM((groups, ROW), jnp.int32),
            pltpu.SMEM((slots,), jnp.int32),
            pltpu.SemaphoreType.DMA((groups,)),
        ],
        compiler_params=params(),
        name="pack_strips",
    )(
        parent.reshape(channels * tile_x, tile_y),
        strip_dest.reshape(groups, ROW),
        strip_col,
        strip_pos,
    )

    packed, late_parent, late_metric, late_dest = lax.optimization_barrier(
        (packed, parent, metric, panel_dest)
    )
    moved = exchange(packed, devices)
    late_parent = late_parent.reshape(channels, tile_x, tile_y)
    after_x, before_x = gx_rims(late_parent, late_metric)
    strip_type = jax.ShapeDtypeStruct(
        (pl.cdiv(channels + 1, ROW // WIDTH) * (tile_x + 2 * WIDTH), ROW), jnp.float32
    )
    first, last, panel_slots = pl.pallas_call(
        rim_kernel,
        out_shape=(strip_type, strip_type, jax.ShapeDtypeStruct((groups, ROW), jnp.int32)),
        in_specs=[vmem()] * 5,
        out_specs=(vmem(),) * 3,
        compiler_params=params(),
        cost_estimate=pl.CostEstimate(flops=3_000_000, bytes_accessed=2_000_000, transcendentals=0),
        name="pack_rims",
    )(late_parent, late_metric, after_x, before_x, late_dest.reshape(groups, ROW))
    after_y, before_y = shifted(first, last, "gy")
    moved, after_x, before_x, after_y, before_y, panel_slots = lax.optimization_barrier(
        (moved, after_x, before_x, after_y, before_y, panel_slots)
    )
    edge = jnp.stack([lax.axis_index("gx") == 0, lax.axis_index("gy") == 0]).astype(jnp.int32)
    tall = tile_x + 2 * WIDTH
    parent_state = pl.pallas_call(
        parent_kernel,
        out_shape=jax.ShapeDtypeStruct((channels, tile_x, tile_y), jnp.float32),
        in_specs=[smem(), smem()] + [vmem()] * 6,
        out_specs=vmem(),
        scratch_shapes=[
            pltpu.VMEM((channels, tall, 2 * ROW), jnp.float32),
            pltpu.VMEM((tall, 2 * ROW), jnp.float32),
        ],
        compiler_params=params(),
        cost_estimate=pl.CostEstimate(flops=20_000_000, bytes_accessed=8_000_000, transcendentals=0),
        name="step_parent",
    )(edge, buoyancy, late_parent, late_metric, after_x, before_x, after_y, before_y)

    nest_out, packed = pl.pallas_call(
        functools.partial(nest_kernel, size_x=block_x),
        out_shape=(
            jax.ShapeDtypeStruct((channels * block_x, block_y), jnp.float32),
            packed_type,
        ),
        in_specs=[vmem(), vmem(), vmem(), smem(), smem(), smem(), smem()],
        out_specs=(vmem(), vmem()),
        scratch_shapes=[
            pltpu.VMEM((block_x * block_y, 2 * ROW), jnp.float32),
            pltpu.VMEM((block_x * block_y, ROW), jnp.float32),
        ],
        compiler_params=params(),
        name="step_nest",
    )(
        moved,
        nest.reshape(channels * block_x, block_y),
        nest_metric,
        buoyancy,
        panel_src,
        panel_col,
        panel_slots.reshape(slots),
    )
    moved = exchange(packed, devices)

    parent_out = pl.pallas_call(
        functools.partial(final_kernel, size_x=tile_x),
        out_shape=jax.ShapeDtypeStruct((channels * tile_x, tile_y), jnp.float32),
        in_specs=[vmem(), vmem()],
        out_specs=vmem(),
        scratch_shapes=[pltpu.VMEM((tile_x * tile_y, 2 * ROW), jnp.float32)],
        compiler_params=params(),
        name="add_panels",
    )(moved, parent_state.reshape(channels * tile_x, tile_y))
    return (parent_out.reshape(parent.shape), nest_out.reshape(nest.shape))


def solution(mesh):
    placed = (
        P(None, None, "gx", "gy"),
        P("gx", "gy"),
        P(),
        P(None, None, "gx", "gy"),
        P("gx", "gy"),
        P(("gx", "gy")),
        P(("gx", "gy"), None),
        P(("gx", "gy")),
        P(("gx", "gy")),
        P(("gx", "gy"), None),
        P(("gx", "gy")),
    )
    return jax.shard_map(
        on_device,
        mesh=mesh,
        in_specs=placed,
        out_specs=(P(None, None, "gx", "gy"), P(None, None, "gx", "gy")),
        check_vma=False,
    )
```

```python
import functools

import jax
import jax.numpy as jnp
from jax import lax
from jax.experimental import pallas as pl
from jax.experimental.pallas import tpu as pltpu
from jax.sharding import PartitionSpec as P

CAP = 32
NSP = 4
NSN = 6
COURANT = 0.35
WIDTH = NSP

ROW = 128
SPOT = 100
TALLY = 101
FREE = SPOT + 1
PIECE = ROW - FREE
PIECES = 4
KEEP = 26
REST = CAP - KEEP
GROUP = 8
STEP = 4
VMEM_BYTES = 60 * 1024 * 1024


def slot_rows(dest, spot, cells):
    groups = dest.shape[0]
    shape = (ROW, ROW)
    row = lax.broadcasted_iota(jnp.int32, dest.shape, 0)
    lane = lax.broadcasted_iota(jnp.int32, dest.shape, 1)
    high = spot >= cells // 2
    side = jnp.where(high, 1, 0)
    inward = jnp.where(high, cells - 1 - spot, spot)
    least = (dest * 2 + side) << 21
    key = least + (inward << 10) + (row * ROW + lane)
    counts = [jnp.zeros((8, ROW), jnp.float32) for _ in range(groups)]
    for a in range(groups):
        column = jnp.broadcast_to(key[a : a + 1], shape).T
        for b in range(groups):
            before = (column >= least[b : b + 1]) & (column < key[b : b + 1])
            ones = jnp.where(before, 1.0, 0.0)
            counts[b] = counts[b] + jnp.sum(ones.reshape(ROW // 8, 8, ROW), axis=0)
    rank = jnp.concatenate([jnp.sum(c, axis=0, keepdims=True) for c in counts], 0)
    rank = rank.astype(jnp.int32)
    slot = jnp.where(high, CAP - 1 - rank, rank)
    devices = ROW
    spill = devices * KEEP + (slot - KEEP) * devices + dest
    return jnp.where(slot < KEEP, dest * KEEP + slot, spill)


def to_rows(fields, rows, channels, size_x):
    tail = jnp.zeros((ROW - channels, ROW), jnp.float32)
    for i in range(size_x):
        block = fields[pl.ds(i, channels, stride=size_x), :]
        rows[i * ROW : (i + 1) * ROW, :] = jnp.concatenate([block, tail], 0).T


def clear_rows(staged):
    lane = lax.broadcasted_iota(jnp.int32, (1, ROW), 1)
    staged[...] = jnp.broadcast_to(jnp.where(lane == SPOT, -1.0, 0.0), staged.shape)


def pack_rows(rows, picks, spots, slots, staged, packed, sems):
    lane = lax.broadcasted_iota(jnp.int32, (1, ROW), 1)
    devices = packed.shape[0] // KEEP

    def move(r, carry):
        spot = jnp.full((1, ROW), spots[r], jnp.int32).astype(jnp.float32)
        row = rows[pl.ds(picks[r], 1), :]
        staged[pl.ds(slots[r], 1), :] = jnp.where(lane == SPOT, spot, row)
        return carry

    lax.fori_loop(0, slots.shape[0], move, 0, unroll=32)
    parts = sems.shape[0]
    count = devices // parts
    free = lax.broadcasted_iota(jnp.int32, (count, ROW), 1) >= FREE
    copies = []
    for part in range(parts):
        base = part * count
        for a in range(REST):
            start = devices * (KEEP + a) + base
            values = staged[start : start + count, :]
            for b in range(PIECES):
                where = pl.ds(base * KEEP + b * REST + a, count, stride=KEEP)
                piece = pltpu.roll(values, (FREE - b * PIECE) % ROW, 1)
                staged[where, :] = jnp.where(free, piece, staged[where, :])
        block = pl.ds(base * KEEP, count * KEEP)
        copies.append(pltpu.make_async_copy(staged.at[block], packed.at[block], sems.at[part]))
        copies[-1].start()
    return copies


def slot_values(moved, s):
    devices = moved.shape[0] // KEEP
    if s < KEEP:
        return moved[pl.ds(s, devices, stride=KEEP), :]
    lane = lax.broadcasted_iota(jnp.int32, (devices, ROW), 1)
    values = jnp.zeros((devices, ROW), jnp.float32)
    for b in range(PIECES):
        piece = moved[pl.ds(b * REST + s - KEEP, devices, stride=KEEP), :]
        piece = pltpu.roll(piece, (b * PIECE - FREE) % ROW, 1)
        values = jnp.where((lane >= b * PIECE) & (lane < (b + 1) * PIECE), piece, values)
    return values


def add_rows(moved, sums, size_x):
    lane = lax.broadcasted_iota(jnp.int32, (16, 2 * ROW), 1)
    pick = jnp.where((lane == SPOT) | (lane == SPOT + ROW), 1.0, 0.0).astype(jnp.bfloat16)
    depth = moved.shape[0] // KEEP * GROUP
    north = lax.broadcasted_iota(jnp.int32, (ROW, depth), 0)
    tally = lax.broadcasted_iota(jnp.int32, (depth, ROW), 1) == TALLY
    for t in range(CAP // GROUP):
        values = [slot_values(moved, t * GROUP + k) for k in range(GROUP)]
        values = jnp.where(tally, 1.0, jnp.concatenate(values, 0))
        high = values.astype(jnp.bfloat16)
        low = (values - high.astype(jnp.float32)).astype(jnp.bfloat16)
        both = jnp.concatenate([high, low], 1)
        spot = lax.dot_general(
            pick, both, (((1,), (1,)), ((), ())), preferred_element_type=jnp.float32
        )
        whole = spot.astype(jnp.int32)
        east, within = whole >> 7, whole & (ROW - 1)
        used = spot[0:8] >= 0.0
        reach = east[0:8].astype(jnp.float32)
        first = jnp.min(jnp.where(used, reach, float(size_x))).astype(jnp.int32)
        last = jnp.max(jnp.where(used, reach, -1.0)).astype(jnp.int32)
        blocks = jnp.maximum(last - first + STEP, 0) // STEP
        start = jnp.minimum(first, size_x - blocks * STEP)
        column = jnp.where(north == within[0:1], 1.0, 0.0).astype(jnp.bfloat16)
        column = column.reshape(ROW // 16, 16, depth)

        def block(g, carry, start=start, east=east, column=column, both=both):
            here = start + g * STEP
            parts = []
            for k in range(STEP):
                mine = jnp.where(east == here + k, 1.0, 0.0).astype(jnp.bfloat16)
                parts.append((column * mine[None]).reshape(ROW, depth))
            where = pl.ds(pl.multiple_of(here * ROW, ROW), STEP * ROW)
            sums[where, :] += jnp.dot(
                jnp.concatenate(parts, 0), both, preferred_element_type=jnp.float32
            )
            return carry

        lax.fori_loop(0, blocks, block, 0)


def relax(fields, sums, out, channels, size_x, i):
    block = slice(i * ROW, (i + 1) * ROW)
    total = (sums[block, :ROW] + sums[block, ROW:]).T
    share = 1.0 / (1.0 + total[TALLY : TALLY + 1])
    where = pl.ds(i, channels, stride=size_x)
    out[where, :] = (fields[where, :] + total[:channels]) * share


def nest_step(state, metric, buoyancy, levels, size_x):
    shape = (size_x, ROW)
    row = lax.broadcasted_iota(jnp.int32, shape, 0)
    lane = lax.broadcasted_iota(jnp.int32, shape, 1)
    scaled = COURANT * metric[...]

    def at(field, k):
        start = (field * levels + k) * size_x
        return slice(start, start + size_x)

    w_below = jnp.zeros(shape, jnp.float32)
    p = state[at(4, 0), :]
    for k in range(levels):
        n = COURANT * buoyancy[k]
        p_above = state[at(4, k + 1), :] if k + 1 < levels else jnp.zeros(shape, jnp.float32)
        p_east = jnp.where(row == size_x - 1, 0.0, pltpu.roll(p, size_x - 1, 0))
        p_north = jnp.where(lane == ROW - 1, 0.0, pltpu.roll(p, ROW - 1, 1))
        u = state[at(0, k), :] - COURANT * (p_east - p)
        v = state[at(1, k), :] - COURANT * (p_north - p)
        edge = -COURANT * p
        u_west = jnp.where(row == 0, edge, pltpu.roll(u, 1, 0))
        v_south = jnp.where(lane == 0, edge, pltpu.roll(v, 1, 1))
        theta = state[at(3, k), :]
        w = state[at(2, k), :] - COURANT * (p_above - p) + n * theta
        state[at(0, k), :] = u
        state[at(1, k), :] = v
        state[at(2, k), :] = w
        state[at(3, k), :] = theta - n * w
        state[at(4, k), :] = p - scaled * ((u - u_west) + (v - v_south) + (w - w_below))
        w_below = w
        p = p_above


def fetch(pairs, sems):
    copies = [pltpu.make_async_copy(a, b, sems.at[i]) for i, (a, b) in enumerate(pairs)]
    for copy in copies:
        copy.start()
    return copies


def strip_kernel(
    parent, dest, picks, spots, spot_rows, packed,
    tile, dest_v, picks_s, spots_s, spots_v, rows, staged, slots_v, slots, sems, slot_sems, out_sems,
    *, size_x, cells
):
    channels = parent.shape[0] // size_x
    copies = fetch(
        [(dest, dest_v), (spot_rows, spots_v), (parent, tile), (picks, picks_s), (spots, spots_s)],
        sems,
    )
    clear_rows(staged)
    copies[0].wait()
    copies[1].wait()
    slots_v[...] = slot_rows(dest_v[...], spots_v[...], cells)
    moves = fetch(
        [(slots_v.at[a], slots.at[pl.ds(a * ROW, ROW)]) for a in range(slots_v.shape[0])], slot_sems
    )
    copies[2].wait()
    to_rows(tile, rows, channels, size_x)
    for copy in copies[3:] + moves:
        copy.wait()
    for copy in pack_rows(rows, picks_s, spots_s, slots, staged, packed, out_sems):
        copy.wait()


def nest_kernel(
    moved, nest, metric, buoyancy, picks, spots, slots, out, packed,
    came, tile, state, sums, rows, staged, sems, out_sems,
    *, size_x
):
    channels = nest.shape[0] // size_x
    copies = fetch([(moved, came), (nest, tile)], sems)
    sums[...] = jnp.zeros(sums.shape, jnp.float32)
    clear_rows(staged)
    copies[0].wait()
    add_rows(came, sums, size_x)
    copies[1].wait()
    for i in range(size_x):
        relax(tile, sums, state, channels, size_x, i)

    def step(_, carry):
        nest_step(state, metric, buoyancy, channels // 5, size_x)
        return carry

    lax.fori_loop(0, NSN, step, 0)
    result = pltpu.make_async_copy(state, out, sems.at[2])
    result.start()
    to_rows(state, rows, channels, size_x)
    for copy in pack_rows(rows, picks, spots, slots, staged, packed, out_sems):
        copy.wait()
    result.wait()


def rim_kernel(parent, metric, dest, spots, first_x, last_x, first_y, last_y, slots):
    size_x = metric.shape[0]
    channels = parent.shape[0] // size_x
    slots[...] = slot_rows(dest[...], spots[...], size_x * ROW)
    for r in range(WIDTH):
        there = pl.ds(r, channels, stride=WIDTH)
        end = size_x - WIDTH + r
        first_x[there, :] = parent[pl.ds(r, channels, stride=size_x), :]
        last_x[there, :] = parent[pl.ds(end, channels, stride=size_x), :]
        own = channels * WIDTH + r
        first_x[own : own + 1, :] = metric[r : r + 1]
        last_x[own : own + 1, :] = metric[end : end + 1]

    def rows(c):
        return parent[c * size_x : (c + 1) * size_x, :] if c < channels else metric[...]

    gather_lanes(rows, channels + 1, size_x, first_y, last_y, size_x, 0)


def gather_lanes(rows, count, height, first, last, pitch, offset):
    per = ROW // WIDTH
    lane = lax.broadcasted_iota(jnp.int32, (height, ROW), 1) // WIDTH
    for q in range(pl.cdiv(count, per)):
        ahead = jnp.zeros((height, ROW), jnp.float32)
        behind = ahead
        for m in range(min(per, count - q * per)):
            own = rows(q * per + m)
            ahead = jnp.where(lane == m, pltpu.roll(own, m * WIDTH, 1), ahead)
            behind = jnp.where(lane == m, pltpu.roll(own, (m + 1) * WIDTH % ROW, 1), behind)
        where = slice(q * pitch + offset, q * pitch + offset + height)
        first[where, :] = ahead
        last[where, :] = behind


def corner_kernel(own_first, own_last, after, before, first, last):
    count = after.shape[0] // WIDTH
    quarters = pl.cdiv(count, ROW // WIDTH)
    size_x = own_first.shape[0] // quarters
    tall = size_x + 2 * WIDTH
    for q in range(quarters):
        first[q * tall : q * tall + size_x, :] = own_first[q * size_x : (q + 1) * size_x, :]
        last[q * tall : q * tall + size_x, :] = own_last[q * size_x : (q + 1) * size_x, :]

    def rows(c):
        rim = slice(c * WIDTH, (c + 1) * WIDTH)
        return jnp.concatenate([after[rim, :], before[rim, :]], 0)

    gather_lanes(rows, count, 2 * WIDTH, first, last, tall, size_x)


def parent_kernel(
    edge, buoyancy, parent, metric, after_x, before_x, after_y, before_y, out, state, scaled
):
    size_x = metric.shape[0]
    channels = parent.shape[0] // size_x
    levels = channels // 5
    tall = size_x + 2 * WIDTH
    per = ROW // WIDTH
    shape = (tall, 2 * ROW)
    group = lax.broadcasted_iota(jnp.int32, (tall, ROW), 1) // WIDTH

    def extended(c, own):
        m = c % per
        rows = slice(c // per * tall, (c // per + 1) * tall)
        ahead = pltpu.roll(after_y[rows, :], -m * WIDTH % ROW, 1)
        behind = pltpu.roll(before_y[rows, :], (per - 1 - m) * WIDTH, 1)
        side = jnp.where(group == 0, ahead, jnp.where(group == per - 1, behind, 0.0))
        rim = slice(c * WIDTH, (c + 1) * WIDTH)
        beyond = jnp.concatenate([after_x[rim, :], before_x[rim, :]], 0)
        return jnp.concatenate([jnp.concatenate([own, beyond], 0), side], 1)

    for c in range(channels):
        state[c] = extended(c, parent[c * size_x : (c + 1) * size_x, :])
    scaled[...] = COURANT * extended(channels, metric[...])
    row = lax.broadcasted_iota(jnp.int32, shape, 0)
    lane = lax.broadcasted_iota(jnp.int32, shape, 1)
    u_keep = jnp.where((row >= tall - WIDTH) & (edge[0] == 1), 0.0, 1.0)
    v_keep = jnp.where((lane >= 2 * ROW - WIDTH) & (edge[1] == 1), 0.0, 1.0)

    def step(_, carry):
        w_below = jnp.zeros(shape, jnp.float32)
        p = state[4 * levels]
        for k in range(levels):
            n = COURANT * buoyancy[k]
            p_above = state[4 * levels + k + 1] if k + 1 < levels else jnp.zeros(shape, jnp.float32)
            u = state[k] - COURANT * (pltpu.roll(p, tall - 1, 0) - p)
            v = state[levels + k] - COURANT * (pltpu.roll(p, 2 * ROW - 1, 1) - p)
            theta = state[3 * levels + k]
            w = state[2 * levels + k] - COURANT * (p_above - p) + n * theta
            spread = (u - pltpu.roll(u, 1, 0)) + (v - pltpu.roll(v, 1, 1)) + (w - w_below)
            state[k] = u * u_keep
            state[levels + k] = v * v_keep
            state[2 * levels + k] = w
            state[3 * levels + k] = theta - n * w
            state[4 * levels + k] = p - scaled[...] * spread
            w_below = w
            p = p_above
        return carry

    lax.fori_loop(0, NSP, step, 0)
    for c in range(channels):
        out[c * size_x : (c + 1) * size_x, :] = state[c, :size_x, :ROW]


def final_kernel(moved, parent, out, came, tile, sums, sems, *, size_x):
    channels = parent.shape[0] // size_x
    copies = fetch([(moved, came), (parent, tile)], sems)
    sums[...] = jnp.zeros(sums.shape, jnp.float32)
    copies[0].wait()
    add_rows(came, sums, size_x)
    copies[1].wait()
    for i in range(size_x):
        relax(tile, sums, tile, channels, size_x, i)
    result = pltpu.make_async_copy(tile, out, sems.at[2])
    result.start()
    result.wait()


def vmem():
    return pl.BlockSpec(memory_space=pltpu.VMEM)


def smem():
    return pl.BlockSpec(memory_space=pltpu.SMEM)


def anywhere():
    return pl.BlockSpec(memory_space=pltpu.HBM)


def params():
    return pltpu.CompilerParams(vmem_limit_bytes=VMEM_BYTES)


def exchange(packed, devices):
    moved = lax.all_to_all(
        packed.reshape(devices, KEEP * ROW), ("gx", "gy"), split_axis=0, concat_axis=0, tiled=True
    )
    return moved.reshape(devices * KEEP, ROW)


def shifted(first, last, axis):
    size = lax.axis_size(axis)
    up = [(i, i + 1) for i in range(size - 1)]
    down = [(j, i) for i, j in up]
    return lax.ppermute(first, axis, down), lax.ppermute(last, axis, up)


def on_device(
    parent,
    metric,
    buoyancy,
    nest,
    nest_metric,
    strip_col,
    strip_dest,
    strip_pos,
    panel_src,
    panel_dest,
    panel_col,
):
    devices = lax.axis_size("gx") * lax.axis_size("gy")
    channels = parent.shape[0] * parent.shape[1]
    tile_x, tile_y = parent.shape[2:]
    block_x, block_y = nest.shape[2:]
    slots = strip_col.shape[0]
    groups = slots // ROW
    tile_shape = (channels * tile_x, tile_y)
    block_shape = (channels * block_x, block_y)
    packed_shape = (devices * KEEP, ROW)
    parts = 4

    def shape(*dims, dtype=jnp.float32):
        return jax.ShapeDtypeStruct(dims, dtype)

    def index(memory):
        return memory((slots,), jnp.int32)

    listed = pltpu.VMEM((groups, ROW), jnp.int32)
    packed = pl.pallas_call(
        functools.partial(strip_kernel, size_x=tile_x, cells=block_x * block_y),
        out_shape=shape(*packed_shape),
        in_specs=[anywhere()] * 5,
        out_specs=anywhere(),
        scratch_shapes=[
            pltpu.VMEM(tile_shape, jnp.float32),
            listed,
            index(pltpu.SMEM),
            index(pltpu.SMEM),
            listed,
            pltpu.VMEM((tile_x * tile_y, ROW), jnp.float32),
            pltpu.VMEM((devices * CAP, ROW), jnp.float32),
            listed,
            index(pltpu.SMEM),
            pltpu.SemaphoreType.DMA((5,)),
            pltpu.SemaphoreType.DMA((groups,)),
            pltpu.SemaphoreType.DMA((parts,)),
        ],
        compiler_params=params(),
        name="pack_strips",
    )(
        parent.reshape(tile_shape),
        strip_dest.reshape(groups, ROW),
        strip_col,
        strip_pos,
        strip_pos.reshape(groups, ROW),
    )

    packed, late_parent, late_metric, late_dest, late_col = lax.optimization_barrier(
        (packed, parent.reshape(tile_shape), metric, panel_dest, panel_col)
    )
    moved = exchange(packed, devices)
    rim_x = shape((channels + 1) * WIDTH, ROW)
    quarters = pl.cdiv(channels + 1, ROW // WIDTH)
    rim_y = shape(quarters * tile_x, ROW)
    first_x, last_x, own_first, own_last, panel_slots = pl.pallas_call(
        rim_kernel,
        out_shape=(rim_x, rim_x, rim_y, rim_y, shape(groups, ROW, dtype=jnp.int32)),
        in_specs=[vmem()] * 4,
        out_specs=(vmem(),) * 5,
        compiler_params=params(),
        cost_estimate=pl.CostEstimate(flops=3_000_000, bytes_accessed=2_000_000, transcendentals=0),
        name="pack_rims",
    )(late_parent, late_metric, late_dest.reshape(groups, ROW), late_col.reshape(groups, ROW))
    after_x, before_x = shifted(first_x, last_x, "gx")
    moved, after_x, before_x, panel_slots = lax.optimization_barrier(
        (moved, after_x, before_x, panel_slots)
    )
    tall = tile_x + 2 * WIDTH
    tall_y = shape(quarters * tall, ROW)
    first_y, last_y = pl.pallas_call(
        corner_kernel,
        out_shape=(tall_y, tall_y),
        in_specs=[vmem()] * 4,
        out_specs=(vmem(),) * 2,
        compiler_params=params(),
        name="pack_corners",
    )(own_first, own_last, after_x, before_x)
    after_y, before_y = shifted(first_y, last_y, "gy")
    nest_out, packed = pl.pallas_call(
        functools.partial(nest_kernel, size_x=block_x),
        out_shape=(shape(*block_shape), shape(*packed_shape)),
        in_specs=[anywhere(), anywhere(), vmem()] + [smem()] * 4,
        out_specs=(anywhere(), anywhere()),
        scratch_shapes=[
            pltpu.VMEM(packed_shape, jnp.float32),
            pltpu.VMEM(block_shape, jnp.float32),
            pltpu.VMEM(block_shape, jnp.float32),
            pltpu.VMEM((block_x * block_y, 2 * ROW), jnp.float32),
            pltpu.VMEM((block_x * block_y, ROW), jnp.float32),
            pltpu.VMEM((devices * CAP, ROW), jnp.float32),
            pltpu.SemaphoreType.DMA((3,)),
            pltpu.SemaphoreType.DMA((parts,)),
        ],
        compiler_params=params(),
        name="step_nest",
    )(
        moved,
        nest.reshape(block_shape),
        nest_metric,
        buoyancy,
        panel_src,
        panel_col,
        panel_slots.reshape(slots),
    )
    packed, after_y, before_y = lax.optimization_barrier((packed, after_y, before_y))
    moved = exchange(packed, devices)
    edge = jnp.stack([lax.axis_index("gx") == 0, lax.axis_index("gy") == 0]).astype(jnp.int32)
    parent_state = pl.pallas_call(
        parent_kernel,
        out_shape=shape(*tile_shape),
        in_specs=[smem(), smem()] + [vmem()] * 6,
        out_specs=vmem(),
        scratch_shapes=[
            pltpu.VMEM((channels, tall, 2 * ROW), jnp.float32),
            pltpu.VMEM((tall, 2 * ROW), jnp.float32),
        ],
        compiler_params=params(),
        cost_estimate=pl.CostEstimate(flops=20_000_000, bytes_accessed=8_000_000, transcendentals=0),
        name="step_parent",
    )(edge, buoyancy, late_parent, late_metric, after_x, before_x, after_y, before_y)

    parent_out = pl.pallas_call(
        functools.partial(final_kernel, size_x=tile_x),
        out_shape=shape(*tile_shape),
        in_specs=[anywhere(), anywhere()],
        out_specs=anywhere(),
        scratch_shapes=[
            pltpu.VMEM(packed_shape, jnp.float32),
            pltpu.VMEM(tile_shape, jnp.float32),
            pltpu.VMEM((tile_x * tile_y, 2 * ROW), jnp.float32),
            pltpu.SemaphoreType.DMA((3,)),
        ],
        compiler_params=params(),
        name="add_panels",
    )(moved, parent_state)
    return (parent_out.reshape(parent.shape), nest_out.reshape(nest.shape))


def solution(mesh):
    placed = (
        P(None, None, "gx", "gy"),
        P("gx", "gy"),
        P(),
        P(None, None, "gx", "gy"),
        P("gx", "gy"),
        P(("gx", "gy")),
        P(("gx", "gy"), None),
        P(("gx", "gy")),
        P(("gx", "gy")),
        P(("gx", "gy"), None),
        P(("gx", "gy")),
    )
    return jax.shard_map(
        on_device,
        mesh=mesh,
        in_specs=placed,
        out_specs=(P(None, None, "gx", "gy"), P(None, None, "gx", "gy")),
        check_vma=False,
    )
```

```python
import functools

import jax
import jax.numpy as jnp
from jax import lax
from jax.experimental import pallas as pl
from jax.experimental.pallas import tpu as pltpu
from jax.sharding import PartitionSpec as P

CAP = 32
NSP = 4
NSN = 6
COURANT = 0.35
WIDTH = NSP

ROW = 128
SPOT = 100
TALLY = 101
FREE = SPOT + 1
PIECE = ROW - FREE
PIECES = 4
KEEP = 26
REST = CAP - KEEP
GROUP = 8
STEP = 2
VMEM_BYTES = 65500 * 1024


def slot_rows(dest, spot, cells):
    groups = dest.shape[0]
    shape = (ROW, ROW)
    row = lax.broadcasted_iota(jnp.int32, dest.shape, 0)
    lane = lax.broadcasted_iota(jnp.int32, dest.shape, 1)
    high = spot >= cells // 2
    side = jnp.where(high, 1, 0)
    inward = jnp.where(high, cells - 1 - spot, spot)
    least = (dest * 2 + side) << 21
    key = least + (inward << 10) + (row * ROW + lane)
    counts = [jnp.zeros((8, ROW), jnp.float32) for _ in range(groups)]
    for a in range(groups):
        column = jnp.broadcast_to(key[a : a + 1], shape).T
        for b in range(groups):
            before = (column >= least[b : b + 1]) & (column < key[b : b + 1])
            ones = jnp.where(before, 1.0, 0.0)
            counts[b] = counts[b] + jnp.sum(ones.reshape(ROW // 8, 8, ROW), axis=0)
    rank = jnp.concatenate([jnp.sum(c, axis=0, keepdims=True) for c in counts], 0)
    rank = rank.astype(jnp.int32)
    slot = jnp.where(high, CAP - 1 - rank, rank)
    devices = ROW
    spill = devices * KEEP + (slot - KEEP) * devices + dest
    return jnp.where(slot < KEEP, dest * KEEP + slot, spill)


def to_rows(fields, rows, channels, size_x):
    tail = jnp.zeros((ROW - channels, ROW), jnp.float32)
    for i in range(size_x):
        block = fields[pl.ds(i, channels, stride=size_x), :]
        rows[i * ROW : (i + 1) * ROW, :] = jnp.concatenate([block, tail], 0).T


def clear_rows(staged):
    lane = lax.broadcasted_iota(jnp.int32, (1, ROW), 1)
    staged[...] = jnp.broadcast_to(jnp.where(lane == SPOT, -1.0, 0.0), staged.shape)


def pack_rows(rows, picks, spots, slots, staged, packed, sems):
    lane = lax.broadcasted_iota(jnp.int32, (1, ROW), 1)
    devices = packed.shape[0] // KEEP

    def move(r, carry):
        spot = jnp.full((1, ROW), spots[r], jnp.int32).astype(jnp.float32)
        row = rows[pl.ds(picks[r], 1), :]
        staged[pl.ds(slots[r], 1), :] = jnp.where(lane == SPOT, spot, row)
        return carry

    lax.fori_loop(0, slots.shape[0], move, 0, unroll=32)
    parts = sems.shape[0]
    count = devices // parts
    free = lax.broadcasted_iota(jnp.int32, (count, ROW), 1) >= FREE
    copies = []
    for part in range(parts):
        base = part * count
        for a in range(REST):
            start = devices * (KEEP + a) + base
            values = staged[start : start + count, :]
            for b in range(PIECES):
                where = pl.ds(base * KEEP + b * REST + a, count, stride=KEEP)
                piece = pltpu.roll(values, (FREE - b * PIECE) % ROW, 1)
                staged[where, :] = jnp.where(free, piece, staged[where, :])
        block = pl.ds(base * KEEP, count * KEEP)
        copies.append(pltpu.make_async_copy(staged.at[block], packed.at[block], sems.at[part]))
        copies[-1].start()
    return copies


def slot_values(moved, s):
    devices = moved.shape[0] // KEEP
    if s < KEEP:
        return moved[pl.ds(s, devices, stride=KEEP), :]
    lane = lax.broadcasted_iota(jnp.int32, (devices, ROW), 1)
    values = jnp.zeros((devices, ROW), jnp.float32)
    for b in range(PIECES):
        piece = moved[pl.ds(b * REST + s - KEEP, devices, stride=KEEP), :]
        piece = pltpu.roll(piece, (b * PIECE - FREE) % ROW, 1)
        values = jnp.where((lane >= b * PIECE) & (lane < (b + 1) * PIECE), piece, values)
    return values


def prepare(moved, weights, columns, easts, size_x):
    lane = lax.broadcasted_iota(jnp.int32, (16, 2 * ROW), 1)
    pick = jnp.where((lane == SPOT) | (lane == SPOT + ROW), 1.0, 0.0).astype(jnp.bfloat16)
    devices = moved.shape[0] // KEEP
    depth = devices * GROUP
    tiles = CAP // GROUP
    north = lax.broadcasted_iota(jnp.int32, (ROW, depth), 0)
    tally = lax.broadcasted_iota(jnp.int32, (devices, ROW), 1) == TALLY
    reaches = []
    for t in range(tiles):
        for k in range(GROUP):
            values = jnp.where(tally, 1.0, slot_values(moved, t * GROUP + k))
            high = values.astype(jnp.bfloat16)
            low = (values - high.astype(jnp.float32)).astype(jnp.bfloat16)
            where = slice(k * devices, (k + 1) * devices)
            weights[t, where, :ROW] = high
            weights[t, where, ROW:] = low
        spot = lax.dot_general(
            pick, weights[t], (((1,), (1,)), ((), ())), preferred_element_type=jnp.float32
        )
        whole = spot.astype(jnp.int32)
        east, within = whole >> 7, whole & (ROW - 1)
        easts[t] = east
        columns[t] = jnp.where(north == within[0:1], 1.0, 0.0).astype(jnp.bfloat16)
        used = spot[0:8] >= 0.0
        reach = east[0:8].astype(jnp.float32)
        first = jnp.min(jnp.where(used, reach, float(size_x)))
        last = jnp.max(jnp.where(used, reach, -1.0))
        reaches.append((first.astype(jnp.int32), last.astype(jnp.int32)))
    return reaches


def add_rows(moved, sums, weights, columns, easts, size_x):
    tiles, depth = easts.shape[0], easts.shape[2]
    reaches = prepare(moved, weights, columns, easts, size_x)

    def block(t, here):
        column = columns[t].reshape(ROW // 16, 16, depth)
        parts = []
        for k in range(STEP):
            mine = jnp.where(easts[t] == here + k, 1.0, 0.0).astype(jnp.bfloat16)
            parts.append((column * mine[None]).reshape(ROW, depth))
        where = pl.ds(pl.multiple_of(here * ROW, ROW), STEP * ROW)
        sums[where, :] += jnp.dot(
            jnp.concatenate(parts, 0), weights[t], preferred_element_type=jnp.float32
        )

    windows = []
    for t in range(tiles):
        share = 9 if t in (0, tiles - 1) else 12
        windows.append(min(size_x, pl.cdiv(size_x * share, 16 * STEP) * STEP))
    narrow = functools.reduce(
        jnp.logical_and, [last - first < width for (first, last), width in zip(reaches, windows)]
    )

    @pl.when(narrow)
    def _():
        for t in range(tiles):
            start = jnp.minimum(reaches[t][0], size_x - windows[t])
            for g in range(windows[t] // STEP):
                block(t, start + g * STEP)

    @pl.when(jnp.logical_not(narrow))
    def _():
        for t in range(tiles):

            def whole_tile(g, carry, t=t):
                block(t, g * STEP)
                return carry

            lax.fori_loop(0, size_x // STEP, whole_tile, 0)


def add_scratch(devices):
    depth = devices * GROUP
    tiles = CAP // GROUP
    return [
        pltpu.VMEM((tiles, depth, 2 * ROW), jnp.bfloat16),
        pltpu.VMEM((tiles, ROW, depth), jnp.bfloat16),
        pltpu.VMEM((tiles, 16, depth), jnp.int32),
    ]


def relax(fields, sums, out, channels, size_x, i):
    block = slice(i * ROW, (i + 1) * ROW)
    total = (sums[block, :ROW] + sums[block, ROW:]).T
    share = 1.0 / (1.0 + total[TALLY : TALLY + 1])
    where = pl.ds(i, channels, stride=size_x)
    out[where, :] = (fields[where, :] + total[:channels]) * share


def nest_step(state, metric, buoyancy, levels, size_x):
    shape = (size_x, ROW)
    row = lax.broadcasted_iota(jnp.int32, shape, 0)
    lane = lax.broadcasted_iota(jnp.int32, shape, 1)
    scaled = COURANT * metric[...]

    def at(field, k):
        start = (field * levels + k) * size_x
        return slice(start, start + size_x)

    w_below = jnp.zeros(shape, jnp.float32)
    p = state[at(4, 0), :]
    for k in range(levels):
        n = COURANT * buoyancy[k]
        p_above = state[at(4, k + 1), :] if k + 1 < levels else jnp.zeros(shape, jnp.float32)
        p_east = jnp.where(row == size_x - 1, 0.0, pltpu.roll(p, size_x - 1, 0))
        p_north = jnp.where(lane == ROW - 1, 0.0, pltpu.roll(p, ROW - 1, 1))
        u = state[at(0, k), :] - COURANT * (p_east - p)
        v = state[at(1, k), :] - COURANT * (p_north - p)
        edge = -COURANT * p
        u_west = jnp.where(row == 0, edge, pltpu.roll(u, 1, 0))
        v_south = jnp.where(lane == 0, edge, pltpu.roll(v, 1, 1))
        theta = state[at(3, k), :]
        w = state[at(2, k), :] - COURANT * (p_above - p) + n * theta
        state[at(0, k), :] = u
        state[at(1, k), :] = v
        state[at(2, k), :] = w
        state[at(3, k), :] = theta - n * w
        state[at(4, k), :] = p - scaled * ((u - u_west) + (v - v_south) + (w - w_below))
        w_below = w
        p = p_above


def fetch(pairs, sems):
    copies = [pltpu.make_async_copy(a, b, sems.at[i]) for i, (a, b) in enumerate(pairs)]
    for copy in copies:
        copy.start()
    return copies


def split(source, target, parts):
    count = source.shape[0] // parts
    blocks = [pl.ds(part * count, count) for part in range(parts)]
    return [(source.at[block], target.at[block]) for block in blocks]


def strip_kernel(
    parent, dest, picks, spots, spot_rows, packed,
    tile, dest_v, picks_s, spots_s, spots_v, rows, staged, slots_v, slots, sems, slot_sems, out_sems,
    *, size_x, cells
):
    channels = parent.shape[0] // size_x
    copies = fetch(
        [(dest, dest_v), (spot_rows, spots_v), (picks, picks_s), (spots, spots_s)], sems
    )
    arrivals = fetch(split(parent, tile, out_sems.shape[0]), out_sems)
    clear_rows(staged)
    copies[0].wait()
    copies[1].wait()
    slots_v[...] = slot_rows(dest_v[...], spots_v[...], cells)
    moves = fetch(
        [(slots_v.at[a], slots.at[pl.ds(a * ROW, ROW)]) for a in range(slots_v.shape[0])], slot_sems
    )
    for copy in arrivals:
        copy.wait()
    to_rows(tile, rows, channels, size_x)
    for copy in copies[2:] + moves:
        copy.wait()
    for copy in pack_rows(rows, picks_s, spots_s, slots, staged, packed, out_sems):
        copy.wait()


def nest_kernel(
    moved, nest, metric, buoyancy, picks, spots, slots, out, packed,
    came, tile, metric_v, buoyancy_s, picks_s, spots_s, slots_s, state, sums, rows, staged,
    weights, columns, easts, sems, out_sems,
    *, size_x
):
    channels = nest.shape[0] // size_x
    arrivals = fetch(split(moved, came, out_sems.shape[0]), out_sems)
    copies = fetch(
        [(nest, tile), (metric, metric_v), (buoyancy, buoyancy_s)]
        + [(picks, picks_s), (spots, spots_s), (slots, slots_s)],
        sems,
    )
    sums[...] = jnp.zeros(sums.shape, jnp.float32)
    clear_rows(staged)
    for copy in arrivals:
        copy.wait()
    add_rows(came, sums, weights, columns, easts, size_x)
    for copy in copies:
        copy.wait()
    for i in range(size_x):
        relax(tile, sums, state, channels, size_x, i)

    def step(_, carry):
        nest_step(state, metric_v, buoyancy_s, channels // 5, size_x)
        return carry

    lax.fori_loop(0, NSN, step, 0)
    result = pltpu.make_async_copy(state, out, sems.at[0])
    result.start()
    to_rows(state, rows, channels, size_x)
    for copy in pack_rows(rows, picks_s, spots_s, slots_s, staged, packed, out_sems):
        copy.wait()
    result.wait()


def rim_kernel(odd, head, tail, metric, near, far):
    channels, block = head.shape[:2]
    head, tail = (ref.reshape(channels * block, ROW) for ref in (head, tail))
    size_x = metric.shape[0]

    def cut(first, last):
        for r in range(WIDTH):
            there = pl.ds(r, channels, stride=WIDTH)
            end = block - WIDTH + r
            first[there, :] = head[pl.ds(r, channels, stride=block), :]
            last[there, :] = tail[pl.ds(end, channels, stride=block), :]
            own, end = channels * WIDTH + r, size_x - WIDTH + r
            first[own : own + 1, :] = metric[r : r + 1]
            last[own : own + 1, :] = metric[end : end + 1]

    @pl.when(odd[0] == 1)
    def _():
        cut(near, far)

    @pl.when(odd[0] == 0)
    def _():
        cut(far, near)


def rim_rows(odd, near, far, c):
    rim = slice(c * WIDTH, (c + 1) * WIDTH)
    ours, theirs = near[rim, :], far[rim, :]
    even = odd[0] == 0
    return jnp.concatenate([jnp.where(even, ours, theirs), jnp.where(even, theirs, ours)], 0)


def strip_rim_kernel(odd, parent, metric, near, far, dest, spots, first, last, slots):
    size_x = metric.shape[0]
    channels = parent.shape[0] // size_x
    slots[...] = slot_rows(dest[...], spots[...], size_x * ROW)

    def rows(c):
        own = parent[c * size_x : (c + 1) * size_x, :] if c < channels else metric[...]
        return jnp.concatenate([own, rim_rows(odd, near, far, c)], 0)

    gather_lanes(rows, channels + 1, size_x + 2 * WIDTH, first, last)


def gather_lanes(rows, count, height, first, last):
    per = ROW // WIDTH
    lane = lax.broadcasted_iota(jnp.int32, (height, ROW), 1) // WIDTH
    for q in range(pl.cdiv(count, per)):
        ahead = jnp.zeros((height, ROW), jnp.float32)
        behind = ahead
        for m in range(min(per, count - q * per)):
            own = rows(q * per + m)
            ahead = jnp.where(lane == m, pltpu.roll(own, m * WIDTH, 1), ahead)
            behind = jnp.where(lane == m, pltpu.roll(own, (m + 1) * WIDTH % ROW, 1), behind)
        where = slice(q * height, (q + 1) * height)
        first[where, :] = ahead
        last[where, :] = behind


def parent_kernel(
    odd, edge, buoyancy, parent, metric, near, far, after_y, before_y, out, state, scaled
):
    size_x = metric.shape[0]
    channels = parent.shape[0] // size_x
    levels = channels // 5
    tall = size_x + 2 * WIDTH
    per = ROW // WIDTH
    shape = (tall, 2 * ROW)
    group = lax.broadcasted_iota(jnp.int32, (tall, ROW), 1) // WIDTH

    def extended(c, own):
        m = c % per
        rows = slice(c // per * tall, (c // per + 1) * tall)
        ahead = pltpu.roll(after_y[rows, :], -m * WIDTH % ROW, 1)
        behind = pltpu.roll(before_y[rows, :], (per - 1 - m) * WIDTH, 1)
        side = jnp.where(group == 0, ahead, jnp.where(group == per - 1, behind, 0.0))
        middle = jnp.concatenate([own, rim_rows(odd, near, far, c)], 0)
        return jnp.concatenate([middle, side], 1)

    for c in range(channels):
        state[c] = extended(c, parent[c * size_x : (c + 1) * size_x, :])
    scaled[...] = COURANT * extended(channels, metric[...])
    row = lax.broadcasted_iota(jnp.int32, shape, 0)
    lane = lax.broadcasted_iota(jnp.int32, shape, 1)
    u_keep = jnp.where((row >= tall - WIDTH) & (edge[0] == 1), 0.0, 1.0)
    v_keep = jnp.where((lane >= 2 * ROW - WIDTH) & (edge[1] == 1), 0.0, 1.0)

    def step(_, carry):
        w_below = jnp.zeros(shape, jnp.float32)
        p = state[4 * levels]
        for k in range(levels):
            n = COURANT * buoyancy[k]
            p_above = state[4 * levels + k + 1] if k + 1 < levels else jnp.zeros(shape, jnp.float32)
            u = state[k] - COURANT * (pltpu.roll(p, tall - 1, 0) - p)
            v = state[levels + k] - COURANT * (pltpu.roll(p, 2 * ROW - 1, 1) - p)
            theta = state[3 * levels + k]
            w = state[2 * levels + k] - COURANT * (p_above - p) + n * theta
            spread = (u - pltpu.roll(u, 1, 0)) + (v - pltpu.roll(v, 1, 1)) + (w - w_below)
            state[k] = u * u_keep
            state[levels + k] = v * v_keep
            state[2 * levels + k] = w
            state[3 * levels + k] = theta - n * w
            state[4 * levels + k] = p - scaled[...] * spread
            w_below = w
            p = p_above
        return carry

    lax.fori_loop(0, NSP, step, 0)
    for c in range(channels):
        out[c * size_x : (c + 1) * size_x, :] = state[c, :size_x, :ROW]


def final_kernel(
    moved, parent, out, came, tile, result, sums, weights, columns, easts, sems, out_sems, *, size_x
):
    channels = parent.shape[0] // size_x
    arrivals = fetch(split(moved, came, out_sems.shape[0]), out_sems)
    copies = fetch([(parent, tile)], sems)
    sums[...] = jnp.zeros(sums.shape, jnp.float32)
    for copy in arrivals:
        copy.wait()
    add_rows(came, sums, weights, columns, easts, size_x)
    copies[0].wait()
    flat = result.reshape(channels * size_x, ROW)
    parts = out_sems.shape[0]
    count = size_x // parts
    copies = []
    for part in range(parts):
        for i in range(part * count, (part + 1) * count):
            relax(tile, sums, flat, channels, size_x, i)
        block = (slice(None), pl.ds(part * count, count))
        copies.append(pltpu.make_async_copy(result.at[block], out.at[block], out_sems.at[part]))
        copies[-1].start()
    for copy in copies:
        copy.wait()


def vmem():
    return pl.BlockSpec(memory_space=pltpu.VMEM)


def smem():
    return pl.BlockSpec(memory_space=pltpu.SMEM)


def anywhere():
    return pl.BlockSpec(memory_space=pltpu.HBM)


def params():
    return pltpu.CompilerParams(vmem_limit_bytes=VMEM_BYTES)


def exchange(packed, devices):
    moved = lax.all_to_all(
        packed.reshape(devices, KEEP * ROW), ("gx", "gy"), split_axis=0, concat_axis=0, tiled=True
    )
    return moved.reshape(devices * KEEP, ROW)


def swapped(near, far, axis):
    size = lax.axis_size(axis)
    pairs = [[(i, i + 1) for i in range(start, size - 1, 2)] for start in (0, 1)]
    pairs = [some + [(j, i) for i, j in some] for some in pairs]
    return lax.ppermute(near, axis, pairs[0]), lax.ppermute(far, axis, pairs[1])


def shifted(first, last, axis):
    size = lax.axis_size(axis)
    up = [(i, i + 1) for i in range(size - 1)]
    down = [(j, i) for i, j in up]
    return lax.ppermute(first, axis, down), lax.ppermute(last, axis, up)


def on_device(
    parent,
    metric,
    buoyancy,
    nest,
    nest_metric,
    strip_col,
    strip_dest,
    strip_pos,
    panel_src,
    panel_dest,
    panel_col,
):
    devices = lax.axis_size("gx") * lax.axis_size("gy")
    channels = parent.shape[0] * parent.shape[1]
    tile_x, tile_y = parent.shape[2:]
    block_x, block_y = nest.shape[2:]
    slots = strip_col.shape[0]
    groups = slots // ROW
    tile_shape = (channels * tile_x, tile_y)
    block_shape = (channels * block_x, block_y)
    packed_shape = (devices * KEEP, ROW)
    parts = 4

    def shape(*dims, dtype=jnp.float32):
        return jax.ShapeDtypeStruct(dims, dtype)

    def index(memory):
        return memory((slots,), jnp.int32)

    listed = pltpu.VMEM((groups, ROW), jnp.int32)
    rim_x = shape((channels + 1) * WIDTH, ROW)
    tile = parent.reshape(channels, tile_x, tile_y)
    ends = [
        pl.BlockSpec((channels, GROUP, ROW), lambda i, place=place: (0, place, 0))
        for place in (0, tile_x // GROUP - 1)
    ]
    whole_rim = pl.BlockSpec(rim_x.shape, lambda i: (0, 0))
    odd = (lax.axis_index("gx") % 2).astype(jnp.int32).reshape(1)
    near, far = pl.pallas_call(
        rim_kernel,
        grid=(1,),
        out_shape=(rim_x, rim_x),
        in_specs=[smem()] + ends + [pl.BlockSpec(metric.shape, lambda i: (0, 0))],
        out_specs=(whole_rim, whole_rim),
        compiler_params=params(),
        name="cut_rims",
    )(odd, tile, tile, metric)
    near, far = swapped(near, far, "gx")
    packed = pl.pallas_call(
        functools.partial(strip_kernel, size_x=tile_x, cells=block_x * block_y),
        out_shape=shape(*packed_shape),
        in_specs=[anywhere()] * 5,
        out_specs=anywhere(),
        scratch_shapes=[
            pltpu.VMEM(tile_shape, jnp.float32),
            listed,
            index(pltpu.SMEM),
            index(pltpu.SMEM),
            listed,
            pltpu.VMEM((tile_x * tile_y, ROW), jnp.float32),
            pltpu.VMEM((devices * CAP, ROW), jnp.float32),
            listed,
            index(pltpu.SMEM),
            pltpu.SemaphoreType.DMA((4,)),
            pltpu.SemaphoreType.DMA((groups,)),
            pltpu.SemaphoreType.DMA((parts,)),
        ],
        compiler_params=params(),
        name="pack_strips",
    )(
        parent.reshape(tile_shape),
        strip_dest.reshape(groups, ROW),
        strip_col,
        strip_pos,
        strip_pos.reshape(groups, ROW),
    )

    packed, near, far, late_parent, late_metric, late_dest, late_col = (
        lax.optimization_barrier(
            (packed, near, far, parent.reshape(tile_shape), metric, panel_dest, panel_col)
        )
    )
    moved = exchange(packed, devices)
    tall = tile_x + 2 * WIDTH
    rim_y = shape(pl.cdiv(channels + 1, ROW // WIDTH) * tall, ROW)
    first_y, last_y, panel_slots = pl.pallas_call(
        strip_rim_kernel,
        out_shape=(rim_y, rim_y, shape(groups, ROW, dtype=jnp.int32)),
        in_specs=[smem()] + [vmem()] * 6,
        out_specs=(vmem(),) * 3,
        compiler_params=params(),
        cost_estimate=pl.CostEstimate(flops=3_000_000, bytes_accessed=2_000_000, transcendentals=0),
        name="pack_rims",
    )(
        odd,
        late_parent,
        late_metric,
        near,
        far,
        late_dest.reshape(groups, ROW),
        late_col.reshape(groups, ROW),
    )
    after_y, before_y = shifted(first_y, last_y, "gy")
    moved, after_y, before_y, panel_slots = lax.optimization_barrier(
        (moved, after_y, before_y, panel_slots)
    )
    nest_out, packed = pl.pallas_call(
        functools.partial(nest_kernel, size_x=block_x),
        out_shape=(shape(*block_shape), shape(*packed_shape)),
        in_specs=[anywhere()] * 7,
        out_specs=(anywhere(), anywhere()),
        scratch_shapes=[
            pltpu.VMEM(packed_shape, jnp.float32),
            pltpu.VMEM(block_shape, jnp.float32),
            pltpu.VMEM((block_x, block_y), jnp.float32),
            pltpu.SMEM(buoyancy.shape, jnp.float32),
            index(pltpu.SMEM),
            index(pltpu.SMEM),
            index(pltpu.SMEM),
            pltpu.VMEM(block_shape, jnp.float32),
            pltpu.VMEM((block_x * block_y, 2 * ROW), jnp.float32),
            pltpu.VMEM((block_x * block_y, ROW), jnp.float32),
            pltpu.VMEM((devices * CAP, ROW), jnp.float32),
        ]
        + add_scratch(devices)
        + [pltpu.SemaphoreType.DMA((6,)), pltpu.SemaphoreType.DMA((parts,))],
        compiler_params=params(),
        name="step_nest",
    )(
        moved,
        nest.reshape(block_shape),
        nest_metric,
        buoyancy,
        panel_src,
        panel_col,
        panel_slots.reshape(slots),
    )
    moved = exchange(packed, devices)
    edge = jnp.stack([lax.axis_index("gx") == 0, lax.axis_index("gy") == 0]).astype(jnp.int32)
    parent_state = pl.pallas_call(
        parent_kernel,
        out_shape=shape(*tile_shape),
        in_specs=[smem()] * 3 + [vmem()] * 6,
        out_specs=vmem(),
        scratch_shapes=[
            pltpu.VMEM((channels, tall, 2 * ROW), jnp.float32),
            pltpu.VMEM((tall, 2 * ROW), jnp.float32),
        ],
        compiler_params=params(),
        cost_estimate=pl.CostEstimate(flops=20_000_000, bytes_accessed=8_000_000, transcendentals=0),
        name="step_parent",
    )(odd, edge, buoyancy, late_parent, late_metric, near, far, after_y, before_y)

    parent_out = pl.pallas_call(
        functools.partial(final_kernel, size_x=tile_x),
        out_shape=shape(channels, tile_x, tile_y),
        in_specs=[anywhere(), anywhere()],
        out_specs=anywhere(),
        scratch_shapes=[
            pltpu.VMEM(packed_shape, jnp.float32),
            pltpu.VMEM(tile_shape, jnp.float32),
            pltpu.VMEM((channels, tile_x, tile_y), jnp.float32),
            pltpu.VMEM((tile_x * tile_y, 2 * ROW), jnp.float32),
        ]
        + add_scratch(devices)
        + [pltpu.SemaphoreType.DMA((1,)), pltpu.SemaphoreType.DMA((parts,))],
        compiler_params=params(),
        name="add_panels",
    )(moved, parent_state)
    return (parent_out.reshape(parent.shape), nest_out.reshape(nest.shape))


def solution(mesh):
    placed = (
        P(None, None, "gx", "gy"),
        P("gx", "gy"),
        P(),
        P(None, None, "gx", "gy"),
        P("gx", "gy"),
        P(("gx", "gy")),
        P(("gx", "gy"), None),
        P(("gx", "gy")),
        P(("gx", "gy")),
        P(("gx", "gy"), None),
        P(("gx", "gy")),
    )
    return jax.shard_map(
        on_device,
        mesh=mesh,
        in_specs=placed,
        out_specs=(P(None, None, "gx", "gy"), P(None, None, "gx", "gy")),
        check_vma=False,
    )
```

```python
import functools

import jax
import jax.numpy as jnp
from jax import lax
from jax.experimental import pallas as pl
from jax.experimental.pallas import tpu as pltpu
from jax.sharding import PartitionSpec as P

CAP = 32
NSP = 4
NSN = 6
COURANT = 0.35
WIDTH = NSP

ROW = 128
SPOT = 100
TALLY = 101
FREE = SPOT + 1
PIECE = ROW - FREE
PIECES = 4
KEEP = 26
REST = CAP - KEEP
GROUP = 8
STEP = 2
MARGINS = (4, 8)
VMEM_BYTES = 65500 * 1024


def slot_rows(dest, spot, cells):
    groups = dest.shape[0]
    shape = (ROW, ROW)
    row = lax.broadcasted_iota(jnp.int32, dest.shape, 0)
    lane = lax.broadcasted_iota(jnp.int32, dest.shape, 1)
    high = spot >= cells // 2
    side = jnp.where(high, 1, 0)
    inward = jnp.where(high, cells - 1 - spot, spot)
    least = (dest * 2 + side) << 21
    key = least + (inward << 10) + (row * ROW + lane)
    counts = [jnp.zeros((8, ROW), jnp.float32) for _ in range(groups)]
    for a in range(groups):
        column = jnp.broadcast_to(key[a : a + 1], shape).T
        for b in range(groups):
            before = (column >= least[b : b + 1]) & (column < key[b : b + 1])
            ones = jnp.where(before, 1.0, 0.0)
            counts[b] = counts[b] + jnp.sum(ones.reshape(ROW // 8, 8, ROW), axis=0)
    rank = jnp.concatenate([jnp.sum(c, axis=0, keepdims=True) for c in counts], 0)
    rank = rank.astype(jnp.int32)
    slot = jnp.where(high, CAP - 1 - rank, rank)
    devices = ROW
    spill = devices * KEEP + (slot - KEEP) * devices + dest
    return jnp.where(slot < KEEP, dest * KEEP + slot, spill)


def padded(channels):
    return pl.cdiv(channels, 8) * 8


def to_rows(fields, rows, channels, size_x):
    height = padded(channels)
    real = lax.broadcasted_iota(jnp.int32, (8, ROW), 0) < channels - (height - 8)
    tail = jnp.zeros((ROW - height, ROW), jnp.float32)
    for i in range(size_x):
        block = fields[pl.ds(i, height, stride=size_x), :]
        final = jnp.where(real, block[height - 8 :], 0.0)
        block = jnp.concatenate([block[: height - 8], final, tail], 0)
        rows[i * ROW : (i + 1) * ROW, :] = block.T


def clear_rows(staged):
    lane = lax.broadcasted_iota(jnp.int32, (1, ROW), 1)
    staged[...] = jnp.broadcast_to(jnp.where(lane == SPOT, -1.0, 0.0), staged.shape)


def pack_rows(rows, picks, spots, slots, staged, packed, sems):
    lane = lax.broadcasted_iota(jnp.int32, (1, ROW), 1)
    devices = packed.shape[0] // KEEP

    def move(r, carry):
        spot = jnp.full((1, ROW), spots[r], jnp.int32).astype(jnp.float32)
        row = rows[pl.ds(picks[r], 1), :]
        staged[pl.ds(slots[r], 1), :] = jnp.where(lane == SPOT, spot, row)
        return carry

    lax.fori_loop(0, slots.shape[0], move, 0, unroll=32)
    parts = sems.shape[0]
    count = devices // parts
    free = lax.broadcasted_iota(jnp.int32, (count, ROW), 1) >= FREE
    copies = []
    for part in range(parts):
        base = part * count
        for a in range(REST):
            start = devices * (KEEP + a) + base
            values = staged[start : start + count, :]
            for b in range(PIECES):
                where = pl.ds(base * KEEP + b * REST + a, count, stride=KEEP)
                piece = pltpu.roll(values, (FREE - b * PIECE) % ROW, 1)
                staged[where, :] = jnp.where(free, piece, staged[where, :])
        block = pl.ds(base * KEEP, count * KEEP)
        copies.append(pltpu.make_async_copy(staged.at[block], packed.at[block], sems.at[part]))
        copies[-1].start()
    return copies


def slot_values(moved, s, base, count):
    if s < KEEP:
        return moved[pl.ds(base * KEEP + s, count, stride=KEEP), :]
    lane = lax.broadcasted_iota(jnp.int32, (count, ROW), 1)
    values = jnp.zeros((count, ROW), jnp.float32)
    for b in range(PIECES):
        where = pl.ds(base * KEEP + b * REST + s - KEEP, count, stride=KEEP)
        piece = pltpu.roll(moved[where, :], (b * PIECE - FREE) % ROW, 1)
        values = jnp.where((lane >= b * PIECE) & (lane < (b + 1) * PIECE), piece, values)
    return values


def prepare(moved, arrivals, later, weights, columns, easts, size_x):
    lane = lax.broadcasted_iota(jnp.int32, (16, 2 * ROW), 1)
    pick = jnp.where((lane == SPOT) | (lane == SPOT + ROW), 1.0, 0.0).astype(jnp.bfloat16)
    devices = moved.shape[0] // KEEP
    depth = devices * GROUP
    tiles = CAP // GROUP
    count = devices // len(arrivals)
    north = lax.broadcasted_iota(jnp.int32, (ROW, depth), 0)
    tally = lax.broadcasted_iota(jnp.int32, (count, ROW), 1) == TALLY
    for part, arrival in enumerate(arrivals):
        arrival.wait()
        base = part * count
        for s in range(CAP):
            values = jnp.where(tally, 1.0, slot_values(moved, s, base, count))
            high = values.astype(jnp.bfloat16)
            low = (values - high.astype(jnp.float32)).astype(jnp.bfloat16)
            t, k = s // GROUP, s % GROUP
            start = t * depth + k * devices + base
            weights[start : start + count, :ROW] = high
            weights[start : start + count, ROW:] = low
    for copy in later:
        copy.start()
    reaches = []
    for t in range(tiles):
        spot = lax.dot_general(
            pick, weights[t * depth : (t + 1) * depth, :], (((1,), (1,)), ((), ())), preferred_element_type=jnp.float32
        )
        whole = spot.astype(jnp.int32)
        east, within = whole >> 7, whole & (ROW - 1)
        easts[t] = east.astype(jnp.float32).astype(jnp.bfloat16)
        columns[t] = jnp.where(north == within[0:1], 1.0, 0.0).astype(jnp.bfloat16)
        used = spot[0:8] >= 0.0
        reach = east[0:8].astype(jnp.float32)
        first = jnp.min(jnp.where(used, reach, float(size_x)))
        last = jnp.max(jnp.where(used, reach, -1.0))
        reaches.append((first.astype(jnp.int32), last.astype(jnp.int32)))
    return reaches


def add_rows(moved, arrivals, later, sums, weights, columns, easts, size_x):
    tiles, depth = easts.shape[0], easts.shape[2]
    reaches = prepare(moved, arrivals, later, weights, columns, easts, size_x)

    def block(t, here):
        column = columns[t].reshape(ROW // 16, 16, depth)
        parts = []
        for k in range(STEP):
            place = jnp.asarray(here + k, jnp.float32).astype(jnp.bfloat16)
            mine = jnp.where(easts[t] == place, 1.0, 0.0).astype(jnp.bfloat16)
            parts.append((column * mine[None]).reshape(ROW, depth))
        where = pl.ds(pl.multiple_of(here * ROW, ROW), STEP * ROW)
        sums[where, :] += jnp.dot(
            jnp.concatenate(parts, 0),
            weights[t * depth : (t + 1) * depth, :],
            preferred_element_type=jnp.float32,
        )

    low = [min(size_x, size_x // 2 + margin) for margin in MARGINS]
    widths = low + low[::-1]
    fits = [last - first < width for (first, last), width in zip(reaches, widths)]
    narrow = functools.reduce(jnp.logical_and, fits)

    @pl.when(narrow)
    def _():
        for t in range(tiles):
            start = jnp.minimum(reaches[t][0], size_x - widths[t])
            for g in range(widths[t] // STEP):
                block(t, start + g * STEP)

    @pl.when(jnp.logical_not(narrow))
    def _():
        for t in range(tiles):
            first, last = reaches[t]
            blocks = jnp.maximum(last - first + STEP, 0) // STEP
            start = jnp.minimum(first, size_x - blocks * STEP)

            def reached(g, carry, t=t, start=start):
                block(t, start + g * STEP)
                return carry

            lax.fori_loop(0, blocks, reached, 0)


def add_scratch(devices):
    depth = devices * GROUP
    tiles = CAP // GROUP
    return [
        pltpu.VMEM((tiles * depth, 2 * ROW), jnp.bfloat16),
        pltpu.VMEM((tiles, ROW, depth), jnp.bfloat16),
        pltpu.VMEM((tiles, 16, depth), jnp.bfloat16),
    ]


def relax(fields, sums, out, channels, size_x, i):
    block = slice(i * ROW, (i + 1) * ROW)
    total = (sums[block, :ROW] + sums[block, ROW:]).T
    share = 1.0 / (1.0 + total[TALLY : TALLY + 1])
    height = padded(channels)
    where = pl.ds(i, height, stride=size_x)
    out[where, :] = (fields[where, :] + total[:height]) * share


def nest_step(state, metric, buoyancy, levels, size_x):
    shape = (size_x, ROW)
    row = lax.broadcasted_iota(jnp.int32, shape, 0)
    lane = lax.broadcasted_iota(jnp.int32, shape, 1)
    scaled = COURANT * metric[...]

    def at(field, k):
        start = (field * levels + k) * size_x
        return slice(start, start + size_x)

    w_below = jnp.zeros(shape, jnp.float32)
    p = state[at(4, 0), :]
    for k in range(levels):
        n = COURANT * buoyancy[k]
        p_above = state[at(4, k + 1), :] if k + 1 < levels else jnp.zeros(shape, jnp.float32)
        p_east = jnp.where(row == size_x - 1, 0.0, pltpu.roll(p, size_x - 1, 0))
        p_north = jnp.where(lane == ROW - 1, 0.0, pltpu.roll(p, ROW - 1, 1))
        u = state[at(0, k), :] - COURANT * (p_east - p)
        v = state[at(1, k), :] - COURANT * (p_north - p)
        edge = -COURANT * p
        u_west = jnp.where(row == 0, edge, pltpu.roll(u, 1, 0))
        v_south = jnp.where(lane == 0, edge, pltpu.roll(v, 1, 1))
        theta = state[at(3, k), :]
        w = state[at(2, k), :] - COURANT * (p_above - p) + n * theta
        state[at(0, k), :] = u
        state[at(1, k), :] = v
        state[at(2, k), :] = w
        state[at(3, k), :] = theta - n * w
        state[at(4, k), :] = p - scaled * ((u - u_west) + (v - v_south) + (w - w_below))
        w_below = w
        p = p_above


def planned(pairs, sems):
    return [pltpu.make_async_copy(a, b, sems.at[i]) for i, (a, b) in enumerate(pairs)]


def fetch(pairs, sems):
    copies = planned(pairs, sems)
    for copy in copies:
        copy.start()
    return copies


def split(source, target, parts):
    count = source.shape[0] // parts
    blocks = [pl.ds(part * count, count) for part in range(parts)]
    return [(source.at[block], target.at[block]) for block in blocks]


def strip_kernel(
    parent, dest, picks, spots, spot_rows, packed,
    tile, dest_v, picks_s, spots_s, spots_v, rows, staged, slots_v, slots, sems, slot_sems, out_sems,
    *, size_x, cells
):
    channels = parent.shape[0] // size_x
    copies = fetch(
        [(dest, dest_v), (spot_rows, spots_v), (picks, picks_s), (spots, spots_s)], sems
    )
    arrivals = fetch(split(parent, tile, out_sems.shape[0]), out_sems)
    clear_rows(staged)
    copies[0].wait()
    copies[1].wait()
    slots_v[...] = slot_rows(dest_v[...], spots_v[...], cells)
    moves = fetch(
        [(slots_v.at[a], slots.at[pl.ds(a * ROW, ROW)]) for a in range(slots_v.shape[0])], slot_sems
    )
    for copy in arrivals:
        copy.wait()
    to_rows(tile, rows, channels, size_x)
    for copy in copies[2:] + moves:
        copy.wait()
    for copy in pack_rows(rows, picks_s, spots_s, slots, staged, packed, out_sems):
        copy.wait()


def nest_kernel(
    moved, nest, metric, buoyancy, picks, spots, slots, out, packed,
    came, tile, metric_v, buoyancy_s, picks_s, spots_s, slots_s, state, sums, rows, staged,
    weights, columns, easts, sems, out_sems,
    *, size_x
):
    channels = nest.shape[0] // size_x
    arrivals = fetch(split(moved, came, out_sems.shape[0]), out_sems)
    copies = planned(
        [(nest, tile.at[pl.ds(0, nest.shape[0])]), (metric, metric_v), (buoyancy, buoyancy_s)]
        + [(picks, picks_s), (spots, spots_s), (slots, slots_s)],
        sems,
    )
    sums[...] = jnp.zeros(sums.shape, jnp.float32)
    clear_rows(staged)
    add_rows(came, arrivals, copies, sums, weights, columns, easts, size_x)
    for copy in copies:
        copy.wait()
    for i in range(size_x):
        relax(tile, sums, state, channels, size_x, i)

    def step(_, carry):
        nest_step(state, metric_v, buoyancy_s, channels // 5, size_x)
        return carry

    lax.fori_loop(0, NSN, step, 0)
    result = pltpu.make_async_copy(state.at[pl.ds(0, out.shape[0])], out, sems.at[0])
    result.start()
    to_rows(state, rows, channels, size_x)
    for copy in pack_rows(rows, picks_s, spots_s, slots_s, staged, packed, out_sems):
        copy.wait()
    result.wait()


def rim_kernel(odd, head, tail, metric, near, far):
    channels, block = head.shape[:2]
    size_x = metric.shape[0]

    def cut(first, last):
        for c in range(0, channels, 2):
            pair = slice(c * WIDTH, (c + 2) * WIDTH)
            first[pair, :] = jnp.concatenate([head[c, :WIDTH], head[c + 1, :WIDTH]], 0)
            last[pair, :] = jnp.concatenate(
                [tail[c, block - WIDTH :], tail[c + 1, block - WIDTH :]], 0
            )
        own = slice(channels * WIDTH, (channels + 1) * WIDTH)
        first[own, :] = metric[:WIDTH]
        last[own, :] = metric[size_x - WIDTH :]

    @pl.when(odd[0] == 1)
    def _():
        cut(near, far)

    @pl.when(odd[0] == 0)
    def _():
        cut(far, near)


def rim_rows(odd, near, far, c):
    rim = slice(c * WIDTH, (c + 1) * WIDTH)
    ours, theirs = near[rim, :], far[rim, :]
    even = odd[0] == 0
    return jnp.concatenate([jnp.where(even, ours, theirs), jnp.where(even, theirs, ours)], 0)


def strip_rim_kernel(odd, parent, metric, near, far, dest, spots, first, last, slots):
    size_x = metric.shape[0]
    channels = parent.shape[0] // size_x
    slots[...] = slot_rows(dest[...], spots[...], size_x * ROW)

    def rows(c):
        own = parent[c * size_x : (c + 1) * size_x, :] if c < channels else metric[...]
        return jnp.concatenate([own, rim_rows(odd, near, far, c)], 0)

    gather_lanes(rows, channels + 1, size_x + 2 * WIDTH, first, last)


def gather_lanes(rows, count, height, first, last):
    per = ROW // WIDTH
    lane = lax.broadcasted_iota(jnp.int32, (height, ROW), 1) // WIDTH
    for q in range(pl.cdiv(count, per)):
        ahead = jnp.zeros((height, ROW), jnp.float32)
        behind = ahead
        for m in range(min(per, count - q * per)):
            own = rows(q * per + m)
            ahead = jnp.where(lane == m, pltpu.roll(own, m * WIDTH, 1), ahead)
            behind = jnp.where(lane == m, pltpu.roll(own, (m + 1) * WIDTH % ROW, 1), behind)
        where = slice(q * height, (q + 1) * height)
        first[where, :] = ahead
        last[where, :] = behind


def parent_kernel(
    odd, edge, buoyancy, parent, metric, near, far, after_y, before_y, out, state, scaled
):
    size_x = metric.shape[0]
    channels = parent.shape[0] // size_x
    levels = channels // 5
    tall = size_x + 2 * WIDTH
    per = ROW // WIDTH
    shape = (tall, 2 * ROW)
    group = lax.broadcasted_iota(jnp.int32, (tall, ROW), 1) // WIDTH

    def extended(c, own):
        m = c % per
        rows = slice(c // per * tall, (c // per + 1) * tall)
        ahead = pltpu.roll(after_y[rows, :], -m * WIDTH % ROW, 1)
        behind = pltpu.roll(before_y[rows, :], (per - 1 - m) * WIDTH, 1)
        side = jnp.where(group == 0, ahead, jnp.where(group == per - 1, behind, 0.0))
        middle = jnp.concatenate([own, rim_rows(odd, near, far, c)], 0)
        return jnp.concatenate([middle, side], 1)

    for c in range(channels):
        state[c] = extended(c, parent[c * size_x : (c + 1) * size_x, :])
    scaled[...] = COURANT * extended(channels, metric[...])
    row = lax.broadcasted_iota(jnp.int32, shape, 0)
    lane = lax.broadcasted_iota(jnp.int32, shape, 1)
    u_keep = jnp.where((row >= tall - WIDTH) & (edge[0] == 1), 0.0, 1.0)
    v_keep = jnp.where((lane >= 2 * ROW - WIDTH) & (edge[1] == 1), 0.0, 1.0)

    def step(_, carry):
        w_below = jnp.zeros(shape, jnp.float32)
        p = state[4 * levels]
        for k in range(levels):
            n = COURANT * buoyancy[k]
            p_above = state[4 * levels + k + 1] if k + 1 < levels else jnp.zeros(shape, jnp.float32)
            u = state[k] - COURANT * (pltpu.roll(p, tall - 1, 0) - p)
            v = state[levels + k] - COURANT * (pltpu.roll(p, 2 * ROW - 1, 1) - p)
            theta = state[3 * levels + k]
            w = state[2 * levels + k] - COURANT * (p_above - p) + n * theta
            spread = (u - pltpu.roll(u, 1, 0)) + (v - pltpu.roll(v, 1, 1)) + (w - w_below)
            state[k] = u * u_keep
            state[levels + k] = v * v_keep
            state[2 * levels + k] = w
            state[3 * levels + k] = theta - n * w
            state[4 * levels + k] = p - scaled[...] * spread
            w_below = w
            p = p_above
        return carry

    lax.fori_loop(0, NSP, step, 0)
    for c in range(channels):
        out[c * size_x : (c + 1) * size_x, :] = state[c, :size_x, :ROW]


def final_kernel(
    moved, parent, out, came, tile, result, sums, weights, columns, easts, sems, out_sems, *, size_x
):
    channels = parent.shape[0] // size_x
    arrivals = fetch(split(moved, came, out_sems.shape[0]), out_sems)
    copies = planned([(parent, tile.at[pl.ds(0, parent.shape[0])])], sems)
    flat = result.reshape(padded(channels) * size_x, ROW)
    count = size_x // out_sems.shape[0]
    blocks = [(pl.ds(0, channels), pl.ds(start, count)) for start in range(0, size_x, count)]
    leaving = planned([(result.at[block], out.at[block]) for block in blocks], out_sems)

    sums[...] = jnp.zeros(sums.shape, jnp.float32)
    add_rows(came, arrivals, copies, sums, weights, columns, easts, size_x)
    copies[0].wait()
    for i in range(size_x):
        relax(tile, sums, flat, channels, size_x, i)
        if i % count == count - 1:
            leaving[i // count].start()
    for copy in leaving:
        copy.wait()


def vmem():
    return pl.BlockSpec(memory_space=pltpu.VMEM)


def smem():
    return pl.BlockSpec(memory_space=pltpu.SMEM)


def anywhere():
    return pl.BlockSpec(memory_space=pltpu.HBM)


def params():
    return pltpu.CompilerParams(vmem_limit_bytes=VMEM_BYTES)


def exchange(packed, devices):
    moved = lax.all_to_all(
        packed.reshape(devices, KEEP * ROW), ("gx", "gy"), split_axis=0, concat_axis=0, tiled=True
    )
    return moved.reshape(devices * KEEP, ROW)


def swapped(near, far, axis):
    size = lax.axis_size(axis)
    pairs = [[(i, i + 1) for i in range(start, size - 1, 2)] for start in (0, 1)]
    pairs = [some + [(j, i) for i, j in some] for some in pairs]
    return lax.ppermute(near, axis, pairs[0]), lax.ppermute(far, axis, pairs[1])


def shifted(first, last, axis):
    size = lax.axis_size(axis)
    up = [(i, i + 1) for i in range(size - 1)]
    down = [(j, i) for i, j in up]
    return lax.ppermute(first, axis, down), lax.ppermute(last, axis, up)


def on_device(
    parent,
    metric,
    buoyancy,
    nest,
    nest_metric,
    strip_col,
    strip_dest,
    strip_pos,
    panel_src,
    panel_dest,
    panel_col,
):
    devices = lax.axis_size("gx") * lax.axis_size("gy")
    channels = parent.shape[0] * parent.shape[1]
    tile_x, tile_y = parent.shape[2:]
    block_x, block_y = nest.shape[2:]
    slots = strip_col.shape[0]
    groups = slots // ROW
    tile_shape = (channels * tile_x, tile_y)
    block_shape = (channels * block_x, block_y)
    packed_shape = (devices * KEEP, ROW)
    parts = 4

    def shape(*dims, dtype=jnp.float32):
        return jax.ShapeDtypeStruct(dims, dtype)

    def index(memory):
        return memory((slots,), jnp.int32)

    listed = pltpu.VMEM((groups, ROW), jnp.int32)
    rim_x = shape((channels + 1) * WIDTH, ROW)
    tile = parent.reshape(channels, tile_x, tile_y)
    ends = [
        pl.BlockSpec((channels, GROUP, ROW), lambda i, place=place: (0, place, 0))
        for place in (0, tile_x // GROUP - 1)
    ]
    whole_rim = pl.BlockSpec(rim_x.shape, lambda i: (0, 0))
    odd = (lax.axis_index("gx") % 2).astype(jnp.int32).reshape(1)
    near, far = pl.pallas_call(
        rim_kernel,
        grid=(1,),
        out_shape=(rim_x, rim_x),
        in_specs=[smem()] + ends + [pl.BlockSpec(metric.shape, lambda i: (0, 0))],
        out_specs=(whole_rim, whole_rim),
        compiler_params=params(),
        name="cut_rims",
    )(odd, tile, tile, metric)
    near, far = swapped(near, far, "gx")
    packed = pl.pallas_call(
        functools.partial(strip_kernel, size_x=tile_x, cells=block_x * block_y),
        out_shape=shape(*packed_shape),
        in_specs=[anywhere()] * 5,
        out_specs=anywhere(),
        scratch_shapes=[
            pltpu.VMEM((padded(channels) * tile_x, tile_y), jnp.float32),
            listed,
            index(pltpu.SMEM),
            index(pltpu.SMEM),
            listed,
            pltpu.VMEM((tile_x * tile_y, ROW), jnp.float32),
            pltpu.VMEM((devices * CAP, ROW), jnp.float32),
            listed,
            index(pltpu.SMEM),
            pltpu.SemaphoreType.DMA((4,)),
            pltpu.SemaphoreType.DMA((groups,)),
            pltpu.SemaphoreType.DMA((parts,)),
        ],
        compiler_params=params(),
        name="pack_strips",
    )(
        parent.reshape(tile_shape),
        strip_dest.reshape(groups, ROW),
        strip_col,
        strip_pos,
        strip_pos.reshape(groups, ROW),
    )

    packed, near, far, late_parent, late_metric, late_dest, late_col = (
        lax.optimization_barrier(
            (packed, near, far, parent.reshape(tile_shape), metric, panel_dest, panel_col)
        )
    )
    moved = exchange(packed, devices)
    tall = tile_x + 2 * WIDTH
    rim_y = shape(pl.cdiv(channels + 1, ROW // WIDTH) * tall, ROW)
    first_y, last_y, panel_slots = pl.pallas_call(
        strip_rim_kernel,
        out_shape=(rim_y, rim_y, shape(groups, ROW, dtype=jnp.int32)),
        in_specs=[smem()] + [vmem()] * 6,
        out_specs=(vmem(),) * 3,
        compiler_params=params(),
        cost_estimate=pl.CostEstimate(flops=3_000_000, bytes_accessed=2_000_000, transcendentals=0),
        name="pack_rims",
    )(
        odd,
        late_parent,
        late_metric,
        near,
        far,
        late_dest.reshape(groups, ROW),
        late_col.reshape(groups, ROW),
    )
    after_y, before_y = shifted(first_y, last_y, "gy")
    moved, after_y, before_y, panel_slots = lax.optimization_barrier(
        (moved, after_y, before_y, panel_slots)
    )
    nest_out, packed = pl.pallas_call(
        functools.partial(nest_kernel, size_x=block_x),
        out_shape=(shape(*block_shape), shape(*packed_shape)),
        in_specs=[anywhere()] * 7,
        out_specs=(anywhere(), anywhere()),
        scratch_shapes=[
            pltpu.VMEM(packed_shape, jnp.float32),
            pltpu.VMEM((padded(channels) * block_x, block_y), jnp.float32),
            pltpu.VMEM((block_x, block_y), jnp.float32),
            pltpu.SMEM(buoyancy.shape, jnp.float32),
            index(pltpu.SMEM),
            index(pltpu.SMEM),
            index(pltpu.SMEM),
            pltpu.VMEM((padded(channels) * block_x, block_y), jnp.float32),
            pltpu.VMEM((block_x * block_y, 2 * ROW), jnp.float32),
            pltpu.VMEM((block_x * block_y, ROW), jnp.float32),
            pltpu.VMEM((devices * CAP, ROW), jnp.float32),
        ]
        + add_scratch(devices)
        + [pltpu.SemaphoreType.DMA((6,)), pltpu.SemaphoreType.DMA((parts,))],
        compiler_params=params(),
        name="step_nest",
    )(
        moved,
        nest.reshape(block_shape),
        nest_metric,
        buoyancy,
        panel_src,
        panel_col,
        panel_slots.reshape(slots),
    )
    moved = exchange(packed, devices)
    edge = jnp.stack([lax.axis_index("gx") == 0, lax.axis_index("gy") == 0]).astype(jnp.int32)
    parent_state = pl.pallas_call(
        parent_kernel,
        out_shape=shape(*tile_shape),
        in_specs=[smem()] * 3 + [vmem()] * 6,
        out_specs=vmem(),
        scratch_shapes=[
            pltpu.VMEM((channels, tall, 2 * ROW), jnp.float32),
            pltpu.VMEM((tall, 2 * ROW), jnp.float32),
        ],
        compiler_params=params(),
        cost_estimate=pl.CostEstimate(flops=20_000_000, bytes_accessed=8_000_000, transcendentals=0),
        name="step_parent",
    )(odd, edge, buoyancy, late_parent, late_metric, near, far, after_y, before_y)

    parent_out = pl.pallas_call(
        functools.partial(final_kernel, size_x=tile_x),
        out_shape=shape(channels, tile_x, tile_y),
        in_specs=[anywhere(), anywhere()],
        out_specs=anywhere(),
        scratch_shapes=[
            pltpu.VMEM(packed_shape, jnp.float32),
            pltpu.VMEM((padded(channels) * tile_x, tile_y), jnp.float32),
            pltpu.VMEM((padded(channels), tile_x, tile_y), jnp.float32),
            pltpu.VMEM((tile_x * tile_y, 2 * ROW), jnp.float32),
        ]
        + add_scratch(devices)
        + [pltpu.SemaphoreType.DMA((1,)), pltpu.SemaphoreType.DMA((parts,))],
        compiler_params=params(),
        name="add_panels",
    )(moved, parent_state)
    return (parent_out.reshape(parent.shape), nest_out.reshape(nest.shape))


def solution(mesh):
    placed = (
        P(None, None, "gx", "gy"),
        P("gx", "gy"),
        P(),
        P(None, None, "gx", "gy"),
        P("gx", "gy"),
        P(("gx", "gy")),
        P(("gx", "gy"), None),
        P(("gx", "gy")),
        P(("gx", "gy")),
        P(("gx", "gy"), None),
        P(("gx", "gy")),
    )
    return jax.shard_map(
        on_device,
        mesh=mesh,
        in_specs=placed,
        out_specs=(P(None, None, "gx", "gy"), P(None, None, "gx", "gy")),
        check_vma=False,
    )
```

```python
import functools

import jax
import jax.numpy as jnp
from jax import lax
from jax.experimental import pallas as pl
from jax.experimental.pallas import tpu as pltpu
from jax.sharding import PartitionSpec as P

CAP = 32
NSP = 4
NSN = 6
COURANT = 0.35
WIDTH = NSP

ROW = 128
SPOT = 100
TALLY = 101
FREE = SPOT + 1
PIECE = ROW - FREE
PIECES = 4
KEEP = 26
REST = CAP - KEEP
GROUP = 8
STEP = 4
MARGINS = (4, 8)
VMEM_BYTES = 65500 * 1024


def slot_rows(dest, spot, cells):
    groups = dest.shape[0]
    shape = (ROW, ROW)
    row = lax.broadcasted_iota(jnp.int32, dest.shape, 0)
    lane = lax.broadcasted_iota(jnp.int32, dest.shape, 1)
    high = spot >= cells // 2
    side = jnp.where(high, 1, 0)
    inward = jnp.where(high, cells - 1 - spot, spot)
    least = (dest * 2 + side) << 21
    key = least + (inward << 10) + (row * ROW + lane)
    counts = [jnp.zeros((8, ROW), jnp.float32) for _ in range(groups)]
    for a in range(groups):
        column = jnp.broadcast_to(key[a : a + 1], shape).T
        for b in range(groups):
            before = (column >= least[b : b + 1]) & (column < key[b : b + 1])
            ones = jnp.where(before, 1.0, 0.0)
            counts[b] = counts[b] + jnp.sum(ones.reshape(ROW // 8, 8, ROW), axis=0)
    rank = jnp.concatenate([jnp.sum(c, axis=0, keepdims=True) for c in counts], 0)
    rank = rank.astype(jnp.int32)
    slot = jnp.where(high, CAP - 1 - rank, rank)
    devices = ROW
    spill = devices * KEEP + (slot - KEEP) * devices + dest
    return jnp.where(slot < KEEP, dest * KEEP + slot, spill)


def padded(channels):
    return pl.cdiv(channels, 8) * 8


def to_rows(fields, rows, channels, size_x):
    height = padded(channels)
    real = lax.broadcasted_iota(jnp.int32, (8, ROW), 0) < channels - (height - 8)
    tail = jnp.zeros((ROW - height, ROW), jnp.float32)
    for i in range(size_x):
        block = fields[pl.ds(i, height, stride=size_x), :]
        final = jnp.where(real, block[height - 8 :], 0.0)
        block = jnp.concatenate([block[: height - 8], final, tail], 0)
        rows[i * ROW : (i + 1) * ROW, :] = block.T


def clear_rows(staged):
    lane = lax.broadcasted_iota(jnp.int32, (1, ROW), 1)
    staged[...] = jnp.broadcast_to(jnp.where(lane == SPOT, -1.0, 0.0), staged.shape)


def pack_rows(rows, picks, spots, slots, staged, packed, sems):
    lane = lax.broadcasted_iota(jnp.int32, (1, ROW), 1)
    devices = packed.shape[0] // KEEP

    def move(r, carry):
        spot = jnp.full((1, ROW), spots[r], jnp.int32).astype(jnp.float32)
        row = rows[pl.ds(picks[r], 1), :]
        staged[pl.ds(slots[r], 1), :] = jnp.where(lane == SPOT, spot, row)
        return carry

    lax.fori_loop(0, slots.shape[0], move, 0, unroll=32)
    parts = sems.shape[0]
    count = devices // parts
    free = lax.broadcasted_iota(jnp.int32, (count, ROW), 1) >= FREE
    copies = []
    for part in range(parts):
        base = part * count
        for a in range(REST):
            start = devices * (KEEP + a) + base
            values = staged[start : start + count, :]
            for b in range(PIECES):
                where = pl.ds(base * KEEP + b * REST + a, count, stride=KEEP)
                piece = pltpu.roll(values, (FREE - b * PIECE) % ROW, 1)
                staged[where, :] = jnp.where(free, piece, staged[where, :])
        block = pl.ds(base * KEEP, count * KEEP)
        copies.append(pltpu.make_async_copy(staged.at[block], packed.at[block], sems.at[part]))
        copies[-1].start()
    return copies


def slot_values(moved, s, base, count):
    if s < KEEP:
        return moved[pl.ds(base * KEEP + s, count, stride=KEEP), :]
    lane = lax.broadcasted_iota(jnp.int32, (count, ROW), 1)
    values = jnp.zeros((count, ROW), jnp.float32)
    for b in range(PIECES):
        where = pl.ds(base * KEEP + b * REST + s - KEEP, count, stride=KEEP)
        piece = pltpu.roll(moved[where, :], (b * PIECE - FREE) % ROW, 1)
        values = jnp.where((lane >= b * PIECE) & (lane < (b + 1) * PIECE), piece, values)
    return values


def prepare(moved, arrivals, later, weights, columns, easts, size_x):
    lane = lax.broadcasted_iota(jnp.int32, (16, 2 * ROW), 1)
    pick = jnp.where((lane == SPOT) | (lane == SPOT + ROW), 1.0, 0.0).astype(jnp.bfloat16)
    devices = moved.shape[0] // KEEP
    depth = devices * GROUP
    tiles = CAP // GROUP
    count = devices // len(arrivals)
    north = lax.broadcasted_iota(jnp.int32, (ROW, depth), 0)
    tally = lax.broadcasted_iota(jnp.int32, (count, ROW), 1) == TALLY
    for part, arrival in enumerate(arrivals):
        arrival.wait()
        base = part * count
        for s in range(CAP):
            values = jnp.where(tally, 1.0, slot_values(moved, s, base, count))
            high = values.astype(jnp.bfloat16)
            low = (values - high.astype(jnp.float32)).astype(jnp.bfloat16)
            t, k = s // GROUP, s % GROUP
            start = t * depth + k * devices + base
            weights[start : start + count, :ROW] = high
            weights[start : start + count, ROW:] = low
    for copy in later:
        copy.start()
    reaches = []
    for t in range(tiles):
        spot = lax.dot_general(
            pick, weights[t * depth : (t + 1) * depth, :], (((1,), (1,)), ((), ())), preferred_element_type=jnp.float32
        )
        whole = spot.astype(jnp.int32)
        east, within = whole >> 7, whole & (ROW - 1)
        easts[t] = east.astype(jnp.float32).astype(jnp.bfloat16)
        columns[t] = jnp.where(north == within[0:1], 1.0, 0.0).astype(jnp.bfloat16)
        used = spot[0:8] >= 0.0
        reach = east[0:8].astype(jnp.float32)
        first = jnp.min(jnp.where(used, reach, float(size_x)))
        last = jnp.max(jnp.where(used, reach, -1.0))
        reaches.append((first.astype(jnp.int32), last.astype(jnp.int32)))
    return reaches


def add_rows(moved, arrivals, later, sums, weights, columns, easts, size_x):
    tiles, depth = easts.shape[0], easts.shape[2]
    reaches = prepare(moved, arrivals, later, weights, columns, easts, size_x)

    def block(t, here):
        column = columns[t].reshape(ROW // 16, 16, depth)
        parts = []
        for k in range(STEP):
            place = jnp.asarray(here + k, jnp.float32).astype(jnp.bfloat16)
            mine = jnp.where(easts[t] == place, 1.0, 0.0).astype(jnp.bfloat16)
            parts.append((column * mine[None]).reshape(ROW, depth))
        where = pl.ds(pl.multiple_of(here * ROW, ROW), STEP * ROW)
        both = jnp.dot(
            jnp.concatenate(parts, 0),
            weights[t * depth : (t + 1) * depth, :],
            preferred_element_type=jnp.float32,
        )
        sums[where, :] += both[:, :ROW] + both[:, ROW:]

    low = [min(size_x, size_x // 2 + margin) for margin in MARGINS]
    widths = low + low[::-1]
    fits = [last - first < width for (first, last), width in zip(reaches, widths)]
    narrow = functools.reduce(jnp.logical_and, fits)

    @pl.when(narrow)
    def _():
        for t in range(tiles):
            start = jnp.minimum(reaches[t][0], size_x - widths[t])
            for g in range(widths[t] // STEP):
                block(t, start + g * STEP)

    @pl.when(jnp.logical_not(narrow))
    def _():
        for t in range(tiles):
            first, last = reaches[t]
            blocks = jnp.maximum(last - first + STEP, 0) // STEP
            start = jnp.minimum(first, size_x - blocks * STEP)

            def reached(g, carry, t=t, start=start):
                block(t, start + g * STEP)
                return carry

            lax.fori_loop(0, blocks, reached, 0)


def add_scratch(devices):
    depth = devices * GROUP
    tiles = CAP // GROUP
    return [
        pltpu.VMEM((tiles * depth, 2 * ROW), jnp.bfloat16),
        pltpu.VMEM((tiles, ROW, depth), jnp.bfloat16),
        pltpu.VMEM((tiles, 16, depth), jnp.bfloat16),
    ]


def relax(fields, sums, out, channels, size_x, i):
    block = slice(i * ROW, (i + 1) * ROW)
    total = sums[block, :].T
    share = 1.0 / (1.0 + total[TALLY : TALLY + 1])
    height = padded(channels)
    where = pl.ds(i, height, stride=size_x)
    out[where, :] = (fields[where, :] + total[:height]) * share


def nest_step(state, metric, buoyancy, levels, size_x):
    shape = (size_x, ROW)
    row = lax.broadcasted_iota(jnp.int32, shape, 0)
    lane = lax.broadcasted_iota(jnp.int32, shape, 1)
    scaled = COURANT * metric[...]

    def at(field, k):
        start = (field * levels + k) * size_x
        return slice(start, start + size_x)

    w_below = jnp.zeros(shape, jnp.float32)
    p = state[at(4, 0), :]
    for k in range(levels):
        n = COURANT * buoyancy[k]
        p_above = state[at(4, k + 1), :] if k + 1 < levels else jnp.zeros(shape, jnp.float32)
        p_east = jnp.where(row == size_x - 1, 0.0, pltpu.roll(p, size_x - 1, 0))
        p_north = jnp.where(lane == ROW - 1, 0.0, pltpu.roll(p, ROW - 1, 1))
        u = state[at(0, k), :] - COURANT * (p_east - p)
        v = state[at(1, k), :] - COURANT * (p_north - p)
        edge = -COURANT * p
        u_west = jnp.where(row == 0, edge, pltpu.roll(u, 1, 0))
        v_south = jnp.where(lane == 0, edge, pltpu.roll(v, 1, 1))
        theta = state[at(3, k), :]
        w = state[at(2, k), :] - COURANT * (p_above - p) + n * theta
        state[at(0, k), :] = u
        state[at(1, k), :] = v
        state[at(2, k), :] = w
        state[at(3, k), :] = theta - n * w
        state[at(4, k), :] = p - scaled * ((u - u_west) + (v - v_south) + (w - w_below))
        w_below = w
        p = p_above


def planned(pairs, sems):
    return [pltpu.make_async_copy(a, b, sems.at[i]) for i, (a, b) in enumerate(pairs)]


def fetch(pairs, sems):
    copies = planned(pairs, sems)
    for copy in copies:
        copy.start()
    return copies


def split(source, target, parts):
    count = source.shape[0] // parts
    blocks = [pl.ds(part * count, count) for part in range(parts)]
    return [(source.at[block], target.at[block]) for block in blocks]


def strip_kernel(
    parent, dest, picks, spots, spot_rows, packed,
    tile, dest_v, picks_s, spots_s, spots_v, rows, staged, slots_v, slots, sems, slot_sems, out_sems,
    *, size_x, cells
):
    channels = parent.shape[0] // size_x
    copies = fetch(
        [(dest, dest_v), (spot_rows, spots_v), (picks, picks_s), (spots, spots_s)], sems
    )
    arrivals = fetch(split(parent, tile, out_sems.shape[0]), out_sems)
    clear_rows(staged)
    copies[0].wait()
    copies[1].wait()
    slots_v[...] = slot_rows(dest_v[...], spots_v[...], cells)
    moves = fetch(
        [(slots_v.at[a], slots.at[pl.ds(a * ROW, ROW)]) for a in range(slots_v.shape[0])], slot_sems
    )
    for copy in arrivals:
        copy.wait()
    to_rows(tile, rows, channels, size_x)
    for copy in copies[2:] + moves:
        copy.wait()
    for copy in pack_rows(rows, picks_s, spots_s, slots, staged, packed, out_sems):
        copy.wait()


def nest_kernel(
    moved, nest, metric, buoyancy, picks, spots, slots, out, packed,
    came, tile, metric_v, buoyancy_s, picks_s, spots_s, slots_s, state, sums, rows, staged,
    weights, columns, easts, sems, out_sems,
    *, size_x
):
    channels = nest.shape[0] // size_x
    arrivals = fetch(split(moved, came, out_sems.shape[0]), out_sems)
    copies = planned(
        [(nest, tile.at[pl.ds(0, nest.shape[0])]), (metric, metric_v), (buoyancy, buoyancy_s)]
        + [(picks, picks_s), (spots, spots_s), (slots, slots_s)],
        sems,
    )
    sums[...] = jnp.zeros(sums.shape, jnp.float32)
    clear_rows(staged)
    add_rows(came, arrivals, copies, sums, weights, columns, easts, size_x)
    for copy in copies:
        copy.wait()
    for i in range(size_x):
        relax(tile, sums, state, channels, size_x, i)

    def step(_, carry):
        nest_step(state, metric_v, buoyancy_s, channels // 5, size_x)
        return carry

    lax.fori_loop(0, NSN, step, 0)
    result = pltpu.make_async_copy(state.at[pl.ds(0, out.shape[0])], out, sems.at[0])
    result.start()
    to_rows(state, rows, channels, size_x)
    for copy in pack_rows(rows, picks_s, spots_s, slots_s, staged, packed, out_sems):
        copy.wait()
    result.wait()


def rim_kernel(odd, head, tail, metric, near, far):
    channels, block = head.shape[:2]
    size_x = metric.shape[0]

    def cut(first, last):
        for c in range(0, channels, 2):
            pair = slice(c * WIDTH, (c + 2) * WIDTH)
            first[pair, :] = jnp.concatenate([head[c, :WIDTH], head[c + 1, :WIDTH]], 0)
            last[pair, :] = jnp.concatenate(
                [tail[c, block - WIDTH :], tail[c + 1, block - WIDTH :]], 0
            )
        own = slice(channels * WIDTH, (channels + 1) * WIDTH)
        first[own, :] = metric[:WIDTH]
        last[own, :] = metric[size_x - WIDTH :]

    @pl.when(odd[0] == 1)
    def _():
        cut(near, far)

    @pl.when(odd[0] == 0)
    def _():
        cut(far, near)


def rim_rows(odd, near, far, c):
    rim = slice(c * WIDTH, (c + 1) * WIDTH)
    ours, theirs = near[rim, :], far[rim, :]
    even = odd[0] == 0
    return jnp.concatenate([jnp.where(even, ours, theirs), jnp.where(even, theirs, ours)], 0)


def strip_rim_kernel(odd, parent, metric, near, far, dest, spots, first, last, slots):
    size_x = metric.shape[0]
    channels = parent.shape[0] // size_x
    slots[...] = slot_rows(dest[...], spots[...], size_x * ROW)

    def rows(c):
        own = parent[c * size_x : (c + 1) * size_x, :] if c < channels else metric[...]
        return jnp.concatenate([own, rim_rows(odd, near, far, c)], 0)

    gather_lanes(rows, channels + 1, size_x + 2 * WIDTH, first, last)


def gather_lanes(rows, count, height, first, last):
    per = ROW // WIDTH
    lane = lax.broadcasted_iota(jnp.int32, (height, ROW), 1) // WIDTH
    for q in range(pl.cdiv(count, per)):
        ahead = jnp.zeros((height, ROW), jnp.float32)
        behind = ahead
        for m in range(min(per, count - q * per)):
            own = rows(q * per + m)
            ahead = jnp.where(lane == m, pltpu.roll(own, m * WIDTH, 1), ahead)
            behind = jnp.where(lane == m, pltpu.roll(own, (m + 1) * WIDTH % ROW, 1), behind)
        where = slice(q * height, (q + 1) * height)
        first[where, :] = ahead
        last[where, :] = behind


def parent_kernel(
    odd, edge, buoyancy, parent, metric, near, far, after_y, before_y, out, state, scaled
):
    size_x = metric.shape[0]
    channels = parent.shape[0] // size_x
    levels = channels // 5
    tall = size_x + 2 * WIDTH
    per = ROW // WIDTH
    shape = (tall, 2 * ROW)
    group = lax.broadcasted_iota(jnp.int32, (tall, ROW), 1) // WIDTH

    def extended(c, own):
        m = c % per
        rows = slice(c // per * tall, (c // per + 1) * tall)
        ahead = pltpu.roll(after_y[rows, :], -m * WIDTH % ROW, 1)
        behind = pltpu.roll(before_y[rows, :], (per - 1 - m) * WIDTH, 1)
        side = jnp.where(group == 0, ahead, jnp.where(group == per - 1, behind, 0.0))
        middle = jnp.concatenate([own, rim_rows(odd, near, far, c)], 0)
        return jnp.concatenate([middle, side], 1)

    for c in range(channels):
        state[c] = extended(c, parent[c * size_x : (c + 1) * size_x, :])
    scaled[...] = COURANT * extended(channels, metric[...])
    row = lax.broadcasted_iota(jnp.int32, shape, 0)
    lane = lax.broadcasted_iota(jnp.int32, shape, 1)
    u_keep = jnp.where((row >= tall - WIDTH) & (edge[0] == 1), 0.0, 1.0)
    v_keep = jnp.where((lane >= 2 * ROW - WIDTH) & (edge[1] == 1), 0.0, 1.0)

    def step(_, carry):
        w_below = jnp.zeros(shape, jnp.float32)
        p = state[4 * levels]
        for k in range(levels):
            n = COURANT * buoyancy[k]
            p_above = state[4 * levels + k + 1] if k + 1 < levels else jnp.zeros(shape, jnp.float32)
            u = state[k] - COURANT * (pltpu.roll(p, tall - 1, 0) - p)
            v = state[levels + k] - COURANT * (pltpu.roll(p, 2 * ROW - 1, 1) - p)
            theta = state[3 * levels + k]
            w = state[2 * levels + k] - COURANT * (p_above - p) + n * theta
            spread = (u - pltpu.roll(u, 1, 0)) + (v - pltpu.roll(v, 1, 1)) + (w - w_below)
            state[k] = u * u_keep
            state[levels + k] = v * v_keep
            state[2 * levels + k] = w
            state[3 * levels + k] = theta - n * w
            state[4 * levels + k] = p - scaled[...] * spread
            w_below = w
            p = p_above
        return carry

    lax.fori_loop(0, NSP, step, 0)
    for c in range(channels):
        out[c * size_x : (c + 1) * size_x, :] = state[c, :size_x, :ROW]


def final_kernel(
    moved, parent, out, came, tile, result, sums, weights, columns, easts, sems, out_sems, *, size_x
):
    channels = parent.shape[0] // size_x
    arrivals = fetch(split(moved, came, out_sems.shape[0]), out_sems)
    copies = planned([(parent, tile.at[pl.ds(0, parent.shape[0])])], sems)
    flat = result.reshape(padded(channels) * size_x, ROW)
    count = size_x // out_sems.shape[0]
    blocks = [(pl.ds(0, channels), pl.ds(start, count)) for start in range(0, size_x, count)]
    leaving = planned([(result.at[block], out.at[block]) for block in blocks], out_sems)

    sums[...] = jnp.zeros(sums.shape, jnp.float32)
    add_rows(came, arrivals, copies, sums, weights, columns, easts, size_x)
    copies[0].wait()
    for i in range(size_x):
        relax(tile, sums, flat, channels, size_x, i)
        if i % count == count - 1:
            leaving[i // count].start()
    for copy in leaving:
        copy.wait()


def vmem():
    return pl.BlockSpec(memory_space=pltpu.VMEM)


def smem():
    return pl.BlockSpec(memory_space=pltpu.SMEM)


def anywhere():
    return pl.BlockSpec(memory_space=pltpu.HBM)


def params():
    return pltpu.CompilerParams(vmem_limit_bytes=VMEM_BYTES)


def exchange(packed, devices):
    moved = lax.all_to_all(
        packed.reshape(devices, KEEP * ROW), ("gx", "gy"), split_axis=0, concat_axis=0, tiled=True
    )
    return moved.reshape(devices * KEEP, ROW)


def swapped(near, far, axis):
    size = lax.axis_size(axis)
    pairs = [[(i, i + 1) for i in range(start, size - 1, 2)] for start in (0, 1)]
    pairs = [some + [(j, i) for i, j in some] for some in pairs]
    return lax.ppermute(near, axis, pairs[0]), lax.ppermute(far, axis, pairs[1])


def shifted(first, last, axis):
    size = lax.axis_size(axis)
    up = [(i, i + 1) for i in range(size - 1)]
    down = [(j, i) for i, j in up]
    return lax.ppermute(first, axis, down), lax.ppermute(last, axis, up)


def on_device(
    parent,
    metric,
    buoyancy,
    nest,
    nest_metric,
    strip_col,
    strip_dest,
    strip_pos,
    panel_src,
    panel_dest,
    panel_col,
):
    devices = lax.axis_size("gx") * lax.axis_size("gy")
    channels = parent.shape[0] * parent.shape[1]
    tile_x, tile_y = parent.shape[2:]
    block_x, block_y = nest.shape[2:]
    slots = strip_col.shape[0]
    groups = slots // ROW
    tile_shape = (channels * tile_x, tile_y)
    block_shape = (channels * block_x, block_y)
    packed_shape = (devices * KEEP, ROW)
    parts = 4

    def shape(*dims, dtype=jnp.float32):
        return jax.ShapeDtypeStruct(dims, dtype)

    def index(memory):
        return memory((slots,), jnp.int32)

    listed = pltpu.VMEM((groups, ROW), jnp.int32)
    rim_x = shape((channels + 1) * WIDTH, ROW)
    tile = parent.reshape(channels, tile_x, tile_y)
    ends = [
        pl.BlockSpec((channels, GROUP, ROW), lambda i, place=place: (0, place, 0))
        for place in (0, tile_x // GROUP - 1)
    ]
    whole_rim = pl.BlockSpec(rim_x.shape, lambda i: (0, 0))
    odd = (lax.axis_index("gx") % 2).astype(jnp.int32).reshape(1)
    near, far = pl.pallas_call(
        rim_kernel,
        grid=(1,),
        out_shape=(rim_x, rim_x),
        in_specs=[smem()] + ends + [pl.BlockSpec(metric.shape, lambda i: (0, 0))],
        out_specs=(whole_rim, whole_rim),
        compiler_params=params(),
        name="cut_rims",
    )(odd, tile, tile, metric)
    near, far = swapped(near, far, "gx")
    packed = pl.pallas_call(
        functools.partial(strip_kernel, size_x=tile_x, cells=block_x * block_y),
        out_shape=shape(*packed_shape),
        in_specs=[anywhere()] * 5,
        out_specs=anywhere(),
        scratch_shapes=[
            pltpu.VMEM((padded(channels) * tile_x, tile_y), jnp.float32),
            listed,
            index(pltpu.SMEM),
            index(pltpu.SMEM),
            listed,
            pltpu.VMEM((tile_x * tile_y, ROW), jnp.float32),
            pltpu.VMEM((devices * CAP, ROW), jnp.float32),
            listed,
            index(pltpu.SMEM),
            pltpu.SemaphoreType.DMA((4,)),
            pltpu.SemaphoreType.DMA((groups,)),
            pltpu.SemaphoreType.DMA((parts,)),
        ],
        compiler_params=params(),
        name="pack_strips",
    )(
        parent.reshape(tile_shape),
        strip_dest.reshape(groups, ROW),
        strip_col,
        strip_pos,
        strip_pos.reshape(groups, ROW),
    )

    packed, near, far, late_parent, late_metric, late_dest, late_col = (
        lax.optimization_barrier(
            (packed, near, far, parent.reshape(tile_shape), metric, panel_dest, panel_col)
        )
    )
    moved = exchange(packed, devices)
    tall = tile_x + 2 * WIDTH
    rim_y = shape(pl.cdiv(channels + 1, ROW // WIDTH) * tall, ROW)
    first_y, last_y, panel_slots = pl.pallas_call(
        strip_rim_kernel,
        out_shape=(rim_y, rim_y, shape(groups, ROW, dtype=jnp.int32)),
        in_specs=[smem()] + [vmem()] * 6,
        out_specs=(vmem(),) * 3,
        compiler_params=params(),
        cost_estimate=pl.CostEstimate(flops=3_000_000, bytes_accessed=2_000_000, transcendentals=0),
        name="pack_rims",
    )(
        odd,
        late_parent,
        late_metric,
        near,
        far,
        late_dest.reshape(groups, ROW),
        late_col.reshape(groups, ROW),
    )
    after_y, before_y = shifted(first_y, last_y, "gy")
    moved, after_y, before_y, panel_slots = lax.optimization_barrier(
        (moved, after_y, before_y, panel_slots)
    )
    nest_out, packed = pl.pallas_call(
        functools.partial(nest_kernel, size_x=block_x),
        out_shape=(shape(*block_shape), shape(*packed_shape)),
        in_specs=[anywhere()] * 7,
        out_specs=(anywhere(), anywhere()),
        scratch_shapes=[
            pltpu.VMEM(packed_shape, jnp.float32),
            pltpu.VMEM((padded(channels) * block_x, block_y), jnp.float32),
            pltpu.VMEM((block_x, block_y), jnp.float32),
            pltpu.SMEM(buoyancy.shape, jnp.float32),
            index(pltpu.SMEM),
            index(pltpu.SMEM),
            index(pltpu.SMEM),
            pltpu.VMEM((padded(channels) * block_x, block_y), jnp.float32),
            pltpu.VMEM((block_x * block_y, ROW), jnp.float32),
            pltpu.VMEM((block_x * block_y, ROW), jnp.float32),
            pltpu.VMEM((devices * CAP, ROW), jnp.float32),
        ]
        + add_scratch(devices)
        + [pltpu.SemaphoreType.DMA((6,)), pltpu.SemaphoreType.DMA((parts,))],
        compiler_params=params(),
        name="step_nest",
    )(
        moved,
        nest.reshape(block_shape),
        nest_metric,
        buoyancy,
        panel_src,
        panel_col,
        panel_slots.reshape(slots),
    )
    moved = exchange(packed, devices)
    edge = jnp.stack([lax.axis_index("gx") == 0, lax.axis_index("gy") == 0]).astype(jnp.int32)
    parent_state = pl.pallas_call(
        parent_kernel,
        out_shape=shape(*tile_shape),
        in_specs=[smem()] * 3 + [vmem()] * 6,
        out_specs=vmem(),
        scratch_shapes=[
            pltpu.VMEM((channels, tall, 2 * ROW), jnp.float32),
            pltpu.VMEM((tall, 2 * ROW), jnp.float32),
        ],
        compiler_params=params(),
        cost_estimate=pl.CostEstimate(flops=20_000_000, bytes_accessed=8_000_000, transcendentals=0),
        name="step_parent",
    )(odd, edge, buoyancy, late_parent, late_metric, near, far, after_y, before_y)

    parent_out = pl.pallas_call(
        functools.partial(final_kernel, size_x=tile_x),
        out_shape=shape(channels, tile_x, tile_y),
        in_specs=[anywhere(), anywhere()],
        out_specs=anywhere(),
        scratch_shapes=[
            pltpu.VMEM(packed_shape, jnp.float32),
            pltpu.VMEM((padded(channels) * tile_x, tile_y), jnp.float32),
            pltpu.VMEM((padded(channels), tile_x, tile_y), jnp.float32),
            pltpu.VMEM((tile_x * tile_y, ROW), jnp.float32),
        ]
        + add_scratch(devices)
        + [pltpu.SemaphoreType.DMA((1,)), pltpu.SemaphoreType.DMA((parts,))],
        compiler_params=params(),
        name="add_panels",
    )(moved, parent_state)
    return (parent_out.reshape(parent.shape), nest_out.reshape(nest.shape))


def solution(mesh):
    placed = (
        P(None, None, "gx", "gy"),
        P("gx", "gy"),
        P(),
        P(None, None, "gx", "gy"),
        P("gx", "gy"),
        P(("gx", "gy")),
        P(("gx", "gy"), None),
        P(("gx", "gy")),
        P(("gx", "gy")),
        P(("gx", "gy"), None),
        P(("gx", "gy")),
    )
    return jax.shard_map(
        on_device,
        mesh=mesh,
        in_specs=placed,
        out_specs=(P(None, None, "gx", "gy"), P(None, None, "gx", "gy")),
        check_vma=False,
    )
```

```python
import functools

import jax
import jax.numpy as jnp
from jax import lax
from jax.experimental import pallas as pl
from jax.experimental.pallas import tpu as pltpu
from jax.sharding import PartitionSpec as P

CAP = 32
NSP = 4
NSN = 6
COURANT = 0.35
WIDTH = NSP

ROW = 128
SPOT = 100
TALLY = 101
FREE = SPOT + 1
PIECE = ROW - FREE
PIECES = 4
KEEP = 26
REST = CAP - KEEP
GROUP = 8
STEP = 4
MARGINS = (4, 8)
VMEM_BYTES = 65500 * 1024


def slot_rows(dest, spot, cells):
    groups = dest.shape[0]
    shape = (ROW, ROW)
    row = lax.broadcasted_iota(jnp.int32, dest.shape, 0)
    lane = lax.broadcasted_iota(jnp.int32, dest.shape, 1)
    high = spot >= cells // 2
    side = jnp.where(high, 1, 0)
    inward = jnp.where(high, cells - 1 - spot, spot)
    least = (dest * 2 + side) << 21
    key = least + (inward << 10) + (row * ROW + lane)
    counts = [jnp.zeros((8, ROW), jnp.float32) for _ in range(groups)]
    for a in range(groups):
        column = jnp.broadcast_to(key[a : a + 1], shape).T
        for b in range(groups):
            before = (column >= least[b : b + 1]) & (column < key[b : b + 1])
            ones = jnp.where(before, 1.0, 0.0)
            counts[b] = counts[b] + jnp.sum(ones.reshape(ROW // 8, 8, ROW), axis=0)
    rank = jnp.concatenate([jnp.sum(c, axis=0, keepdims=True) for c in counts], 0)
    rank = rank.astype(jnp.int32)
    slot = jnp.where(high, CAP - 1 - rank, rank)
    devices = ROW
    spill = devices * KEEP + (slot - KEEP) * devices + dest
    return jnp.where(slot < KEEP, dest * KEEP + slot, spill)


def padded(channels):
    return pl.cdiv(channels, 8) * 8


def to_rows(fields, rows, channels, size_x):
    height = padded(channels)
    real = lax.broadcasted_iota(jnp.int32, (8, ROW), 0) < channels - (height - 8)
    tail = jnp.zeros((ROW - height, ROW), jnp.float32)
    for i in range(size_x):
        block = fields[pl.ds(i, height, stride=size_x), :]
        final = jnp.where(real, block[height - 8 :], 0.0)
        block = jnp.concatenate([block[: height - 8], final, tail], 0)
        rows[i * ROW : (i + 1) * ROW, :] = block.T


def clear_rows(staged):
    lane = lax.broadcasted_iota(jnp.int32, (1, ROW), 1)
    staged[...] = jnp.broadcast_to(jnp.where(lane == SPOT, -1.0, 0.0), staged.shape)


def pack_rows(rows, picks, spots, slots, staged, packed, sems):
    lane = lax.broadcasted_iota(jnp.int32, (1, ROW), 1)
    devices = packed.shape[0] // KEEP

    def move(r, carry):
        spot = jnp.full((1, ROW), spots[r], jnp.int32).astype(jnp.float32)
        row = rows[pl.ds(picks[r], 1), :]
        staged[pl.ds(slots[r], 1), :] = jnp.where(lane == SPOT, spot, row)
        return carry

    lax.fori_loop(0, slots.shape[0], move, 0, unroll=32)
    parts = sems.shape[0]
    count = devices // parts
    free = lax.broadcasted_iota(jnp.int32, (count, ROW), 1) >= FREE
    copies = []
    for part in range(parts):
        base = part * count
        for a in range(REST):
            start = devices * (KEEP + a) + base
            values = staged[start : start + count, :]
            for b in range(PIECES):
                where = pl.ds(base * KEEP + b * REST + a, count, stride=KEEP)
                piece = pltpu.roll(values, (FREE - b * PIECE) % ROW, 1)
                staged[where, :] = jnp.where(free, piece, staged[where, :])
        block = pl.ds(base * KEEP, count * KEEP)
        copies.append(pltpu.make_async_copy(staged.at[block], packed.at[block], sems.at[part]))
        copies[-1].start()
    return copies


def slot_values(moved, s, base, count):
    if s < KEEP:
        return moved[pl.ds(base * KEEP + s, count, stride=KEEP), :]
    lane = lax.broadcasted_iota(jnp.int32, (count, ROW), 1)
    values = jnp.zeros((count, ROW), jnp.float32)
    for b in range(PIECES):
        where = pl.ds(base * KEEP + b * REST + s - KEEP, count, stride=KEEP)
        piece = pltpu.roll(moved[where, :], (b * PIECE - FREE) % ROW, 1)
        values = jnp.where((lane >= b * PIECE) & (lane < (b + 1) * PIECE), piece, values)
    return values


def prepare(moved, arrivals, later, weights, columns, easts, size_x):
    lane = lax.broadcasted_iota(jnp.int32, (16, 2 * ROW), 1)
    pick = jnp.where((lane == SPOT) | (lane == SPOT + ROW), 1.0, 0.0).astype(jnp.bfloat16)
    devices = moved.shape[0] // KEEP
    depth = devices * GROUP
    tiles = CAP // GROUP
    count = devices // len(arrivals)
    north = lax.broadcasted_iota(jnp.int32, (ROW, depth), 0)
    tally = lax.broadcasted_iota(jnp.int32, (count, ROW), 1) == TALLY
    for part, arrival in enumerate(arrivals):
        arrival.wait()
        base = part * count
        for s in range(CAP):
            values = jnp.where(tally, 1.0, slot_values(moved, s, base, count))
            high = values.astype(jnp.bfloat16)
            low = (values - high.astype(jnp.float32)).astype(jnp.bfloat16)
            t, k = s // GROUP, s % GROUP
            start = t * depth + k * devices + base
            weights[start : start + count, :ROW] = high
            weights[start : start + count, ROW:] = low
    for copy in later:
        copy.start()
    reaches = []
    for t in range(tiles):
        spot = lax.dot_general(
            pick, weights[t * depth : (t + 1) * depth, :], (((1,), (1,)), ((), ())), preferred_element_type=jnp.float32
        )
        whole = spot.astype(jnp.int32)
        east, within = whole >> 7, whole & (ROW - 1)
        easts[t] = east.astype(jnp.float32).astype(jnp.bfloat16)
        columns[t] = jnp.where(north == within[0:1], 1.0, 0.0).astype(jnp.bfloat16)
        used = spot[0:8] >= 0.0
        reach = east[0:8].astype(jnp.float32)
        first = jnp.min(jnp.where(used, reach, float(size_x)))
        last = jnp.max(jnp.where(used, reach, -1.0))
        reaches.append((first.astype(jnp.int32), last.astype(jnp.int32)))
    return reaches


def add_rows(moved, arrivals, later, sums, weights, columns, easts, size_x):
    tiles, depth = easts.shape[0], easts.shape[2]
    reaches = prepare(moved, arrivals, later, weights, columns, easts, size_x)

    def block(t, here):
        column = columns[t].reshape(ROW // 16, 16, depth)
        parts = []
        for k in range(STEP):
            place = jnp.asarray(here + k, jnp.float32).astype(jnp.bfloat16)
            mine = jnp.where(easts[t] == place, 1.0, 0.0).astype(jnp.bfloat16)
            parts.append((column * mine[None]).reshape(ROW, depth))
        where = pl.ds(pl.multiple_of(here * ROW, ROW), STEP * ROW)
        both = jnp.dot(
            jnp.concatenate(parts, 0),
            weights[t * depth : (t + 1) * depth, :],
            preferred_element_type=jnp.float32,
        )
        sums[where, :] += both[:, :ROW] + both[:, ROW:]

    low = [min(size_x, size_x // 2 + margin) for margin in MARGINS]
    widths = low + low[::-1]
    fits = [last - first < width for (first, last), width in zip(reaches, widths)]
    narrow = functools.reduce(jnp.logical_and, fits)

    @pl.when(narrow)
    def _():
        for t in range(tiles):
            start = jnp.minimum(reaches[t][0], size_x - widths[t])
            for g in range(widths[t] // STEP):
                block(t, start + g * STEP)

    @pl.when(jnp.logical_not(narrow))
    def _():
        for t in range(tiles):
            first, last = reaches[t]
            blocks = jnp.maximum(last - first + STEP, 0) // STEP
            start = jnp.minimum(first, size_x - blocks * STEP)

            def reached(g, carry, t=t, start=start):
                block(t, start + g * STEP)
                return carry

            lax.fori_loop(0, blocks, reached, 0)


def add_scratch(devices):
    depth = devices * GROUP
    tiles = CAP // GROUP
    return [
        pltpu.VMEM((tiles * depth, 2 * ROW), jnp.bfloat16),
        pltpu.VMEM((tiles, ROW, depth), jnp.bfloat16),
        pltpu.VMEM((tiles, 16, depth), jnp.bfloat16),
    ]


def relax(fields, sums, out, channels, size_x, i):
    block = slice(i * ROW, (i + 1) * ROW)
    total = sums[block, :].T
    share = 1.0 / (1.0 + total[TALLY : TALLY + 1])
    height = padded(channels)
    where = pl.ds(i, height, stride=size_x)
    out[where, :] = (fields[where, :] + total[:height]) * share


def nest_step(state, metric, buoyancy, levels, size_x):
    shape = (size_x, ROW)
    row = lax.broadcasted_iota(jnp.int32, shape, 0)
    lane = lax.broadcasted_iota(jnp.int32, shape, 1)
    scaled = COURANT * metric[...]

    def at(field, k):
        start = (field * levels + k) * size_x
        return slice(start, start + size_x)

    w_below = jnp.zeros(shape, jnp.float32)
    p = state[at(4, 0), :]
    for k in range(levels):
        n = COURANT * buoyancy[k]
        p_above = state[at(4, k + 1), :] if k + 1 < levels else jnp.zeros(shape, jnp.float32)
        p_east = jnp.where(row == size_x - 1, 0.0, pltpu.roll(p, size_x - 1, 0))
        p_north = jnp.where(lane == ROW - 1, 0.0, pltpu.roll(p, ROW - 1, 1))
        u = state[at(0, k), :] - COURANT * (p_east - p)
        v = state[at(1, k), :] - COURANT * (p_north - p)
        edge = -COURANT * p
        u_west = jnp.where(row == 0, edge, pltpu.roll(u, 1, 0))
        v_south = jnp.where(lane == 0, edge, pltpu.roll(v, 1, 1))
        theta = state[at(3, k), :]
        w = state[at(2, k), :] - COURANT * (p_above - p) + n * theta
        state[at(0, k), :] = u
        state[at(1, k), :] = v
        state[at(2, k), :] = w
        state[at(3, k), :] = theta - n * w
        state[at(4, k), :] = p - scaled * ((u - u_west) + (v - v_south) + (w - w_below))
        w_below = w
        p = p_above


def planned(pairs, sems):
    return [pltpu.make_async_copy(a, b, sems.at[i]) for i, (a, b) in enumerate(pairs)]


def fetch(pairs, sems):
    copies = planned(pairs, sems)
    for copy in copies:
        copy.start()
    return copies


def split(source, target, parts):
    count = source.shape[0] // parts
    blocks = [pl.ds(part * count, count) for part in range(parts)]
    return [(source.at[block], target.at[block]) for block in blocks]


def strip_kernel(
    parent, dest, picks, spots, spot_rows, packed,
    tile, dest_v, picks_s, spots_s, spots_v, rows, staged, slots_v, slots, sems, slot_sems, out_sems,
    *, size_x, cells
):
    channels = parent.shape[0] // size_x
    copies = fetch(
        [(dest, dest_v), (spot_rows, spots_v), (picks, picks_s), (spots, spots_s)], sems
    )
    arrivals = fetch(split(parent, tile, out_sems.shape[0]), out_sems)
    clear_rows(staged)
    copies[0].wait()
    copies[1].wait()
    slots_v[...] = slot_rows(dest_v[...], spots_v[...], cells)
    moves = fetch(
        [(slots_v.at[a], slots.at[pl.ds(a * ROW, ROW)]) for a in range(slots_v.shape[0])], slot_sems
    )
    for copy in arrivals:
        copy.wait()
    to_rows(tile, rows, channels, size_x)
    for copy in copies[2:] + moves:
        copy.wait()
    for copy in pack_rows(rows, picks_s, spots_s, slots, staged, packed, out_sems):
        copy.wait()


def nest_kernel(
    moved, nest, metric, buoyancy, picks, spots, slots, out, packed,
    came, tile, metric_v, buoyancy_s, picks_s, spots_s, slots_s, state, sums, rows, staged,
    weights, columns, easts, sems, out_sems,
    *, size_x
):
    channels = nest.shape[0] // size_x
    arrivals = fetch(split(moved, came, out_sems.shape[0]), out_sems)
    copies = planned(
        [(nest, tile.at[pl.ds(0, nest.shape[0])]), (metric, metric_v), (buoyancy, buoyancy_s)]
        + [(picks, picks_s), (spots, spots_s), (slots, slots_s)],
        sems,
    )
    sums[...] = jnp.zeros(sums.shape, jnp.float32)
    clear_rows(staged)
    add_rows(came, arrivals, copies, sums, weights, columns, easts, size_x)
    for copy in copies:
        copy.wait()
    for i in range(size_x):
        relax(tile, sums, state, channels, size_x, i)

    def step(_, carry):
        nest_step(state, metric_v, buoyancy_s, channels // 5, size_x)
        return carry

    lax.fori_loop(0, NSN, step, 0)
    result = pltpu.make_async_copy(state.at[pl.ds(0, out.shape[0])], out, sems.at[0])
    result.start()
    to_rows(state, rows, channels, size_x)
    for copy in pack_rows(rows, picks_s, spots_s, slots_s, staged, packed, out_sems):
        copy.wait()
    result.wait()


def rim_kernel(odd, head, tail, metric, near, far):
    channels, block = head.shape[:2]
    size_x = metric.shape[0]

    def cut(first, last):
        for c in range(0, channels, 2):
            pair = slice(c * WIDTH, (c + 2) * WIDTH)
            first[pair, :] = jnp.concatenate([head[c, :WIDTH], head[c + 1, :WIDTH]], 0)
            last[pair, :] = jnp.concatenate(
                [tail[c, block - WIDTH :], tail[c + 1, block - WIDTH :]], 0
            )
        own = slice(channels * WIDTH, (channels + 1) * WIDTH)
        first[own, :] = metric[:WIDTH]
        last[own, :] = metric[size_x - WIDTH :]

    @pl.when(odd[0] == 1)
    def _():
        cut(near, far)

    @pl.when(odd[0] == 0)
    def _():
        cut(far, near)


def rim_rows(odd, near, far, c):
    rim = slice(c * WIDTH, (c + 1) * WIDTH)
    ours, theirs = near[rim, :], far[rim, :]
    even = odd[0] == 0
    return jnp.concatenate([jnp.where(even, ours, theirs), jnp.where(even, theirs, ours)], 0)


def strip_rim_kernel(odd, parent, metric, near, far, dest, spots, first, last, slots):
    size_x = metric.shape[0]
    channels = parent.shape[0] // size_x
    slots[...] = slot_rows(dest[...], spots[...], size_x * ROW)

    def rows(c):
        own = parent[c * size_x : (c + 1) * size_x, :] if c < channels else metric[...]
        return jnp.concatenate([own, rim_rows(odd, near, far, c)], 0)

    gather_lanes(rows, channels + 1, size_x + 2 * WIDTH, first, last)


def gather_lanes(rows, count, height, first, last):
    per = ROW // WIDTH
    lane = lax.broadcasted_iota(jnp.int32, (height, ROW), 1) // WIDTH
    for q in range(pl.cdiv(count, per)):
        ahead = jnp.zeros((height, ROW), jnp.float32)
        behind = ahead
        for m in range(min(per, count - q * per)):
            own = rows(q * per + m)
            ahead = jnp.where(lane == m, pltpu.roll(own, m * WIDTH, 1), ahead)
            behind = jnp.where(lane == m, pltpu.roll(own, (m + 1) * WIDTH % ROW, 1), behind)
        where = slice(q * height, (q + 1) * height)
        first[where, :] = ahead
        last[where, :] = behind


def parent_kernel(
    odd, edge, buoyancy, parent, metric, near, far, after_y, before_y, out, state, scaled
):
    size_x = metric.shape[0]
    channels = parent.shape[0] // size_x
    levels = channels // 5
    tall = size_x + 2 * WIDTH
    per = ROW // WIDTH
    shape = (tall, 2 * ROW)
    group = lax.broadcasted_iota(jnp.int32, (tall, ROW), 1) // WIDTH

    def extended(c, own):
        m = c % per
        rows = slice(c // per * tall, (c // per + 1) * tall)
        ahead = pltpu.roll(after_y[rows, :], -m * WIDTH % ROW, 1)
        behind = pltpu.roll(before_y[rows, :], (per - 1 - m) * WIDTH, 1)
        side = jnp.where(group == 0, ahead, jnp.where(group == per - 1, behind, 0.0))
        middle = jnp.concatenate([own, rim_rows(odd, near, far, c)], 0)
        return jnp.concatenate([middle, side], 1)

    for c in range(channels):
        state[c] = extended(c, parent[c * size_x : (c + 1) * size_x, :])
    scaled[...] = COURANT * extended(channels, metric[...])
    row = lax.broadcasted_iota(jnp.int32, shape, 0)
    lane = lax.broadcasted_iota(jnp.int32, shape, 1)
    u_keep = jnp.where((row >= tall - WIDTH) & (edge[0] == 1), 0.0, 1.0)
    v_keep = jnp.where((lane >= 2 * ROW - WIDTH) & (edge[1] == 1), 0.0, 1.0)

    def step(_, carry):
        w_below = jnp.zeros(shape, jnp.float32)
        p = state[4 * levels]
        for k in range(levels):
            n = COURANT * buoyancy[k]
            p_above = state[4 * levels + k + 1] if k + 1 < levels else jnp.zeros(shape, jnp.float32)
            u = state[k] - COURANT * (pltpu.roll(p, tall - 1, 0) - p)
            v = state[levels + k] - COURANT * (pltpu.roll(p, 2 * ROW - 1, 1) - p)
            theta = state[3 * levels + k]
            w = state[2 * levels + k] - COURANT * (p_above - p) + n * theta
            spread = (u - pltpu.roll(u, 1, 0)) + (v - pltpu.roll(v, 1, 1)) + (w - w_below)
            state[k] = u * u_keep
            state[levels + k] = v * v_keep
            state[2 * levels + k] = w
            state[3 * levels + k] = theta - n * w
            state[4 * levels + k] = p - scaled[...] * spread
            w_below = w
            p = p_above
        return carry

    lax.fori_loop(0, NSP, step, 0)
    for c in range(channels):
        out[c * size_x : (c + 1) * size_x, :] = state[c, :size_x, :ROW]


def final_kernel(
    moved, parent, out, came, tile, result, sums, weights, columns, easts, sems, out_sems, *, size_x
):
    channels = parent.shape[0] // size_x
    arrivals = fetch(split(moved, came, out_sems.shape[0]), out_sems)
    copies = planned([(parent, tile.at[pl.ds(0, parent.shape[0])])], sems)
    flat = result.reshape(padded(channels) * size_x, ROW)
    count = size_x // out_sems.shape[0]
    blocks = [(pl.ds(0, channels), pl.ds(start, count)) for start in range(0, size_x, count)]
    leaving = planned([(result.at[block], out.at[block]) for block in blocks], out_sems)

    sums[...] = jnp.zeros(sums.shape, jnp.float32)
    add_rows(came, arrivals, copies, sums, weights, columns, easts, size_x)
    copies[0].wait()
    for i in range(size_x):
        relax(tile, sums, flat, channels, size_x, i)
        if i % count == count - 1:
            leaving[i // count].start()
    for copy in leaving:
        copy.wait()


def vmem():
    return pl.BlockSpec(memory_space=pltpu.VMEM)


def smem():
    return pl.BlockSpec(memory_space=pltpu.SMEM)


def anywhere():
    return pl.BlockSpec(memory_space=pltpu.HBM)


def params():
    return pltpu.CompilerParams(vmem_limit_bytes=VMEM_BYTES)


def exchange(packed, devices):
    moved = lax.all_to_all(
        packed.reshape(devices, KEEP * ROW), ("gx", "gy"), split_axis=0, concat_axis=0, tiled=True
    )
    return moved.reshape(devices * KEEP, ROW)


def swapped(near, far, axis):
    size = lax.axis_size(axis)
    pairs = [[(i, i + 1) for i in range(start, size - 1, 2)] for start in (0, 1)]
    pairs = [some + [(j, i) for i, j in some] for some in pairs]
    return lax.ppermute(near, axis, pairs[0]), lax.ppermute(far, axis, pairs[1])


def shifted(first, last, axis):
    size = lax.axis_size(axis)
    up = [(i, i + 1) for i in range(size - 1)]
    down = [(j, i) for i, j in up]
    return lax.ppermute(first, axis, down), lax.ppermute(last, axis, up)


def on_device(
    parent,
    metric,
    buoyancy,
    nest,
    nest_metric,
    strip_col,
    strip_dest,
    strip_pos,
    panel_src,
    panel_dest,
    panel_col,
):
    devices = lax.axis_size("gx") * lax.axis_size("gy")
    channels = parent.shape[0] * parent.shape[1]
    tile_x, tile_y = parent.shape[2:]
    block_x, block_y = nest.shape[2:]
    slots = strip_col.shape[0]
    groups = slots // ROW
    tile_shape = (channels * tile_x, tile_y)
    block_shape = (channels * block_x, block_y)
    packed_shape = (devices * KEEP, ROW)
    parts = 2

    def shape(*dims, dtype=jnp.float32):
        return jax.ShapeDtypeStruct(dims, dtype)

    def index(memory):
        return memory((slots,), jnp.int32)

    listed = pltpu.VMEM((groups, ROW), jnp.int32)
    rim_x = shape((channels + 1) * WIDTH, ROW)
    tile = parent.reshape(channels, tile_x, tile_y)
    ends = [
        pl.BlockSpec((channels, GROUP, ROW), lambda i, place=place: (0, place, 0))
        for place in (0, tile_x // GROUP - 1)
    ]
    whole_rim = pl.BlockSpec(rim_x.shape, lambda i: (0, 0))
    odd = (lax.axis_index("gx") % 2).astype(jnp.int32).reshape(1)
    near, far = pl.pallas_call(
        rim_kernel,
        grid=(1,),
        out_shape=(rim_x, rim_x),
        in_specs=[smem()] + ends + [pl.BlockSpec(metric.shape, lambda i: (0, 0))],
        out_specs=(whole_rim, whole_rim),
        compiler_params=params(),
        name="cut_rims",
    )(odd, tile, tile, metric)
    near, far = swapped(near, far, "gx")
    packed = pl.pallas_call(
        functools.partial(strip_kernel, size_x=tile_x, cells=block_x * block_y),
        out_shape=shape(*packed_shape),
        in_specs=[anywhere()] * 5,
        out_specs=anywhere(),
        scratch_shapes=[
            pltpu.VMEM((padded(channels) * tile_x, tile_y), jnp.float32),
            listed,
            index(pltpu.SMEM),
            index(pltpu.SMEM),
            listed,
            pltpu.VMEM((tile_x * tile_y, ROW), jnp.float32),
            pltpu.VMEM((devices * CAP, ROW), jnp.float32),
            listed,
            index(pltpu.SMEM),
            pltpu.SemaphoreType.DMA((4,)),
            pltpu.SemaphoreType.DMA((groups,)),
            pltpu.SemaphoreType.DMA((parts,)),
        ],
        compiler_params=params(),
        name="pack_strips",
    )(
        parent.reshape(tile_shape),
        strip_dest.reshape(groups, ROW),
        strip_col,
        strip_pos,
        strip_pos.reshape(groups, ROW),
    )

    packed, near, far, late_parent, late_metric, late_dest, late_col = (
        lax.optimization_barrier(
            (packed, near, far, parent.reshape(tile_shape), metric, panel_dest, panel_col)
        )
    )
    moved = exchange(packed, devices)
    tall = tile_x + 2 * WIDTH
    rim_y = shape(pl.cdiv(channels + 1, ROW // WIDTH) * tall, ROW)
    first_y, last_y, panel_slots = pl.pallas_call(
        strip_rim_kernel,
        out_shape=(rim_y, rim_y, shape(groups, ROW, dtype=jnp.int32)),
        in_specs=[smem()] + [vmem()] * 6,
        out_specs=(vmem(),) * 3,
        compiler_params=params(),
        cost_estimate=pl.CostEstimate(flops=3_000_000, bytes_accessed=2_000_000, transcendentals=0),
        name="pack_rims",
    )(
        odd,
        late_parent,
        late_metric,
        near,
        far,
        late_dest.reshape(groups, ROW),
        late_col.reshape(groups, ROW),
    )
    after_y, before_y = shifted(first_y, last_y, "gy")
    moved, after_y, before_y, panel_slots = lax.optimization_barrier(
        (moved, after_y, before_y, panel_slots)
    )
    nest_out, packed = pl.pallas_call(
        functools.partial(nest_kernel, size_x=block_x),
        out_shape=(shape(*block_shape), shape(*packed_shape)),
        in_specs=[anywhere()] * 7,
        out_specs=(anywhere(), anywhere()),
        scratch_shapes=[
            pltpu.VMEM(packed_shape, jnp.float32),
            pltpu.VMEM((padded(channels) * block_x, block_y), jnp.float32),
            pltpu.VMEM((block_x, block_y), jnp.float32),
            pltpu.SMEM(buoyancy.shape, jnp.float32),
            index(pltpu.SMEM),
            index(pltpu.SMEM),
            index(pltpu.SMEM),
            pltpu.VMEM((padded(channels) * block_x, block_y), jnp.float32),
            pltpu.VMEM((block_x * block_y, ROW), jnp.float32),
            pltpu.VMEM((block_x * block_y, ROW), jnp.float32),
            pltpu.VMEM((devices * CAP, ROW), jnp.float32),
        ]
        + add_scratch(devices)
        + [pltpu.SemaphoreType.DMA((6,)), pltpu.SemaphoreType.DMA((parts,))],
        compiler_params=params(),
        name="step_nest",
    )(
        moved,
        nest.reshape(block_shape),
        nest_metric,
        buoyancy,
        panel_src,
        panel_col,
        panel_slots.reshape(slots),
    )
    moved = exchange(packed, devices)
    edge = jnp.stack([lax.axis_index("gx") == 0, lax.axis_index("gy") == 0]).astype(jnp.int32)
    parent_state = pl.pallas_call(
        parent_kernel,
        out_shape=shape(*tile_shape),
        in_specs=[smem()] * 3 + [vmem()] * 6,
        out_specs=vmem(),
        scratch_shapes=[
            pltpu.VMEM((channels, tall, 2 * ROW), jnp.float32),
            pltpu.VMEM((tall, 2 * ROW), jnp.float32),
        ],
        compiler_params=params(),
        cost_estimate=pl.CostEstimate(flops=20_000_000, bytes_accessed=8_000_000, transcendentals=0),
        name="step_parent",
    )(odd, edge, buoyancy, late_parent, late_metric, near, far, after_y, before_y)

    parent_out = pl.pallas_call(
        functools.partial(final_kernel, size_x=tile_x),
        out_shape=shape(channels, tile_x, tile_y),
        in_specs=[anywhere(), anywhere()],
        out_specs=anywhere(),
        scratch_shapes=[
            pltpu.VMEM(packed_shape, jnp.float32),
            pltpu.VMEM((padded(channels) * tile_x, tile_y), jnp.float32),
            pltpu.VMEM((padded(channels), tile_x, tile_y), jnp.float32),
            pltpu.VMEM((tile_x * tile_y, ROW), jnp.float32),
        ]
        + add_scratch(devices)
        + [pltpu.SemaphoreType.DMA((1,)), pltpu.SemaphoreType.DMA((parts,))],
        compiler_params=params(),
        name="add_panels",
    )(moved, parent_state)
    return (parent_out.reshape(parent.shape), nest_out.reshape(nest.shape))


def solution(mesh):
    placed = (
        P(None, None, "gx", "gy"),
        P("gx", "gy"),
        P(),
        P(None, None, "gx", "gy"),
        P("gx", "gy"),
        P(("gx", "gy")),
        P(("gx", "gy"), None),
        P(("gx", "gy")),
        P(("gx", "gy")),
        P(("gx", "gy"), None),
        P(("gx", "gy")),
    )
    return jax.shard_map(
        on_device,
        mesh=mesh,
        in_specs=placed,
        out_specs=(P(None, None, "gx", "gy"), P(None, None, "gx", "gy")),
        check_vma=False,
    )
```

```python
import functools

import jax
import jax.numpy as jnp
from jax import lax
from jax.experimental import pallas as pl
from jax.experimental.pallas import tpu as pltpu
from jax.sharding import PartitionSpec as P

CAP = 32
NSP = 4
NSN = 6
COURANT = 0.35
WIDTH = NSP

ROW = 128
SPOT = 100
TALLY = 101
FREE = SPOT + 1
PIECE = ROW - FREE
PIECES = 4
KEEP = 26
REST = CAP - KEEP
GROUP = 8
STEP = 4
MARGINS = (4, 8)
VMEM_BYTES = 65500 * 1024


def slot_rows(dest, spot, cells):
    groups = dest.shape[0]
    shape = (ROW, ROW)
    row = lax.broadcasted_iota(jnp.int32, dest.shape, 0)
    lane = lax.broadcasted_iota(jnp.int32, dest.shape, 1)
    high = spot >= cells // 2
    side = jnp.where(high, 1, 0)
    inward = jnp.where(high, cells - 1 - spot, spot)
    least = (dest * 2 + side) << 21
    key = least + (inward << 10) + (row * ROW + lane)
    counts = [jnp.zeros((8, ROW), jnp.float32) for _ in range(groups)]
    for a in range(groups):
        column = jnp.broadcast_to(key[a : a + 1], shape).T
        for b in range(groups):
            before = (column >= least[b : b + 1]) & (column < key[b : b + 1])
            ones = jnp.where(before, 1.0, 0.0)
            counts[b] = counts[b] + jnp.sum(ones.reshape(ROW // 8, 8, ROW), axis=0)
    rank = jnp.concatenate([jnp.sum(c, axis=0, keepdims=True) for c in counts], 0)
    rank = rank.astype(jnp.int32)
    slot = jnp.where(high, CAP - 1 - rank, rank)
    devices = ROW
    spill = devices * KEEP + (slot - KEEP) * devices + dest
    return jnp.where(slot < KEEP, dest * KEEP + slot, spill)


def padded(channels):
    return pl.cdiv(channels, 8) * 8


def to_rows(fields, rows, channels, size_x):
    height = padded(channels)
    real = lax.broadcasted_iota(jnp.int32, (8, ROW), 0) < channels - (height - 8)
    tail = jnp.zeros((ROW - height, ROW), jnp.float32)
    for i in range(size_x):
        block = fields[pl.ds(i, height, stride=size_x), :]
        final = jnp.where(real, block[height - 8 :], 0.0)
        block = jnp.concatenate([block[: height - 8], final, tail], 0)
        rows[i * ROW : (i + 1) * ROW, :] = block.T


def clear_rows(staged):
    lane = lax.broadcasted_iota(jnp.int32, (1, ROW), 1)
    staged[...] = jnp.broadcast_to(jnp.where(lane == SPOT, -1.0, 0.0), staged.shape)


def spread_spots(spots, table):
    for a in range(spots.shape[0]):
        row = spots[a : a + 1, :].astype(jnp.float32)
        table[a * ROW : (a + 1) * ROW, :] = jnp.broadcast_to(row, (ROW, ROW)).T


def pack_rows(rows, picks, spots, slots, staged, packed, sems):
    lane = lax.broadcasted_iota(jnp.int32, (1, ROW), 1)
    devices = packed.shape[0] // KEEP

    def move(r, carry):
        spot = spots[pl.ds(r, 1), :]
        row = rows[pl.ds(picks[r], 1), :]
        staged[pl.ds(slots[r], 1), :] = jnp.where(lane == SPOT, spot, row)
        return carry

    lax.fori_loop(0, slots.shape[0], move, 0, unroll=32)
    parts = sems.shape[0]
    count = devices // parts
    free = lax.broadcasted_iota(jnp.int32, (count, ROW), 1) >= FREE
    copies = []
    for part in range(parts):
        base = part * count
        for a in range(REST):
            start = devices * (KEEP + a) + base
            values = staged[start : start + count, :]
            for b in range(PIECES):
                where = pl.ds(base * KEEP + b * REST + a, count, stride=KEEP)
                piece = pltpu.roll(values, (FREE - b * PIECE) % ROW, 1)
                staged[where, :] = jnp.where(free, piece, staged[where, :])
        block = pl.ds(base * KEEP, count * KEEP)
        copies.append(pltpu.make_async_copy(staged.at[block], packed.at[block], sems.at[part]))
        copies[-1].start()
    return copies


def slot_values(moved, s, base, count):
    if s < KEEP:
        return moved[pl.ds(base * KEEP + s, count, stride=KEEP), :]
    lane = lax.broadcasted_iota(jnp.int32, (count, ROW), 1)
    values = jnp.zeros((count, ROW), jnp.float32)
    for b in range(PIECES):
        where = pl.ds(base * KEEP + b * REST + s - KEEP, count, stride=KEEP)
        piece = pltpu.roll(moved[where, :], (b * PIECE - FREE) % ROW, 1)
        values = jnp.where((lane >= b * PIECE) & (lane < (b + 1) * PIECE), piece, values)
    return values


def prepare(moved, arrivals, later, weights, columns, easts, size_x):
    lane = lax.broadcasted_iota(jnp.int32, (16, 2 * ROW), 1)
    pick = jnp.where((lane == SPOT) | (lane == SPOT + ROW), 1.0, 0.0).astype(jnp.bfloat16)
    devices = moved.shape[0] // KEEP
    depth = devices * GROUP
    tiles = CAP // GROUP
    count = devices // len(arrivals)
    north = lax.broadcasted_iota(jnp.int32, (ROW, depth), 0)
    tally = lax.broadcasted_iota(jnp.int32, (count, ROW), 1) == TALLY
    for part, arrival in enumerate(arrivals):
        arrival.wait()
        base = part * count
        for s in range(CAP):
            values = jnp.where(tally, 1.0, slot_values(moved, s, base, count))
            high = values.astype(jnp.bfloat16)
            low = (values - high.astype(jnp.float32)).astype(jnp.bfloat16)
            t, k = s // GROUP, s % GROUP
            start = t * depth + k * devices + base
            weights[start : start + count, :ROW] = high
            weights[start : start + count, ROW:] = low
    for copy in later:
        copy.start()
    reaches = []
    for t in range(tiles):
        spot = lax.dot_general(
            pick, weights[t * depth : (t + 1) * depth, :], (((1,), (1,)), ((), ())), preferred_element_type=jnp.float32
        )
        whole = spot.astype(jnp.int32)
        east, within = whole >> 7, whole & (ROW - 1)
        easts[t] = east.astype(jnp.float32).astype(jnp.bfloat16)
        columns[t] = jnp.where(north == within[0:1], 1.0, 0.0).astype(jnp.bfloat16)
        used = spot[0:8] >= 0.0
        reach = east[0:8].astype(jnp.float32)
        first = jnp.min(jnp.where(used, reach, float(size_x)))
        last = jnp.max(jnp.where(used, reach, -1.0))
        reaches.append((first.astype(jnp.int32), last.astype(jnp.int32)))
    return reaches


def add_rows(moved, arrivals, later, sums, weights, columns, easts, size_x):
    tiles, depth = easts.shape[0], easts.shape[2]
    reaches = prepare(moved, arrivals, later, weights, columns, easts, size_x)

    def block(t, here):
        column = columns[t].reshape(ROW // 16, 16, depth)
        parts = []
        for k in range(STEP):
            place = jnp.asarray(here + k, jnp.float32).astype(jnp.bfloat16)
            mine = jnp.where(easts[t] == place, 1.0, 0.0).astype(jnp.bfloat16)
            parts.append((column * mine[None]).reshape(ROW, depth))
        where = pl.ds(pl.multiple_of(here * ROW, ROW), STEP * ROW)
        both = jnp.dot(
            jnp.concatenate(parts, 0),
            weights[t * depth : (t + 1) * depth, :],
            preferred_element_type=jnp.float32,
        )
        sums[where, :] += both[:, :ROW] + both[:, ROW:]

    low = [min(size_x, size_x // 2 + margin) for margin in MARGINS]
    widths = low + low[::-1]
    fits = [last - first < width for (first, last), width in zip(reaches, widths)]
    narrow = functools.reduce(jnp.logical_and, fits)

    @pl.when(narrow)
    def _():
        for t in range(tiles):
            start = jnp.minimum(reaches[t][0], size_x - widths[t])
            for g in range(widths[t] // STEP):
                block(t, start + g * STEP)

    @pl.when(jnp.logical_not(narrow))
    def _():
        for t in range(tiles):
            first, last = reaches[t]
            blocks = jnp.maximum(last - first + STEP, 0) // STEP
            start = jnp.minimum(first, size_x - blocks * STEP)

            def reached(g, carry, t=t, start=start):
                block(t, start + g * STEP)
                return carry

            lax.fori_loop(0, blocks, reached, 0)


def add_scratch(devices):
    depth = devices * GROUP
    tiles = CAP // GROUP
    return [
        pltpu.VMEM((tiles * depth, 2 * ROW), jnp.bfloat16),
        pltpu.VMEM((tiles, ROW, depth), jnp.bfloat16),
        pltpu.VMEM((tiles, 16, depth), jnp.bfloat16),
    ]


def relax(fields, sums, out, channels, size_x, i):
    block = slice(i * ROW, (i + 1) * ROW)
    total = sums[block, :].T
    share = 1.0 / (1.0 + total[TALLY : TALLY + 1])
    height = padded(channels)
    where = pl.ds(i, height, stride=size_x)
    out[where, :] = (fields[where, :] + total[:height]) * share


def nest_step(state, metric, buoyancy, levels, size_x):
    shape = (size_x, ROW)
    row = lax.broadcasted_iota(jnp.int32, shape, 0)
    lane = lax.broadcasted_iota(jnp.int32, shape, 1)
    scaled = COURANT * metric[...]

    def at(field, k):
        start = (field * levels + k) * size_x
        return slice(start, start + size_x)

    w_below = jnp.zeros(shape, jnp.float32)
    p = state[at(4, 0), :]
    for k in range(levels):
        n = COURANT * buoyancy[k]
        p_above = state[at(4, k + 1), :] if k + 1 < levels else jnp.zeros(shape, jnp.float32)
        p_east = jnp.where(row == size_x - 1, 0.0, pltpu.roll(p, size_x - 1, 0))
        p_north = jnp.where(lane == ROW - 1, 0.0, pltpu.roll(p, ROW - 1, 1))
        u = state[at(0, k), :] - COURANT * (p_east - p)
        v = state[at(1, k), :] - COURANT * (p_north - p)
        edge = -COURANT * p
        u_west = jnp.where(row == 0, edge, pltpu.roll(u, 1, 0))
        v_south = jnp.where(lane == 0, edge, pltpu.roll(v, 1, 1))
        theta = state[at(3, k), :]
        w = state[at(2, k), :] - COURANT * (p_above - p) + n * theta
        state[at(0, k), :] = u
        state[at(1, k), :] = v
        state[at(2, k), :] = w
        state[at(3, k), :] = theta - n * w
        state[at(4, k), :] = p - scaled * ((u - u_west) + (v - v_south) + (w - w_below))
        w_below = w
        p = p_above


def planned(pairs, sems):
    return [pltpu.make_async_copy(a, b, sems.at[i]) for i, (a, b) in enumerate(pairs)]


def fetch(pairs, sems):
    copies = planned(pairs, sems)
    for copy in copies:
        copy.start()
    return copies


def split(source, target, parts):
    count = source.shape[0] // parts
    blocks = [pl.ds(part * count, count) for part in range(parts)]
    return [(source.at[block], target.at[block]) for block in blocks]


def strip_kernel(
    parent, dest, picks, spots, packed,
    tile, dest_v, picks_s, table, spots_v, rows, staged, slots_v, slots, sems, slot_sems, out_sems,
    *, size_x, cells
):
    channels = parent.shape[0] // size_x
    copies = fetch(
        [(dest, dest_v), (spots, spots_v), (picks, picks_s)], sems
    )
    arrivals = fetch(split(parent, tile, out_sems.shape[0]), out_sems)
    clear_rows(staged)
    copies[0].wait()
    copies[1].wait()
    slots_v[...] = slot_rows(dest_v[...], spots_v[...], cells)
    moves = fetch(
        [(slots_v.at[a], slots.at[pl.ds(a * ROW, ROW)]) for a in range(slots_v.shape[0])], slot_sems
    )
    spread_spots(spots_v, table)
    for copy in arrivals:
        copy.wait()
    to_rows(tile, rows, channels, size_x)
    for copy in copies[2:] + moves:
        copy.wait()
    for copy in pack_rows(rows, picks_s, table, slots, staged, packed, out_sems):
        copy.wait()


def nest_kernel(
    moved, nest, metric, buoyancy, picks, spots, slots, out, packed,
    came, tile, metric_v, buoyancy_s, picks_s, spots_v, table, slots_s, state, sums, rows, staged,
    weights, columns, easts, sems, out_sems,
    *, size_x
):
    channels = nest.shape[0] // size_x
    early = pltpu.make_async_copy(spots, spots_v, sems.at[5])
    early.start()
    arrivals = fetch(split(moved, came, out_sems.shape[0]), out_sems)
    copies = planned(
        [(nest, tile.at[pl.ds(0, nest.shape[0])]), (metric, metric_v), (buoyancy, buoyancy_s)]
        + [(picks, picks_s), (slots, slots_s)],
        sems,
    )
    sums[...] = jnp.zeros(sums.shape, jnp.float32)
    clear_rows(staged)
    early.wait()
    spread_spots(spots_v, table)
    add_rows(came, arrivals, copies, sums, weights, columns, easts, size_x)
    for copy in copies:
        copy.wait()
    for i in range(size_x):
        relax(tile, sums, state, channels, size_x, i)

    def step(_, carry):
        nest_step(state, metric_v, buoyancy_s, channels // 5, size_x)
        return carry

    lax.fori_loop(0, NSN, step, 0)
    result = pltpu.make_async_copy(state.at[pl.ds(0, out.shape[0])], out, sems.at[0])
    result.start()
    to_rows(state, rows, channels, size_x)
    for copy in pack_rows(rows, picks_s, table, slots_s, staged, packed, out_sems):
        copy.wait()
    result.wait()


def rim_kernel(odd, head, tail, metric, near, far):
    channels, block = head.shape[:2]
    size_x = metric.shape[0]

    def cut(first, last):
        for c in range(0, channels, 2):
            pair = slice(c * WIDTH, (c + 2) * WIDTH)
            first[pair, :] = jnp.concatenate([head[c, :WIDTH], head[c + 1, :WIDTH]], 0)
            last[pair, :] = jnp.concatenate(
                [tail[c, block - WIDTH :], tail[c + 1, block - WIDTH :]], 0
            )
        own = slice(channels * WIDTH, (channels + 1) * WIDTH)
        first[own, :] = metric[:WIDTH]
        last[own, :] = metric[size_x - WIDTH :]

    @pl.when(odd[0] == 1)
    def _():
        cut(near, far)

    @pl.when(odd[0] == 0)
    def _():
        cut(far, near)


def rim_rows(odd, near, far, c):
    rim = slice(c * WIDTH, (c + 1) * WIDTH)
    ours, theirs = near[rim, :], far[rim, :]
    even = odd[0] == 0
    return jnp.concatenate([jnp.where(even, ours, theirs), jnp.where(even, theirs, ours)], 0)


def strip_rim_kernel(odd, parent, metric, near, far, dest, spots, first, last, slots):
    size_x = metric.shape[0]
    channels = parent.shape[0] // size_x
    slots[...] = slot_rows(dest[...], spots[...], size_x * ROW)

    def rows(c):
        own = parent[c * size_x : (c + 1) * size_x, :] if c < channels else metric[...]
        return jnp.concatenate([own, rim_rows(odd, near, far, c)], 0)

    gather_lanes(rows, channels + 1, size_x + 2 * WIDTH, first, last)


def gather_lanes(rows, count, height, first, last):
    per = ROW // WIDTH
    lane = lax.broadcasted_iota(jnp.int32, (height, ROW), 1) // WIDTH
    for q in range(pl.cdiv(count, per)):
        ahead = jnp.zeros((height, ROW), jnp.float32)
        behind = ahead
        for m in range(min(per, count - q * per)):
            own = rows(q * per + m)
            ahead = jnp.where(lane == m, pltpu.roll(own, m * WIDTH, 1), ahead)
            behind = jnp.where(lane == m, pltpu.roll(own, (m + 1) * WIDTH % ROW, 1), behind)
        where = slice(q * height, (q + 1) * height)
        first[where, :] = ahead
        last[where, :] = behind


def parent_kernel(
    odd, edge, buoyancy, parent, metric, near, far, after_y, before_y, out, state, scaled
):
    size_x = metric.shape[0]
    channels = parent.shape[0] // size_x
    levels = channels // 5
    tall = size_x + 2 * WIDTH
    per = ROW // WIDTH
    shape = (tall, 2 * ROW)
    group = lax.broadcasted_iota(jnp.int32, (tall, ROW), 1) // WIDTH

    def extended(c, own):
        m = c % per
        rows = slice(c // per * tall, (c // per + 1) * tall)
        ahead = pltpu.roll(after_y[rows, :], -m * WIDTH % ROW, 1)
        behind = pltpu.roll(before_y[rows, :], (per - 1 - m) * WIDTH, 1)
        side = jnp.where(group == 0, ahead, jnp.where(group == per - 1, behind, 0.0))
        middle = jnp.concatenate([own, rim_rows(odd, near, far, c)], 0)
        return jnp.concatenate([middle, side], 1)

    for c in range(channels):
        state[c] = extended(c, parent[c * size_x : (c + 1) * size_x, :])
    scaled[...] = COURANT * extended(channels, metric[...])
    row = lax.broadcasted_iota(jnp.int32, shape, 0)
    lane = lax.broadcasted_iota(jnp.int32, shape, 1)
    u_keep = jnp.where((row >= tall - WIDTH) & (edge[0] == 1), 0.0, 1.0)
    v_keep = jnp.where((lane >= 2 * ROW - WIDTH) & (edge[1] == 1), 0.0, 1.0)

    def step(_, carry):
        w_below = jnp.zeros(shape, jnp.float32)
        p = state[4 * levels]
        for k in range(levels):
            n = COURANT * buoyancy[k]
            p_above = state[4 * levels + k + 1] if k + 1 < levels else jnp.zeros(shape, jnp.float32)
            u = state[k] - COURANT * (pltpu.roll(p, tall - 1, 0) - p)
            v = state[levels + k] - COURANT * (pltpu.roll(p, 2 * ROW - 1, 1) - p)
            theta = state[3 * levels + k]
            w = state[2 * levels + k] - COURANT * (p_above - p) + n * theta
            spread = (u - pltpu.roll(u, 1, 0)) + (v - pltpu.roll(v, 1, 1)) + (w - w_below)
            state[k] = u * u_keep
            state[levels + k] = v * v_keep
            state[2 * levels + k] = w
            state[3 * levels + k] = theta - n * w
            state[4 * levels + k] = p - scaled[...] * spread
            w_below = w
            p = p_above
        return carry

    lax.fori_loop(0, NSP, step, 0)
    for c in range(channels):
        out[c * size_x : (c + 1) * size_x, :] = state[c, :size_x, :ROW]


def final_kernel(
    moved, parent, out, came, tile, result, sums, weights, columns, easts, sems, out_sems, *, size_x
):
    channels = parent.shape[0] // size_x
    arrivals = fetch(split(moved, came, out_sems.shape[0]), out_sems)
    copies = planned([(parent, tile.at[pl.ds(0, parent.shape[0])])], sems)
    flat = result.reshape(padded(channels) * size_x, ROW)
    count = size_x // out_sems.shape[0]
    blocks = [(pl.ds(0, channels), pl.ds(start, count)) for start in range(0, size_x, count)]
    leaving = planned([(result.at[block], out.at[block]) for block in blocks], out_sems)

    sums[...] = jnp.zeros(sums.shape, jnp.float32)
    add_rows(came, arrivals, copies, sums, weights, columns, easts, size_x)
    copies[0].wait()
    for i in range(size_x):
        relax(tile, sums, flat, channels, size_x, i)
        if i % count == count - 1:
            leaving[i // count].start()
    for copy in leaving:
        copy.wait()


def vmem():
    return pl.BlockSpec(memory_space=pltpu.VMEM)


def smem():
    return pl.BlockSpec(memory_space=pltpu.SMEM)


def anywhere():
    return pl.BlockSpec(memory_space=pltpu.HBM)


def params():
    return pltpu.CompilerParams(vmem_limit_bytes=VMEM_BYTES)


def exchange(packed, devices):
    moved = lax.all_to_all(
        packed.reshape(devices, KEEP * ROW), ("gx", "gy"), split_axis=0, concat_axis=0, tiled=True
    )
    return moved.reshape(devices * KEEP, ROW)


def swapped(near, far, axis):
    size = lax.axis_size(axis)
    pairs = [[(i, i + 1) for i in range(start, size - 1, 2)] for start in (0, 1)]
    pairs = [some + [(j, i) for i, j in some] for some in pairs]
    return lax.ppermute(near, axis, pairs[0]), lax.ppermute(far, axis, pairs[1])


def shifted(first, last, axis):
    size = lax.axis_size(axis)
    up = [(i, i + 1) for i in range(size - 1)]
    down = [(j, i) for i, j in up]
    return lax.ppermute(first, axis, down), lax.ppermute(last, axis, up)


def on_device(
    parent,
    metric,
    buoyancy,
    nest,
    nest_metric,
    strip_col,
    strip_dest,
    strip_pos,
    panel_src,
    panel_dest,
    panel_col,
):
    devices = lax.axis_size("gx") * lax.axis_size("gy")
    channels = parent.shape[0] * parent.shape[1]
    tile_x, tile_y = parent.shape[2:]
    block_x, block_y = nest.shape[2:]
    slots = strip_col.shape[0]
    groups = slots // ROW
    tile_shape = (channels * tile_x, tile_y)
    block_shape = (channels * block_x, block_y)
    packed_shape = (devices * KEEP, ROW)
    parts = 4

    def shape(*dims, dtype=jnp.float32):
        return jax.ShapeDtypeStruct(dims, dtype)

    def index(memory):
        return memory((slots,), jnp.int32)

    listed = pltpu.VMEM((groups, ROW), jnp.int32)
    rim_x = shape((channels + 1) * WIDTH, ROW)
    tile = parent.reshape(channels, tile_x, tile_y)
    ends = [
        pl.BlockSpec((channels, GROUP, ROW), lambda i, place=place: (0, place, 0))
        for place in (0, tile_x // GROUP - 1)
    ]
    whole_rim = pl.BlockSpec(rim_x.shape, lambda i: (0, 0))
    odd = (lax.axis_index("gx") % 2).astype(jnp.int32).reshape(1)
    near, far = pl.pallas_call(
        rim_kernel,
        grid=(1,),
        out_shape=(rim_x, rim_x),
        in_specs=[smem()] + ends + [pl.BlockSpec(metric.shape, lambda i: (0, 0))],
        out_specs=(whole_rim, whole_rim),
        compiler_params=params(),
        name="cut_rims",
    )(odd, tile, tile, metric)
    near, far = swapped(near, far, "gx")
    packed = pl.pallas_call(
        functools.partial(strip_kernel, size_x=tile_x, cells=block_x * block_y),
        out_shape=shape(*packed_shape),
        in_specs=[anywhere()] * 4,
        out_specs=anywhere(),
        scratch_shapes=[
            pltpu.VMEM((padded(channels) * tile_x, tile_y), jnp.float32),
            listed,
            index(pltpu.SMEM),
            pltpu.VMEM((slots, ROW), jnp.float32),
            listed,
            pltpu.VMEM((tile_x * tile_y, ROW), jnp.float32),
            pltpu.VMEM((devices * CAP, ROW), jnp.float32),
            listed,
            index(pltpu.SMEM),
            pltpu.SemaphoreType.DMA((4,)),
            pltpu.SemaphoreType.DMA((groups,)),
            pltpu.SemaphoreType.DMA((parts,)),
        ],
        compiler_params=params(),
        name="pack_strips",
    )(
        parent.reshape(tile_shape),
        strip_dest.reshape(groups, ROW),
        strip_col,
        strip_pos.reshape(groups, ROW),
    )

    packed, near, far, late_parent, late_metric, late_dest, late_col = (
        lax.optimization_barrier(
            (packed, near, far, parent.reshape(tile_shape), metric, panel_dest, panel_col)
        )
    )
    moved = exchange(packed, devices)
    tall = tile_x + 2 * WIDTH
    rim_y = shape(pl.cdiv(channels + 1, ROW // WIDTH) * tall, ROW)
    first_y, last_y, panel_slots = pl.pallas_call(
        strip_rim_kernel,
        out_shape=(rim_y, rim_y, shape(groups, ROW, dtype=jnp.int32)),
        in_specs=[smem()] + [vmem()] * 6,
        out_specs=(vmem(),) * 3,
        compiler_params=params(),
        cost_estimate=pl.CostEstimate(flops=3_000_000, bytes_accessed=2_000_000, transcendentals=0),
        name="pack_rims",
    )(
        odd,
        late_parent,
        late_metric,
        near,
        far,
        late_dest.reshape(groups, ROW),
        late_col.reshape(groups, ROW),
    )
    after_y, before_y = shifted(first_y, last_y, "gy")
    moved, after_y, before_y, panel_slots = lax.optimization_barrier(
        (moved, after_y, before_y, panel_slots)
    )
    nest_out, packed = pl.pallas_call(
        functools.partial(nest_kernel, size_x=block_x),
        out_shape=(shape(*block_shape), shape(*packed_shape)),
        in_specs=[anywhere()] * 7,
        out_specs=(anywhere(), anywhere()),
        scratch_shapes=[
            pltpu.VMEM(packed_shape, jnp.float32),
            pltpu.VMEM((padded(channels) * block_x, block_y), jnp.float32),
            pltpu.VMEM((block_x, block_y), jnp.float32),
            pltpu.SMEM(buoyancy.shape, jnp.float32),
            index(pltpu.SMEM),
            listed,
            pltpu.VMEM((slots, ROW), jnp.float32),
            index(pltpu.SMEM),
            pltpu.VMEM((padded(channels) * block_x, block_y), jnp.float32),
            pltpu.VMEM((block_x * block_y, ROW), jnp.float32),
            pltpu.VMEM((block_x * block_y, ROW), jnp.float32),
            pltpu.VMEM((devices * CAP, ROW), jnp.float32),
        ]
        + add_scratch(devices)
        + [pltpu.SemaphoreType.DMA((6,)), pltpu.SemaphoreType.DMA((parts,))],
        compiler_params=params(),
        name="step_nest",
    )(
        moved,
        nest.reshape(block_shape),
        nest_metric,
        buoyancy,
        panel_src,
        panel_col.reshape(groups, ROW),
        panel_slots.reshape(slots),
    )
    moved = exchange(packed, devices)
    edge = jnp.stack([lax.axis_index("gx") == 0, lax.axis_index("gy") == 0]).astype(jnp.int32)
    parent_state = pl.pallas_call(
        parent_kernel,
        out_shape=shape(*tile_shape),
        in_specs=[smem()] * 3 + [vmem()] * 6,
        out_specs=vmem(),
        scratch_shapes=[
            pltpu.VMEM((channels, tall, 2 * ROW), jnp.float32),
            pltpu.VMEM((tall, 2 * ROW), jnp.float32),
        ],
        compiler_params=params(),
        cost_estimate=pl.CostEstimate(flops=20_000_000, bytes_accessed=8_000_000, transcendentals=0),
        name="step_parent",
    )(odd, edge, buoyancy, late_parent, late_metric, near, far, after_y, before_y)

    parent_out = pl.pallas_call(
        functools.partial(final_kernel, size_x=tile_x),
        out_shape=shape(channels, tile_x, tile_y),
        in_specs=[anywhere(), anywhere()],
        out_specs=anywhere(),
        scratch_shapes=[
            pltpu.VMEM(packed_shape, jnp.float32),
            pltpu.VMEM((padded(channels) * tile_x, tile_y), jnp.float32),
            pltpu.VMEM((padded(channels), tile_x, tile_y), jnp.float32),
            pltpu.VMEM((tile_x * tile_y, ROW), jnp.float32),
        ]
        + add_scratch(devices)
        + [pltpu.SemaphoreType.DMA((1,)), pltpu.SemaphoreType.DMA((parts,))],
        compiler_params=params(),
        name="add_panels",
    )(moved, parent_state)
    return (parent_out.reshape(parent.shape), nest_out.reshape(nest.shape))


def solution(mesh):
    placed = (
        P(None, None, "gx", "gy"),
        P("gx", "gy"),
        P(),
        P(None, None, "gx", "gy"),
        P("gx", "gy"),
        P(("gx", "gy")),
        P(("gx", "gy"), None),
        P(("gx", "gy")),
        P(("gx", "gy")),
        P(("gx", "gy"), None),
        P(("gx", "gy")),
    )
    return jax.shard_map(
        on_device,
        mesh=mesh,
        in_specs=placed,
        out_specs=(P(None, None, "gx", "gy"), P(None, None, "gx", "gy")),
        check_vma=False,
    )
```
